128 devices in a mesh: ens: 4 (over x), cols: 32 (over z, y, core).
Axes of the slice: x: 4, y: 4, z: 4, core: 2. Of those that a mesh axis runs over, the one named last changes fastest.
Arguments:
- static_control: float32 [16, 64, 4096], P(None, 'cols'), may hold values from -6 to 6
- ensemble_control: float32 [32, 16, 64, 4096], P('ens', None, 'cols'), may hold values from -6 to 6
- perturbations: bfloat16 [32, 16, 64, 4096], P('ens', None, 'cols'), may hold values from -6 to 6
- vertical_root: float32 [16, 16], replicated, may hold values from 0 to 1.5
- vertical_local: float32 [16, 16], replicated, may hold values from 0 to 1.5
- face_north: float32 [64, 4096], P('cols'), may hold values from 0.02 to 0.24
- face_east: float32 [64, 4096], P('cols'), may hold values from 0.02 to 0.24
- innovation: float32 [2097152], P('cols'), may hold values from -6 to 6
- obs_weight: float32 [2097152], P('cols'), may hold values from 0.5 to 4
- obs_slot: int32 [2097152], P('cols'), may hold values from 0 to 32767
- send_index: int32 [1024, 1024], P('cols'), may hold values from 0 to 131071
- send_count: int32 [1024], P('cols'), may hold values from 256 to 1024, as said below
Outputs:
- static_grad: float32 [16, 64, 4096], P(None, 'cols')
- ensemble_grad: float32 [32, 16, 64, 4096], P('ens', None, 'cols')
The draws below stay inside these ranges and needn't reach their ends.
Inputs may be any that keep to these rules, and one draw needn't show every extreme that they name: `send_count`: in every draw one observation owner, drawn from the seed, receives full lists (count 1024) from every column owner; all other counts are drawn independently.
All inputs are finite; a program needn't handle non-finite values.
Results may differ from the reference program's by a relative error of at most 0.0003.
Values sent between devices are 32-bit elements; how exact they have to be, the bound alone decides.
A program may use at most 128 MiB of HBM per device.

```python
import math
import jax
import jax.numpy as jnp
from jax import lax

LEV = 16
ROWS = 2
NL = 4096
NDIFF = 4
CAP = 1024
OBS_DEV = 65536
NR = 64
MEMBERS = 32
N_COLS = 32


def banded(key, width):
    level_ids = jnp.arange(LEV, dtype=jnp.int32)
    distance = jnp.abs(level_ids[:, None] - level_ids[None, :]).astype(jnp.float32)
    factor = jax.random.uniform(key, (LEV, LEV), jnp.float32, 0.5, 1.5)
    return factor * jnp.exp(-distance / width)


def draw_vertical_root(key, part):
    key = jax.random.fold_in(key, 11)
    return banded(key, 1.5)


def draw_vertical_local(key, part):
    key = jax.random.fold_in(key, 13)
    return banded(key, 3.0)


def draw_send_count(key, part):
    key = jax.random.fold_in(key, 17)
    counts = jax.random.randint(key, (N_COLS, N_COLS), CAP // 4, CAP + 1, dtype=jnp.int32)
    busiest = jax.random.randint(jax.random.fold_in(key, 1), (), 0, N_COLS, dtype=jnp.int32)
    column = jnp.arange(N_COLS, dtype=jnp.int32)[None, :]
    counts = jnp.where(column == busiest, CAP, counts)
    return counts.reshape(-1).astype(jnp.int32)


def draw_send_index(key, part):
    key = jax.random.fold_in(key, 19)
    cell_total = LEV * ROWS * NL
    indices = jax.random.randint(key, (N_COLS * N_COLS, CAP), 0, cell_total, dtype=jnp.int32)
    indices = indices.at[0, 0].set(0).at[0, 1].set(cell_total - 1)
    return indices


def draw_obs_slot(key, part):
    key = jax.random.fold_in(key, 23)
    indices = jax.random.randint(key, (N_COLS * OBS_DEV,), 0, N_COLS * CAP, dtype=jnp.int32)
    indices = indices.at[0].set(0).at[1].set(N_COLS * CAP - 1)
    return indices


def steps_of(rng, shape, split, smallest, largest):
    factor_of = 1.0
    for dim, parts in split:
        steps = jax.random.uniform(jax.random.fold_in(jax.random.fold_in(rng, 6), dim), (parts,), jnp.float32, smallest / len(split), largest / len(split))
        factor_of = factor_of * jnp.repeat(jnp.exp(steps), shape[dim] // parts).reshape((-1,) + (1,) * (len(shape) - 1 - dim))
    return factor_of


def noise(rng, extent, scale, reach, cuts=(), held_as=jnp.bfloat16):
    level = steps_of(rng, extent, cuts, -0.22, 0.18) if cuts else 1.0
    entries = jax.random.normal(rng, extent, jnp.float32) * scale * level
    return jnp.minimum(jnp.maximum(entries, -reach), reach).astype(held_as)


def setup_inputs(seed: int = 0) -> dict:
    seeds = jax.random.split(jax.random.key(seed), 13)
    static_control = noise(seeds[0], (LEV, NR, NL), 1.0, 6.0, ((1, 32),), jnp.float32)
    ensemble_control = noise(seeds[1], (MEMBERS, LEV, NR, NL), 1.0, 6.0, ((0, 4), (2, 32)), jnp.float32)
    perturbations = noise(seeds[2], (MEMBERS, LEV, NR, NL), 1.0, 6.0, ((0, 4), (2, 32)))
    vertical_root = draw_vertical_root(jax.random.fold_in(seeds[12], 71), 0)
    vertical_local = draw_vertical_local(jax.random.fold_in(seeds[12], 71), 0)
    face_north = jnp.clip(0.02 + 0.22 * jax.random.uniform(seeds[5], (NR, NL), jnp.float32) ** steps_of(seeds[5], (NR, NL), ((0, 32),), -0.2, 0.2), 0.02, 0.24)
    face_east = jnp.clip(0.02 + 0.22 * jax.random.uniform(seeds[6], (NR, NL), jnp.float32) ** steps_of(seeds[6], (NR, NL), ((0, 32),), -0.2, 0.2), 0.02, 0.24)
    innovation = noise(seeds[7], (N_COLS * OBS_DEV,), 1.0, 6.0, ((0, 32),), jnp.float32)
    obs_weight = jnp.clip(jnp.exp(math.log(4.0) - 2.0794415 * jax.random.uniform(seeds[8], (N_COLS * OBS_DEV,), jnp.float32) ** steps_of(seeds[8], (N_COLS * OBS_DEV,), ((0, 32),), -0.2, 0.2)), 0.5, 4.0)
    obs_slot = draw_obs_slot(jax.random.fold_in(seeds[12], 71), 0)
    send_index = draw_send_index(jax.random.fold_in(seeds[12], 71), 0)
    send_count = draw_send_count(jax.random.fold_in(seeds[12], 71), 0)
    return {"static_control": static_control, "ensemble_control": ensemble_control, "perturbations": perturbations, "vertical_root": vertical_root, "vertical_local": vertical_local, "face_north": face_north, "face_east": face_east, "innovation": innovation, "obs_weight": obs_weight, "obs_slot": obs_slot, "send_index": send_index, "send_count": send_count}


precise = lax.Precision.HIGHEST

def smooth(source, padded, k_north, k_south, k_east):
    upper_rows = padded[:, :-2]
    lower_rows = padded[:, 2:]
    eastern = jnp.roll(source, -1, axis=2)
    western = jnp.roll(source, 1, axis=2)
    k_west = jnp.roll(k_east, 1, axis=1)
    return source + k_north * (upper_rows - source) + k_south * (lower_rows - source) + k_east * (eastern - source) + k_west * (western - source)

def vertical(matrix, source):
    return jnp.einsum('lm,mrc->lrc', matrix, source, precision=precise)

def reference(static_control, ensemble_control, perturbations, vertical_root, vertical_local, face_north, face_east, innovation, obs_weight, obs_slot, send_index, send_count):
    k_south = jnp.concatenate([face_north[1:], jnp.zeros_like(face_north[:1])], axis=0)

    def diffuse(source):
        for repeat in range(NDIFF):
            padded = jnp.pad(source, ((0, 0), (1, 1), (0, 0)))
            source = smooth(source, padded, face_north, k_south, face_east)
        return source
    static_increment = diffuse(vertical(vertical_root, static_control))
    member_scale = 1.0 / math.sqrt(MEMBERS - 1)

    def add_member(running, members_pair):
        member_pert, member_alpha = members_pair
        localized = vertical(vertical_local, member_alpha)
        return (running + member_pert.astype(jnp.float32) * localized, None)
    ens_sum, unused = lax.scan(add_member, jnp.zeros(static_control.shape, jnp.float32), (perturbations, ensemble_control))
    increment = static_increment + member_scale * ens_sum
    flattened = increment.reshape(-1)
    tile_cells = ROWS * NL
    list_ids = jnp.arange(N_COLS * N_COLS, dtype=jnp.int32)
    column_dev = list_ids // N_COLS
    level_of = send_index // tile_cells
    within = send_index % tile_cells
    global_index = level_of * (N_COLS * tile_cells) + column_dev[:, None] * tile_cells + within
    live_mask = (jnp.arange(CAP, dtype=jnp.int32)[None, :] < send_count[:, None]).astype(jnp.float32)
    values = flattened[global_index] * live_mask
    owner_dev = jnp.arange(N_COLS * OBS_DEV, dtype=jnp.int32) // OBS_DEV
    source_dev = obs_slot // CAP
    position = (source_dev * N_COLS + owner_dev) * CAP + obs_slot % CAP
    model_eq = values.reshape(-1)[position]
    weighted = obs_weight * (model_eq - innovation)
    returned = jax.ops.segment_sum(weighted, position, num_segments=N_COLS * N_COLS * CAP).reshape(N_COLS * N_COLS, CAP) * live_mask
    adjoint = jnp.zeros(flattened.shape, jnp.float32).at[global_index.reshape(-1)].add(returned.reshape(-1)).reshape(increment.shape)
    static_grad = static_control + vertical(vertical_root.T, diffuse(adjoint))

    def member_grad(members_pair):
        member_pert, member_alpha = members_pair
        return member_alpha + member_scale * vertical(vertical_local.T, member_pert.astype(jnp.float32) * adjoint)
    ensemble_grad = lax.map(member_grad, (perturbations, ensemble_control))
    return (static_grad, ensemble_grad)
```

```python
import functools
import math

import jax
import jax.numpy as jnp
from jax import lax
from jax.experimental import pallas as pl
from jax.experimental.pallas import tpu as pltpu
from jax.sharding import PartitionSpec as P

NDIFF = 4
LANES = 128
VMEM_LIMIT = 48 * 1024 * 1024

precise = lax.Precision.HIGHEST

SMEM = pl.BlockSpec(memory_space=pltpu.SMEM)
VMEM = pl.BlockSpec(memory_space=pltpu.VMEM)


def params(**more):
    return pltpu.CompilerParams(vmem_limit_bytes=VMEM_LIMIT, **more)


def to_tiles(cells):
    lead = cells.shape[:-2]
    rows, length = cells.shape[-2:]
    split = cells.reshape(lead + (rows, length // LANES, LANES))
    return jnp.swapaxes(split, -3, -2).reshape(lead + (rows * length // LANES, LANES))


def from_tiles(tiles, rows):
    lead = tiles.shape[:-2]
    count = tiles.shape[-2] // rows
    split = tiles.reshape(lead + (count, rows, LANES))
    return jnp.swapaxes(split, -3, -2).reshape(lead + (rows, count * LANES))


def ens_kernel(scale, root_ref, control_ref, pert_ref, out_ref):
    levels = control_ref.shape[1]

    @pl.when(pl.program_id(0) == 0)
    def _():
        out_ref[...] = jnp.zeros_like(out_ref)

    def chunk(c, carry):
        rows = pl.ds(pl.multiple_of(c * 16, 16), 16)
        source = [control_ref[0, m, rows, :] for m in range(levels)]
        for l in range(levels):
            total = root_ref[l, 0] * source[0]
            for m in range(1, levels):
                total = total + root_ref[l, m] * source[m]
            out_ref[l, rows, :] += pert_ref[0, l, rows, :].astype(jnp.float32) * total * scale
        return carry

    lax.fori_loop(0, control_ref.shape[2] // 16, chunk, 0)


def ens_part(control, pert, root, scale):
    members, levels, rows, lanes = control.shape
    block = pl.BlockSpec((1, levels, rows, lanes), lambda k: (k, 0, 0, 0))
    return pl.pallas_call(
        functools.partial(ens_kernel, scale),
        grid=(members,),
        in_specs=[SMEM, block, block],
        out_specs=pl.BlockSpec((levels, rows, lanes), lambda k: (0, 0, 0)),
        out_shape=jax.ShapeDtypeStruct((levels, rows, lanes), jnp.float32),
        compiler_params=params(),
        name="ens_part",
    )(root, control, pert)


def grad_kernel(scale, root_ref, adjoint_ref, control_ref, pert_ref, out_ref):
    levels = control_ref.shape[1]

    def chunk(c, carry):
        rows = pl.ds(pl.multiple_of(c * 16, 16), 16)
        source = [
            pert_ref[0, m, rows, :].astype(jnp.float32) * adjoint_ref[m, rows, :] for m in range(levels)
        ]
        for l in range(levels):
            total = root_ref[0, l] * source[0]
            for m in range(1, levels):
                total = total + root_ref[m, l] * source[m]
            out_ref[0, l, rows, :] = control_ref[0, l, rows, :] + total * scale
        return carry

    lax.fori_loop(0, control_ref.shape[2] // 16, chunk, 0)


def ens_grad(adjoint, control, pert, root, scale):
    members, levels, rows, lanes = control.shape
    block = pl.BlockSpec((1, levels, rows, lanes), lambda k: (k, 0, 0, 0))
    return pl.pallas_call(
        functools.partial(grad_kernel, scale),
        grid=(members,),
        in_specs=[SMEM, pl.BlockSpec((levels, rows, lanes), lambda k: (0, 0, 0)), block, block],
        out_specs=block,
        out_shape=jax.ShapeDtypeStruct(control.shape, jnp.float32),
        compiler_params=params(),
        name="ens_grad",
    )(root, adjoint, control, pert)


def row_lookup(table_ref, row_ids, lane_ids):
    count = len(row_ids)

    def step(i, found):
        found = list(found)
        base = pl.multiple_of(i * 8, 8)
        rows = table_ref[pl.ds(base, 8), :]
        for s in range(8):
            row = jnp.broadcast_to(rows[s : s + 1, :], (8, LANES))
            for n in range(count):
                value = jnp.take_along_axis(row, lane_ids[n], axis=1)
                found[n] = jnp.where(row_ids[n] == base + s, value, found[n])
        return tuple(found)

    zero = jnp.zeros((8, LANES), jnp.float32)
    return lax.fori_loop(0, table_ref.shape[0] // 8, step, (zero,) * count)


def cell_place(index, first_cell, cells):
    inside = index - first_cell
    level = inside >> 13
    row = (level << 6) + (((inside >> 7) & 31) << 1) + ((inside >> 12) & 1)
    mine = (inside >= 0) & (inside < cells)
    return jnp.where(mine, row, -1), inside & (LANES - 1)


def live(counts_ref, first_list, slot0):
    rows = lax.broadcasted_iota(jnp.int32, (8, LANES), 0)
    limit = jnp.zeros((8, LANES), jnp.int32)
    for i in range(8):
        limit = jnp.where(rows == i, counts_ref[first_list + i], limit)
    slots = slot0 + lax.broadcasted_iota(jnp.int32, (8, LANES), 1)
    return slots < limit


def pick_kernel(first_ref, counts_ref, table_ref, index_ref, out_ref):
    lists, capacity = index_ref.shape
    cells = table_ref.shape[0] * LANES
    tiles = capacity // LANES

    def group(g, carry):
        places = []
        for t in range(tiles):
            index = index_ref[pl.ds(pl.multiple_of(g * 8, 8), 8), t * LANES : (t + 1) * LANES]
            row, lane = cell_place(index, first_ref[0], cells)
            row = jnp.where(live(counts_ref, g * 8, t * LANES), row, -1)
            places.append((row, lane))
        found = row_lookup(table_ref, [p[0] for p in places], [p[1] for p in places])
        for t in range(tiles):
            out_ref[pl.ds(g * 8 * tiles + t, 8, stride=tiles), :] = found[t]
        return carry

    lax.fori_loop(0, lists // 8, group, 0)


def pick(table, index, counts, first_cell):
    lists, capacity = index.shape
    return pl.pallas_call(
        pick_kernel,
        in_specs=[SMEM, SMEM, VMEM, VMEM],
        out_specs=VMEM,
        out_shape=jax.ShapeDtypeStruct((lists * capacity // LANES, LANES), jnp.float32),
        compiler_params=params(),
        name="pick",
    )(first_cell, counts, table, index)


def two_parts(values):
    high = values.astype(jnp.bfloat16)
    low = (values - high.astype(jnp.float32)).astype(jnp.bfloat16)
    return high, low


def one_hot_sum(rows, lanes, values, row_total):
    width = values.shape[1]
    one = jnp.bfloat16(1)
    zero = jnp.bfloat16(0)
    row_ids = lax.broadcasted_iota(jnp.int32, (row_total, width), 0)
    lane_ids = lax.broadcasted_iota(jnp.int32, (LANES, width), 0)
    row_hot = (rows == row_ids).astype(jnp.float32).astype(jnp.bfloat16)
    lane_hot = lanes == lane_ids
    high = values.astype(jnp.bfloat16).astype(jnp.float32)
    low = values - high
    parts = jnp.concatenate(
        [jnp.where(lane_hot, high, 0.0).astype(jnp.bfloat16), jnp.where(lane_hot, low, 0.0).astype(jnp.bfloat16)],
        axis=0,
    )
    both = lax.dot_general(
        row_hot, parts, (((1,), (1,)), ((), ())), preferred_element_type=jnp.float32
    )
    return both


def as_row(block):
    return jnp.concatenate([block[i : i + 1, :] for i in range(block.shape[0])], axis=1)


def obs_kernel(first_ref, table_ref, slot_ref, innovation_ref, weight_ref, out_ref, both_ref):
    rows = table_ref.shape[0]
    both_ref[...] = jnp.zeros_like(both_ref)
    group = 4

    def step(i, carry):
        base = pl.multiple_of(i * 8 * group, 8 * group)
        row_ids, lane_ids = [], []
        for n in range(group):
            inside = slot_ref[pl.ds(base + 8 * n, 8), :] - first_ref[0]
            row_ids.append(inside >> 7)
            lane_ids.append(inside & (LANES - 1))
        found = row_lookup(table_ref, row_ids, lane_ids)
        for n in range(group):
            at = pl.ds(base + 8 * n, 8)
            mine = (row_ids[n] >= 0) & (row_ids[n] < rows)
            weighted = jnp.where(mine, weight_ref[at, :] * (found[n] - innovation_ref[at, :]), 0.0)
            both_ref[...] += one_hot_sum(as_row(row_ids[n]), as_row(lane_ids[n]), as_row(weighted), rows)
        return carry

    lax.fori_loop(0, slot_ref.shape[0] // (8 * group), step, 0)
    out_ref[...] = both_ref[:, :LANES] + both_ref[:, LANES:]


def observe(table, slots, innovation, weight, first_slot):
    rows = table.shape[0]
    shaped = [a.reshape(-1, LANES) for a in (slots, innovation, weight)]
    return pl.pallas_call(
        obs_kernel,
        in_specs=[SMEM, VMEM, VMEM, VMEM, VMEM],
        out_specs=VMEM,
        out_shape=jax.ShapeDtypeStruct((rows, LANES), jnp.float32),
        scratch_shapes=[pltpu.VMEM((rows, 2 * LANES), jnp.float32)],
        compiler_params=params(),
        name="observe",
    )(first_slot, table, *shaped)


def spread_kernel(first_ref, counts_ref, arrived_ref, index_ref, out_ref, both_ref):
    lists, capacity = index_ref.shape
    tiles = capacity // LANES
    rows = out_ref.shape[0]
    cells = rows * LANES
    both_ref[...] = jnp.zeros_like(both_ref)

    def step(q, carry):
        values = as_row(arrived_ref[pl.ds(pl.multiple_of(q * tiles, tiles), tiles), :])
        index = index_ref[pl.ds(q, 1), :]
        row, lane = cell_place(index, first_ref[0], cells)
        slots = lax.broadcasted_iota(jnp.int32, (1, capacity), 1)
        values = jnp.where(slots < counts_ref[q], values, 0.0)
        both_ref[...] += one_hot_sum(row, lane, values, rows)
        return carry

    lax.fori_loop(0, lists, step, 0)
    out_ref[...] = both_ref[:, :LANES] + both_ref[:, LANES:]


def spread(arrived, index, counts, first_cell, rows):
    return pl.pallas_call(
        spread_kernel,
        in_specs=[SMEM, SMEM, VMEM, VMEM],
        out_specs=VMEM,
        out_shape=jax.ShapeDtypeStruct((rows, LANES), jnp.float32),
        scratch_shapes=[pltpu.VMEM((rows, 2 * LANES), jnp.float32)],
        compiler_params=params(),
        name="spread",
    )(first_cell, counts, arrived, index)


def shifted(shard, axis, by):
    length = lax.axis_size(axis)
    pairs = [(i, i + by) for i in range(length) if 0 <= i + by < length]
    return lax.ppermute(shard, axis, pairs)


def smooth(source, padded, k_north, k_south, k_east):
    upper_rows = padded[:, :-2]
    lower_rows = padded[:, 2:]
    eastern = jnp.roll(source, -1, axis=2)
    western = jnp.roll(source, 1, axis=2)
    k_west = jnp.roll(k_east, 1, axis=1)
    return (
        source
        + k_north * (upper_rows - source)
        + k_south * (lower_rows - source)
        + k_east * (eastern - source)
        + k_west * (western - source)
    )


def local(
    static_control,
    ensemble_control,
    perturbations,
    vertical_root,
    vertical_local,
    face_north,
    face_east,
    innovation,
    obs_weight,
    obs_slot,
    send_index,
    send_count,
):
    south_rim = shifted(face_north[:1], "cols", -1)
    k_south = jnp.concatenate([face_north[1:], south_rim], axis=0)

    def diffuse(source):
        for repeat in range(NDIFF):
            padded = jnp.concatenate(
                [shifted(source[:, -1:], "cols", 1), source, shifted(source[:, :1], "cols", -1)], axis=1
            )
            source = smooth(source, padded, face_north, k_south, face_east)
        return source

    levels, grid_rows, length = static_control.shape
    ens = lax.axis_size("ens")
    me = lax.axis_index("ens")
    own_levels = levels // ens
    member_scale = 1.0 / math.sqrt(ensemble_control.shape[0] * ens - 1)
    first_level = me * own_levels
    first_cell = (first_level * grid_rows * length).astype(jnp.int32).reshape(1)
    lists, capacity = send_index.shape
    list_rows = capacity // LANES
    own_lists = lists // ens

    control = to_tiles(ensemble_control)
    pert = to_tiles(perturbations)

    part = ens_part(control, pert, vertical_local, member_scale)
    own_root = lax.dynamic_slice_in_dim(vertical_root, first_level, own_levels, 0)
    static_increment = diffuse(jnp.einsum("lm,mrc->lrc", own_root, static_control, precision=precise))
    increment = lax.psum_scatter(part, "ens", scatter_dimension=0, tiled=True) + to_tiles(static_increment)
    picked = pick(increment.reshape(-1, LANES), send_index, send_count, first_cell)
    picked = lax.psum(picked, "ens").reshape(lists, list_rows, LANES)
    table = lax.all_to_all(picked, "cols", split_axis=0, concat_axis=0, tiled=True)
    table = lax.dynamic_slice_in_dim(table, me * own_lists, own_lists, 0).reshape(-1, LANES)
    first_slot = (me * own_lists * capacity).astype(jnp.int32).reshape(1)
    returned = observe(table, obs_slot, innovation, obs_weight, first_slot)
    sent = lax.dynamic_update_slice_in_dim(
        jnp.zeros((lists, list_rows, LANES), jnp.float32),
        returned.reshape(own_lists, list_rows, LANES),
        me * own_lists,
        0,
    )
    arrived = lax.psum(lax.all_to_all(sent, "cols", split_axis=0, concat_axis=0, tiled=True), "ens")
    adjoint = spread(arrived.reshape(-1, LANES), send_index, send_count, first_cell, own_levels * 64)
    adjoint = adjoint.reshape(own_levels, 64, LANES)
    whole = lax.all_gather(adjoint, "ens", axis=0, tiled=True)
    smoothed = diffuse(from_tiles(adjoint, grid_rows))
    smoothed = lax.all_gather(smoothed, "ens", axis=0, tiled=True)
    static_grad = static_control + jnp.einsum("ml,mrc->lrc", vertical_root, smoothed, precision=precise)
    ensemble_grad = ens_grad(whole, control, pert, vertical_local, member_scale)
    return (static_grad, from_tiles(ensemble_grad, grid_rows))


def solution(mesh):
    placed = (
        P(None, "cols", None),
        P("ens", None, "cols", None),
        P("ens", None, "cols", None),
        P(),
        P(),
        P("cols", None),
        P("cols", None),
        P("cols"),
        P("cols"),
        P("cols"),
        P("cols", None),
        P("cols"),
    )
    return jax.shard_map(
        local,
        mesh=mesh,
        in_specs=placed,
        out_specs=(P(None, "cols", None), P("ens", None, "cols", None)),
        check_vma=False,
    )
```

```python
import functools
import math

import jax
import jax.numpy as jnp
from jax import lax
from jax.experimental import pallas as pl
from jax.experimental.pallas import tpu as pltpu
from jax.sharding import PartitionSpec as P

NDIFF = 4
LANES = 128
VMEM_LIMIT = 48 * 1024 * 1024

precise = lax.Precision.HIGHEST

SMEM = pl.BlockSpec(memory_space=pltpu.SMEM)
VMEM = pl.BlockSpec(memory_space=pltpu.VMEM)


def params(**more):
    return pltpu.CompilerParams(vmem_limit_bytes=VMEM_LIMIT, **more)


def to_tiles(cells):
    lead = cells.shape[:-2]
    rows, length = cells.shape[-2:]
    split = cells.reshape(lead + (rows, length // LANES, LANES))
    return jnp.swapaxes(split, -3, -2).reshape(lead + (rows * length // LANES, LANES))


def from_tiles(tiles, rows):
    lead = tiles.shape[:-2]
    count = tiles.shape[-2] // rows
    split = tiles.reshape(lead + (count, rows, LANES))
    return jnp.swapaxes(split, -3, -2).reshape(lead + (rows, count * LANES))


def ens_kernel(scale, root_ref, control_ref, pert_ref, out_ref):
    levels = control_ref.shape[1]

    @pl.when(pl.program_id(0) == 0)
    def _():
        out_ref[...] = jnp.zeros_like(out_ref)

    def chunk(c, carry):
        rows = pl.ds(pl.multiple_of(c * 16, 16), 16)
        source = [control_ref[0, m, rows, :] for m in range(levels)]
        for l in range(levels):
            total = root_ref[l, 0] * source[0]
            for m in range(1, levels):
                total = total + root_ref[l, m] * source[m]
            out_ref[l, rows, :] += pert_ref[0, l, rows, :].astype(jnp.float32) * total * scale
        return carry

    lax.fori_loop(0, control_ref.shape[2] // 16, chunk, 0)


def ens_part(control, pert, root, scale):
    members, levels, rows, lanes = control.shape
    block = pl.BlockSpec((1, levels, rows, lanes), lambda k: (k, 0, 0, 0))
    return pl.pallas_call(
        functools.partial(ens_kernel, scale),
        grid=(members,),
        in_specs=[SMEM, block, block],
        out_specs=pl.BlockSpec((levels, rows, lanes), lambda k: (0, 0, 0)),
        out_shape=jax.ShapeDtypeStruct((levels, rows, lanes), jnp.float32),
        compiler_params=params(),
        name="ens_part",
    )(root, control, pert)


def grad_kernel(
    scale,
    local_ref,
    root_ref,
    adjoint_ref,
    smooth_ref,
    static_ref,
    control_ref,
    pert_ref,
    out_ref,
    static_out_ref,
):
    levels = control_ref.shape[1]
    k = pl.program_id(0)
    share_of = levels // pl.num_programs(0)

    def chunk(c, carry):
        rows = pl.ds(pl.multiple_of(c * 16, 16), 16)
        source = [
            pert_ref[0, m, rows, :].astype(jnp.float32) * adjoint_ref[m, rows, :] for m in range(levels)
        ]
        for l in range(levels):
            total = local_ref[0, l] * source[0]
            for m in range(1, levels):
                total = total + local_ref[m, l] * source[m]
            out_ref[0, l, rows, :] = control_ref[0, l, rows, :] + total * scale
        for n in range(2):
            l = k * share_of + n
            total = static_ref[l, rows, :]
            for m in range(levels):
                total = total + root_ref[m, l] * smooth_ref[m, rows, :]
            static_out_ref[l, rows, :] = total
        return carry

    lax.fori_loop(0, control_ref.shape[2] // 16, chunk, 0)


def gradients(adjoint, smoothed, control, pert, static, local_root, root, scale):
    members, levels, rows, lanes = control.shape
    block = pl.BlockSpec((1, levels, rows, lanes), lambda k: (k, 0, 0, 0))
    fixed = pl.BlockSpec((levels, rows, lanes), lambda k: (0, 0, 0))
    return pl.pallas_call(
        functools.partial(grad_kernel, scale),
        grid=(members,),
        in_specs=[SMEM, SMEM, fixed, fixed, fixed, block, block],
        out_specs=[block, fixed],
        out_shape=[
            jax.ShapeDtypeStruct(control.shape, jnp.float32),
            jax.ShapeDtypeStruct(static.shape, jnp.float32),
        ],
        compiler_params=params(),
        name="gradients",
    )(local_root, root, adjoint, smoothed, static, control, pert)


def row_lookup(table_ref, row_ids, lane_ids):
    count = len(row_ids)

    def step(i, found):
        found = list(found)
        base = pl.multiple_of(i * 8, 8)
        rows = table_ref[pl.ds(base, 8), :]
        for s in range(8):
            row = jnp.broadcast_to(rows[s : s + 1, :], (8, LANES))
            for n in range(count):
                value = jnp.take_along_axis(row, lane_ids[n], axis=1)
                found[n] = jnp.where(row_ids[n] == base + s, value, found[n])
        return tuple(found)

    zero = jnp.zeros((8, LANES), jnp.float32)
    return lax.fori_loop(0, table_ref.shape[0] // 8, step, (zero,) * count)


def cell_place(index, first_cell, cells):
    inside = index - first_cell
    level = inside >> 13
    row = (level << 6) + (((inside >> 7) & 31) << 1) + ((inside >> 12) & 1)
    mine = (inside >= 0) & (inside < cells)
    return jnp.where(mine, row, -1), inside & (LANES - 1)


def live(counts_ref, first_list, slot0):
    rows = lax.broadcasted_iota(jnp.int32, (8, LANES), 0)
    limit = jnp.zeros((8, LANES), jnp.int32)
    for i in range(8):
        limit = jnp.where(rows == i, counts_ref[first_list + i], limit)
    slots = slot0 + lax.broadcasted_iota(jnp.int32, (8, LANES), 1)
    return slots < limit


def pick_kernel(first_ref, counts_ref, table_ref, index_ref, out_ref):
    lists, capacity = index_ref.shape
    cells = table_ref.shape[0] * LANES
    tiles = capacity // LANES

    def group(g, carry):
        places = []
        for t in range(tiles):
            index = index_ref[pl.ds(pl.multiple_of(g * 8, 8), 8), t * LANES : (t + 1) * LANES]
            row, lane = cell_place(index, first_ref[0], cells)
            row = jnp.where(live(counts_ref, g * 8, t * LANES), row, -1)
            places.append((row, lane))
        found = row_lookup(table_ref, [p[0] for p in places], [p[1] for p in places])
        for t in range(tiles):
            out_ref[pl.ds(g * 8 * tiles + t, 8, stride=tiles), :] = found[t]
        return carry

    lax.fori_loop(0, lists // 8, group, 0)


def pick(table, index, counts, first_cell):
    lists, capacity = index.shape
    return pl.pallas_call(
        pick_kernel,
        in_specs=[SMEM, SMEM, VMEM, VMEM],
        out_specs=VMEM,
        out_shape=jax.ShapeDtypeStruct((lists * capacity // LANES, LANES), jnp.float32),
        compiler_params=params(),
        name="pick",
    )(first_cell, counts, table, index)


def two_parts(values):
    high = values.astype(jnp.bfloat16)
    low = (values - high.astype(jnp.float32)).astype(jnp.bfloat16)
    return high, low


def one_hot_sum(rows, lanes, values, row_total):
    width = values.shape[1]
    one = jnp.bfloat16(1)
    zero = jnp.bfloat16(0)
    row_ids = lax.broadcasted_iota(jnp.int32, (row_total, width), 0)
    lane_ids = lax.broadcasted_iota(jnp.int32, (LANES, width), 0)
    row_hot = (rows == row_ids).astype(jnp.float32).astype(jnp.bfloat16)
    lane_hot = lanes == lane_ids
    high = values.astype(jnp.bfloat16).astype(jnp.float32)
    low = values - high
    parts = jnp.concatenate(
        [jnp.where(lane_hot, high, 0.0).astype(jnp.bfloat16), jnp.where(lane_hot, low, 0.0).astype(jnp.bfloat16)],
        axis=0,
    )
    both = lax.dot_general(
        row_hot, parts, (((1,), (1,)), ((), ())), preferred_element_type=jnp.float32
    )
    return both


def as_row(block):
    return jnp.concatenate([block[i : i + 1, :] for i in range(block.shape[0])], axis=1)


def obs_kernel(first_ref, table_ref, slot_ref, innovation_ref, weight_ref, out_ref, both_ref):
    rows = table_ref.shape[0]
    both_ref[...] = jnp.zeros_like(both_ref)
    group = 4

    def step(i, carry):
        base = pl.multiple_of(i * 8 * group, 8 * group)
        row_ids, lane_ids = [], []
        for n in range(group):
            inside = slot_ref[pl.ds(base + 8 * n, 8), :] - first_ref[0]
            row_ids.append(inside >> 7)
            lane_ids.append(inside & (LANES - 1))
        found = row_lookup(table_ref, row_ids, lane_ids)
        for n in range(group):
            at = pl.ds(base + 8 * n, 8)
            mine = (row_ids[n] >= 0) & (row_ids[n] < rows)
            weighted = jnp.where(mine, weight_ref[at, :] * (found[n] - innovation_ref[at, :]), 0.0)
            both_ref[...] += one_hot_sum(as_row(row_ids[n]), as_row(lane_ids[n]), as_row(weighted), rows)
        return carry

    lax.fori_loop(0, slot_ref.shape[0] // (8 * group), step, 0)
    out_ref[...] = both_ref[:, :LANES] + both_ref[:, LANES:]


def observe(table, slots, innovation, weight, first_slot):
    rows = table.shape[0]
    shaped = [a.reshape(-1, LANES) for a in (slots, innovation, weight)]
    return pl.pallas_call(
        obs_kernel,
        in_specs=[SMEM, VMEM, VMEM, VMEM, VMEM],
        out_specs=VMEM,
        out_shape=jax.ShapeDtypeStruct((rows, LANES), jnp.float32),
        scratch_shapes=[pltpu.VMEM((rows, 2 * LANES), jnp.float32)],
        compiler_params=params(),
        name="observe",
    )(first_slot, table, *shaped)


def spread_kernel(first_ref, counts_ref, arrived_ref, index_ref, out_ref, both_ref):
    lists, capacity = index_ref.shape
    tiles = capacity // LANES
    rows = out_ref.shape[0]
    cells = rows * LANES
    both_ref[...] = jnp.zeros_like(both_ref)

    def step(q, carry):
        values = as_row(arrived_ref[pl.ds(pl.multiple_of(q * tiles, tiles), tiles), :])
        index = index_ref[pl.ds(q, 1), :]
        row, lane = cell_place(index, first_ref[0], cells)
        slots = lax.broadcasted_iota(jnp.int32, (1, capacity), 1)
        values = jnp.where(slots < counts_ref[q], values, 0.0)
        both_ref[...] += one_hot_sum(row, lane, values, rows)
        return carry

    lax.fori_loop(0, lists, step, 0)
    out_ref[...] = both_ref[:, :LANES] + both_ref[:, LANES:]


def spread(arrived, index, counts, first_cell, rows):
    return pl.pallas_call(
        spread_kernel,
        in_specs=[SMEM, SMEM, VMEM, VMEM],
        out_specs=VMEM,
        out_shape=jax.ShapeDtypeStruct((rows, LANES), jnp.float32),
        scratch_shapes=[pltpu.VMEM((rows, 2 * LANES), jnp.float32)],
        compiler_params=params(),
        name="spread",
    )(first_cell, counts, arrived, index)


MESH = pl.DeviceIdType.MESH


def spot(ens, cols):
    return {"ens": ens, "cols": cols}


def places():
    return (lax.axis_index("ens"), lax.axis_index("cols"), lax.axis_size("ens"), lax.axis_size("cols"))


def greet(barrier, target):
    pl.semaphore_signal(barrier, inc=1, device_id=target, device_id_type=MESH)


def send(source, landing, send_sem, recv_sem, target):
    copy = pltpu.make_async_remote_copy(
        src_ref=source,
        dst_ref=landing,
        send_sem=send_sem,
        recv_sem=recv_sem,
        device_id=target,
        device_id_type=MESH,
    )
    copy.start()
    return copy


def to_observers_kernel(picked_ref, out_ref, landing, send_sem, recv_sem):
    e, c, ens, cols = places()
    group = cols // ens
    z = c // group
    barrier = pltpu.get_barrier_semaphore()

    def hello(n, carry):
        e2 = n // group
        p = group * e + n % group

        @pl.when((e2 != e) | (p != c))
        def _():
            greet(barrier, spot(e2, p))

        return carry

    lax.fori_loop(0, cols, hello, 0)

    @pl.when(z == e)
    def _():
        pl.semaphore_wait(barrier, cols - 1)
        landing[e, c % group] = picked_ref[c]

    @pl.when(z != e)
    def _():
        pl.semaphore_wait(barrier, cols)
        send(picked_ref.at[c], landing.at[e, c % group], send_sem, recv_sem, spot(z, c))

    def step(d, carry):
        q = (c + d) % cols
        send(picked_ref.at[q], landing.at[e, c % group], send_sem, recv_sem, spot(z, q))
        return carry

    lax.fori_loop(1, cols, step, 0)
    wait_lists(z == e, picked_ref, send_sem, recv_sem, cols)
    total = landing[0]
    for n in range(1, ens):
        total = total + landing[n]
    out_ref[...] = total


def wait_lists(short, whole_ref, send_sem, recv_sem, count):
    few = whole_ref.at[pl.ds(0, count - 1)]

    @pl.when(short)
    def _():
        pltpu.make_async_copy(few, few, send_sem).wait()
        pltpu.make_async_copy(few, few, recv_sem).wait()

    @pl.when(jnp.logical_not(short))
    def _():
        pltpu.make_async_copy(whole_ref, whole_ref, send_sem).wait()
        pltpu.make_async_copy(whole_ref, whole_ref, recv_sem).wait()


def to_observers(picked, ens):
    lists, rows, lanes = picked.shape
    return pl.pallas_call(
        to_observers_kernel,
        in_specs=[VMEM],
        out_specs=VMEM,
        out_shape=jax.ShapeDtypeStruct((lists // ens, rows, lanes), jnp.float32),
        scratch_shapes=[
            pltpu.VMEM((ens, lists // ens, rows, lanes), jnp.float32),
            pltpu.SemaphoreType.DMA,
            pltpu.SemaphoreType.DMA,
        ],
        compiler_params=params(collective_id=1, has_side_effects=True),
        name="to_observers",
    )(picked)


def to_columns_kernel(returned_ref, out_ref, send_sem, recv_sem):
    e, c, ens, cols = places()
    group = cols // ens
    z = c // group
    barrier = pltpu.get_barrier_semaphore()

    def hello(d, carry):
        greet(barrier, spot(z, (c + d) % cols))
        return carry

    lax.fori_loop(1, cols, hello, 0)

    @pl.when(z == e)
    def _():
        pl.semaphore_wait(barrier, cols - 1)
        out_ref[c] = returned_ref[c % group]

    @pl.when(z != e)
    def _():
        greet(barrier, spot(z, c))
        pl.semaphore_wait(barrier, cols)

    def step(n, carry):
        e2 = n // group
        i = (c + n) % group

        @pl.when((e2 != e) | (group * e + i != c))
        def _():
            send(returned_ref.at[i], out_ref.at[c], send_sem, recv_sem, spot(e2, group * e + i))

        return carry

    lax.fori_loop(0, cols, step, 0)
    wait_lists(z == e, out_ref, send_sem, recv_sem, cols)


def to_columns(returned, ens):
    lists, rows, lanes = returned.shape
    return pl.pallas_call(
        to_columns_kernel,
        in_specs=[VMEM],
        out_specs=VMEM,
        out_shape=jax.ShapeDtypeStruct((lists * ens, rows, lanes), jnp.float32),
        scratch_shapes=[pltpu.SemaphoreType.DMA, pltpu.SemaphoreType.DMA],
        compiler_params=params(collective_id=2, has_side_effects=True),
        name="to_columns",
    )(returned)


def odd_rows():
    return (lax.broadcasted_iota(jnp.int32, (64, LANES), 0) & 1) == 1


def swapped(tile):
    return jnp.where(odd_rows(), pltpu.roll(tile, 1, 0), pltpu.roll(tile, 63, 0))


def east_of(tile):
    near = pltpu.roll(tile, LANES - 1, 1)
    lane = lax.broadcasted_iota(jnp.int32, (64, LANES), 1)
    return jnp.where(lane == LANES - 1, pltpu.roll(near, 62, 0), near)


def west_of(tile):
    near = pltpu.roll(tile, 1, 1)
    lane = lax.broadcasted_iota(jnp.int32, (64, LANES), 1)
    return jnp.where(lane == 0, pltpu.roll(near, 2, 0), near)


COEFS = 10


def make_coefs(coef_ref, north, east, north_up, east_up, north_down, east_down, has_up, has_down):
    odd = odd_rows()
    keep_up = has_up.astype(jnp.float32)
    keep_down = has_down.astype(jnp.float32)
    north_down = north_down * keep_down
    pair = jnp.where(odd, north, swapped(north))
    outer = jnp.where(odd, swapped(north_down), north)
    east_rim = jnp.where(odd, east_up, east_down)
    west = west_of(east)
    west_rim = west_of(east_rim)
    inner = swapped(outer)
    far = jnp.where(odd, north_up, swapped(north_down))
    coef_ref[0] = 1.0 - pair - outer - east - west
    coef_ref[1] = pair
    coef_ref[2] = outer * jnp.where(odd, keep_down, keep_up)
    coef_ref[3] = east
    coef_ref[4] = west
    coef_ref[5] = 1.0 - inner - far - east_rim - west_rim
    coef_ref[6] = inner
    coef_ref[7] = far
    coef_ref[8] = east_rim
    coef_ref[9] = west_rim


def two_steps(coef_ref, own, up, down):
    odd = odd_rows()
    rim = jnp.where(odd, up, down)
    far = jnp.where(odd, down, up)
    own_swap = swapped(own)
    first = (
        coef_ref[0] * own
        + coef_ref[1] * own_swap
        + coef_ref[2] * swapped(rim)
        + coef_ref[3] * east_of(own)
        + coef_ref[4] * west_of(own)
    )
    rim = (
        coef_ref[5] * rim
        + coef_ref[6] * own_swap
        + coef_ref[7] * swapped(far)
        + coef_ref[8] * east_of(rim)
        + coef_ref[9] * west_of(rim)
    )
    return (
        coef_ref[0] * first
        + coef_ref[1] * swapped(first)
        + coef_ref[2] * swapped(rim)
        + coef_ref[3] * east_of(first)
        + coef_ref[4] * west_of(first)
    )


def neighbours():
    e, c, ens, cols = places()
    return spot(e, (c + cols - 1) % cols), spot(e, (c + 1) % cols)


def exchange_tiles(source, landing, send_sems, recv_sems):
    upper, lower = neighbours()
    return [
        send(source, landing.at[0], send_sems.at[0], recv_sems.at[0], lower),
        send(source, landing.at[1], send_sems.at[1], recv_sems.at[1], upper),
    ]


def increment_kernel(
    root_ref,
    static_ref,
    part_ref,
    north_ref,
    east_ref,
    out_ref,
    coef_ref,
    faces,
    fields,
    halos,
    terms,
    face_send,
    face_recv,
    halo_send,
    halo_recv,
    term_send,
    term_recv,
):
    e, c, ens, cols = places()
    levels = static_ref.shape[0]
    own = levels // ens
    upper, lower = neighbours()
    barrier = pltpu.get_barrier_semaphore()
    for target in (upper, lower):
        greet(barrier, target)
    for d in range(1, ens):
        greet(barrier, spot((e + d) % ens, c))
    pl.semaphore_wait(barrier, ens + 1)

    copies = []
    for side, target in enumerate((lower, upper)):
        for n, source in enumerate((north_ref, east_ref)):
            copies.append(
                send(source, faces.at[side, n], face_send.at[side, n], face_recv.at[side, n], target)
            )
    sums = []
    for d in (2, 1, 3):
        peer = (e + d) % ens
        sums.append(
            send(
                part_ref.at[pl.ds(peer * own, own)],
                terms.at[d - 1],
                term_send.at[d - 1],
                term_recv.at[d - 1],
                spot(peer, c),
            )
        )

    def product(i, carry):
        l = i // 4
        rows = pl.ds(pl.multiple_of((i % 4) * 16, 16), 16)
        total = root_ref[e * own + l, 0] * static_ref[0, rows, :]
        for m in range(1, levels):
            total = total + root_ref[e * own + l, m] * static_ref[m, rows, :]
        fields[0, l, rows, :] = total
        return carry

    lax.fori_loop(0, own * 4, product, 0)
    halo = exchange_tiles(fields.at[0], halos.at[0], halo_send.at[0], halo_recv.at[0])
    for copy in copies:
        copy.wait()
    make_coefs(
        coef_ref,
        north_ref[...],
        east_ref[...],
        faces[0, 0],
        faces[0, 1],
        faces[1, 0],
        faces[1, 1],
        c > 0,
        c < cols - 1,
    )
    for copy in halo:
        copy.wait()
    for l in range(own):
        fields[1, l] = two_steps(coef_ref, fields[0, l], halos[0, 0, l], halos[0, 1, l])
    halo = exchange_tiles(fields.at[1], halos.at[1], halo_send.at[1], halo_recv.at[1])
    for copy in sums + halo:
        copy.wait()
    for l in range(own):
        total = two_steps(coef_ref, fields[1, l], halos[1, 0, l], halos[1, 1, l])
        total = total + part_ref[e * own + l]
        for d in range(ens - 1):
            total = total + terms[d, l]
        out_ref[l] = total


def increment_of(root, static, part, north, east, ens):
    levels, rows, lanes = static.shape
    own = levels // ens
    return pl.pallas_call(
        increment_kernel,
        in_specs=[SMEM, VMEM, VMEM, VMEM, VMEM],
        out_specs=[VMEM, VMEM],
        out_shape=[
            jax.ShapeDtypeStruct((own, rows, lanes), jnp.float32),
            jax.ShapeDtypeStruct((COEFS, rows, lanes), jnp.float32),
        ],
        scratch_shapes=[
            pltpu.VMEM((2, 2, rows, lanes), jnp.float32),
            pltpu.VMEM((2, own, rows, lanes), jnp.float32),
            pltpu.VMEM((2, 2, own, rows, lanes), jnp.float32),
            pltpu.VMEM((ens - 1, own, rows, lanes), jnp.float32),
            pltpu.SemaphoreType.DMA((2, 2)),
            pltpu.SemaphoreType.DMA((2, 2)),
            pltpu.SemaphoreType.DMA((2, 2)),
            pltpu.SemaphoreType.DMA((2, 2)),
            pltpu.SemaphoreType.DMA((ens - 1,)),
            pltpu.SemaphoreType.DMA((ens - 1,)),
        ],
        compiler_params=params(collective_id=3, has_side_effects=True),
        name="increment",
    )(root, static, part, north, east)


def share(own_ref, whole_ref, send_sems, recv_sems):
    e, c, ens, cols = places()
    own = own_ref.shape[0]
    return [
        send(
            own_ref,
            whole_ref.at[pl.ds(e * own, own)],
            send_sems.at[d - 1],
            recv_sems.at[d - 1],
            spot((e + d) % ens, c),
        )
        for d in (2, 1, 3)
    ]


def smooth_kernel(
    adjoint_ref,
    coef_ref,
    whole_ref,
    smooth_ref,
    fields,
    halos,
    halo_send,
    halo_recv,
    whole_send,
    whole_recv,
    smooth_send,
    smooth_recv,
):
    e, c, ens, cols = places()
    own = adjoint_ref.shape[0]
    upper, lower = neighbours()
    barrier = pltpu.get_barrier_semaphore()
    for target in (upper, lower):
        greet(barrier, target)
    for d in range(1, ens):
        greet(barrier, spot((e + d) % ens, c))
    pl.semaphore_wait(barrier, ens + 1)
    halo = exchange_tiles(adjoint_ref, halos.at[0], halo_send.at[0], halo_recv.at[0])
    wholes = share(adjoint_ref, whole_ref, whole_send, whole_recv)
    for l in range(own):
        whole_ref[e * own + l] = adjoint_ref[l]
    for copy in halo:
        copy.wait()
    for l in range(own):
        fields[0, l] = two_steps(coef_ref, adjoint_ref[l], halos[0, 0, l], halos[0, 1, l])
    halo = exchange_tiles(fields.at[0], halos.at[1], halo_send.at[1], halo_recv.at[1])
    for copy in halo:
        copy.wait()
    for l in range(own):
        fields[1, l] = two_steps(coef_ref, fields[0, l], halos[1, 0, l], halos[1, 1, l])
    smooths = share(fields.at[1], smooth_ref, smooth_send, smooth_recv)
    for l in range(own):
        smooth_ref[e * own + l] = fields[1, l]
    for copy in wholes + smooths:
        copy.wait()


def smooth_of(adjoint, coefs, ens):
    own, rows, lanes = adjoint.shape
    whole = jax.ShapeDtypeStruct((own * ens, rows, lanes), jnp.float32)
    return pl.pallas_call(
        smooth_kernel,
        in_specs=[VMEM, VMEM],
        out_specs=[VMEM, VMEM],
        out_shape=[whole, whole],
        scratch_shapes=[
            pltpu.VMEM((2, own, rows, lanes), jnp.float32),
            pltpu.VMEM((2, 2, own, rows, lanes), jnp.float32),
            pltpu.SemaphoreType.DMA((2, 2)),
            pltpu.SemaphoreType.DMA((2, 2)),
            pltpu.SemaphoreType.DMA((ens - 1,)),
            pltpu.SemaphoreType.DMA((ens - 1,)),
            pltpu.SemaphoreType.DMA((ens - 1,)),
            pltpu.SemaphoreType.DMA((ens - 1,)),
        ],
        compiler_params=params(collective_id=4, has_side_effects=True),
        name="smooth",
    )(adjoint, coefs)


def local(
    static_control,
    ensemble_control,
    perturbations,
    vertical_root,
    vertical_local,
    face_north,
    face_east,
    innovation,
    obs_weight,
    obs_slot,
    send_index,
    send_count,
):
    levels, grid_rows, length = static_control.shape
    ens = lax.axis_size("ens")
    me = lax.axis_index("ens")
    own_levels = levels // ens
    member_scale = 1.0 / math.sqrt(ensemble_control.shape[0] * ens - 1)
    first_cell = (me * own_levels * grid_rows * length).astype(jnp.int32).reshape(1)
    lists, capacity = send_index.shape
    list_rows = capacity // LANES
    own_lists = lists // ens
    first_slot = (me * own_lists * capacity).astype(jnp.int32).reshape(1)

    static = to_tiles(static_control)
    control = to_tiles(ensemble_control)
    pert = to_tiles(perturbations)

    part = ens_part(control, pert, vertical_local, member_scale)
    increment, coefs = increment_of(
        vertical_root, static, part, to_tiles(face_north), to_tiles(face_east), ens
    )
    picked = pick(increment.reshape(-1, LANES), send_index, send_count, first_cell)
    table = to_observers(picked.reshape(lists, list_rows, LANES), ens).reshape(-1, LANES)
    returned = observe(table, obs_slot, innovation, obs_weight, first_slot)
    arrived = to_columns(returned.reshape(own_lists, list_rows, LANES), ens)
    adjoint = spread(arrived.reshape(-1, LANES), send_index, send_count, first_cell, own_levels * 64)
    whole, smoothed = smooth_of(adjoint.reshape(own_levels, 64, LANES), coefs, ens)
    ensemble_grad, static_grad = gradients(
        whole, smoothed, control, pert, static, vertical_local, vertical_root, member_scale
    )
    return (from_tiles(static_grad, grid_rows), from_tiles(ensemble_grad, grid_rows))


def solution(mesh):
    placed = (
        P(None, "cols", None),
        P("ens", None, "cols", None),
        P("ens", None, "cols", None),
        P(),
        P(),
        P("cols", None),
        P("cols", None),
        P("cols"),
        P("cols"),
        P("cols"),
        P("cols", None),
        P("cols"),
    )
    return jax.shard_map(
        local,
        mesh=mesh,
        in_specs=placed,
        out_specs=(P(None, "cols", None), P("ens", None, "cols", None)),
        check_vma=False,
    )
```

```python
import functools
import math

import jax
import jax.numpy as jnp
from jax import lax
from jax.experimental import pallas as pl
from jax.experimental.pallas import tpu as pltpu
from jax.sharding import PartitionSpec as P

NDIFF = 4
LANES = 128
VMEM_LIMIT = 48 * 1024 * 1024

precise = lax.Precision.HIGHEST

SMEM = pl.BlockSpec(memory_space=pltpu.SMEM)
VMEM = pl.BlockSpec(memory_space=pltpu.VMEM)


def params(**more):
    return pltpu.CompilerParams(vmem_limit_bytes=VMEM_LIMIT, **more)


def to_tiles(cells):
    lead = cells.shape[:-2]
    rows, length = cells.shape[-2:]
    split = cells.reshape(lead + (rows, length // LANES, LANES))
    return jnp.swapaxes(split, -3, -2).reshape(lead + (rows * length // LANES, LANES))


def from_tiles(tiles, rows):
    lead = tiles.shape[:-2]
    count = tiles.shape[-2] // rows
    split = tiles.reshape(lead + (count, rows, LANES))
    return jnp.swapaxes(split, -3, -2).reshape(lead + (rows, count * LANES))


def ens_kernel(scale, root_ref, control_ref, pert_ref, out_ref):
    levels = control_ref.shape[1]

    @pl.when(pl.program_id(0) == 0)
    def _():
        out_ref[...] = jnp.zeros_like(out_ref)

    def chunk(c, carry):
        rows = pl.ds(pl.multiple_of(c * 16, 16), 16)
        source = [control_ref[0, m, rows, :] for m in range(levels)]
        for l in range(levels):
            total = root_ref[l, 0] * source[0]
            for m in range(1, levels):
                total = total + root_ref[l, m] * source[m]
            out_ref[l, rows, :] += pert_ref[0, l, rows, :].astype(jnp.float32) * total * scale
        return carry

    lax.fori_loop(0, control_ref.shape[2] // 16, chunk, 0)


def ens_part(control, pert, root, scale):
    members, levels, rows, lanes = control.shape
    block = pl.BlockSpec((1, levels, rows, lanes), lambda k: (k, 0, 0, 0))
    return pl.pallas_call(
        functools.partial(ens_kernel, scale),
        grid=(members,),
        in_specs=[SMEM, block, block],
        out_specs=pl.BlockSpec((levels, rows, lanes), lambda k: (0, 0, 0)),
        out_shape=jax.ShapeDtypeStruct((levels, rows, lanes), jnp.float32),
        compiler_params=params(),
        name="ens_part",
    )(root, control, pert)


def grad_kernel(
    scale,
    local_ref,
    root_ref,
    adjoint_ref,
    smooth_ref,
    static_ref,
    control_ref,
    pert_ref,
    out_ref,
    static_out_ref,
):
    levels = control_ref.shape[1]
    k = pl.program_id(0)
    share_of = levels // pl.num_programs(0)

    def chunk(c, carry):
        rows = pl.ds(pl.multiple_of(c * 16, 16), 16)
        source = [
            pert_ref[0, m, rows, :].astype(jnp.float32) * adjoint_ref[m, rows, :] for m in range(levels)
        ]
        for l in range(levels):
            total = local_ref[0, l] * source[0]
            for m in range(1, levels):
                total = total + local_ref[m, l] * source[m]
            out_ref[0, l, rows, :] = control_ref[0, l, rows, :] + total * scale
        for n in range(2):
            l = k * share_of + n
            total = static_ref[l, rows, :]
            for m in range(levels):
                total = total + root_ref[m, l] * smooth_ref[m, rows, :]
            static_out_ref[l, rows, :] = total
        return carry

    lax.fori_loop(0, control_ref.shape[2] // 16, chunk, 0)


def gradients(adjoint, smoothed, control, pert, static, local_root, root, scale):
    members, levels, rows, lanes = control.shape
    block = pl.BlockSpec((1, levels, rows, lanes), lambda k: (k, 0, 0, 0))
    fixed = pl.BlockSpec((levels, rows, lanes), lambda k: (0, 0, 0))
    return pl.pallas_call(
        functools.partial(grad_kernel, scale),
        grid=(members,),
        in_specs=[SMEM, SMEM, fixed, fixed, fixed, block, block],
        out_specs=[block, fixed],
        out_shape=[
            jax.ShapeDtypeStruct(control.shape, jnp.float32),
            jax.ShapeDtypeStruct(static.shape, jnp.float32),
        ],
        compiler_params=params(),
        name="gradients",
    )(local_root, root, adjoint, smoothed, static, control, pert)


def iota(shape, dim):
    return lax.broadcasted_iota(jnp.int32, shape, dim)


def small(ids):
    return ids.astype(jnp.float32).astype(jnp.bfloat16)


def one_hot(ids, count):
    width = ids.shape[1]
    hit = small(iota((count, width), 0)) == small(ids)
    return jnp.where(hit, jnp.bfloat16(1), jnp.bfloat16(0))


def table_parts(table, parts_ref):
    lanes = table.shape[1]
    high = table.astype(jnp.bfloat16).astype(jnp.float32)
    parts_ref[:lanes, :] = high.T.astype(jnp.bfloat16)
    parts_ref[lanes:, :] = (table - high).T.astype(jnp.bfloat16)


def look_up(parts_ref, hot, lane):
    lanes = parts_ref.shape[0] // 2
    found = jnp.dot(parts_ref[...], hot, preferred_element_type=jnp.float32)
    found = found[:lanes] + found[lanes:]
    found = jnp.where(iota(found.shape, 0) == lane, found, 0.0)
    return jnp.sum(found, axis=0, keepdims=True)


def sum_up(hot, lane, values, lanes):
    high = values.astype(jnp.bfloat16)
    low = (values - high.astype(jnp.float32)).astype(jnp.bfloat16)
    hit = small(iota((lanes, lane.shape[1]), 0)) == small(lane)
    zero = jnp.bfloat16(0)
    parts = jnp.concatenate([jnp.where(hit, high, zero), jnp.where(hit, low, zero)], axis=0)
    return lax.dot_general(hot, parts, (((1,), (1,)), ((), ())), preferred_element_type=jnp.float32)


def as_row(block):
    return jnp.concatenate([block[i : i + 1, :] for i in range(block.shape[0])], axis=1)


def cell_place(index, first_cell, cells):
    inside = index - first_cell
    level = inside >> 13
    row = (level << 6) + (((inside >> 7) & 31) << 1) + ((inside >> 12) & 1)
    mine = (inside >= 0) & (inside < cells)
    return jnp.where(mine, row, -1), inside & (LANES - 1)


def pick_kernel(first_ref, counts_ref, table_ref, index_ref, out_ref, parts_ref):
    lists, capacity = index_ref.shape
    rows = table_ref.shape[0]
    tiles = capacity // LANES
    table_parts(table_ref[...], parts_ref)
    slots = iota((1, capacity), 1)

    def step(i, carry):
        for j in range(8):
            q = i * 8 + j
            row, lane = cell_place(index_ref[pl.ds(q, 1), :], first_ref[0], rows * LANES)
            row = jnp.where(slots < counts_ref[q], row, -1)
            found = look_up(parts_ref, one_hot(row, rows), lane)
            for t in range(tiles):
                out_ref[pl.ds(q * tiles + t, 1), :] = found[:, t * LANES : (t + 1) * LANES]
        return carry

    lax.fori_loop(0, lists // 8, step, 0)


def pick(table, index, counts, first_cell):
    lists, capacity = index.shape
    return pl.pallas_call(
        pick_kernel,
        in_specs=[SMEM, SMEM, VMEM, VMEM],
        out_specs=VMEM,
        out_shape=jax.ShapeDtypeStruct((lists * capacity // LANES, LANES), jnp.float32),
        scratch_shapes=[pltpu.VMEM((2 * LANES, table.shape[0]), jnp.bfloat16)],
        compiler_params=params(),
        name="pick",
    )(first_cell, counts, table, index)


HALF = 64


def obs_kernel(first_ref, table_ref, slot_ref, innovation_ref, weight_ref, out_ref, parts_ref, both_ref):
    rows = 2 * table_ref.shape[0]
    table = table_ref[...]
    table_parts(jnp.concatenate([table[:, :HALF], table[:, HALF:]], axis=0), parts_ref)
    both_ref[...] = jnp.zeros_like(both_ref)
    group = 32

    def step(i, carry):
        total = jnp.zeros(both_ref.shape, jnp.float32)
        for j in range(2):
            at = pl.ds(pl.multiple_of((i * 2 + j) * group, group), group)
            inside = as_row(slot_ref[at, :]) - first_ref[0]
            whole = inside >> 7
            mine = (inside >= 0) & (whole < rows // 2)
            row = jnp.where(mine, whole + ((inside >> 6) & 1) * (rows // 2), -1)
            lane = inside & (HALF - 1)
            hot = one_hot(row, rows)
            found = look_up(parts_ref, hot, lane)
            weighted = as_row(weight_ref[at, :]) * (found - as_row(innovation_ref[at, :]))
            total = total + sum_up(hot, lane, jnp.where(mine, weighted, 0.0), HALF)
        both_ref[...] += total
        return carry

    lax.fori_loop(0, slot_ref.shape[0] // (2 * group), step, 0)
    sums = both_ref[:, :HALF] + both_ref[:, HALF:]
    out_ref[...] = jnp.concatenate([sums[: rows // 2], sums[rows // 2 :]], axis=1)


def observe(table, slots, innovation, weight, first_slot):
    rows = table.shape[0]
    shaped = [a.reshape(-1, LANES) for a in (slots, innovation, weight)]
    return pl.pallas_call(
        obs_kernel,
        in_specs=[SMEM, VMEM, VMEM, VMEM, VMEM],
        out_specs=VMEM,
        out_shape=jax.ShapeDtypeStruct((rows, LANES), jnp.float32),
        scratch_shapes=[
            pltpu.VMEM((2 * HALF, 2 * rows), jnp.bfloat16),
            pltpu.VMEM((2 * rows, 2 * HALF), jnp.float32),
        ],
        compiler_params=params(),
        name="observe",
    )(first_slot, table, *shaped)


def spread_kernel(first_ref, counts_ref, arrived_ref, index_ref, out_ref, both_ref):
    lists, capacity = index_ref.shape
    tiles = capacity // LANES
    rows = out_ref.shape[0]
    both_ref[...] = jnp.zeros_like(both_ref)
    slots = iota((1, capacity), 1)

    def step(i, carry):
        total = jnp.zeros(both_ref.shape, jnp.float32)
        for j in range(8):
            q = i * 8 + j
            values = as_row(arrived_ref[pl.ds(pl.multiple_of(q * tiles, tiles), tiles), :])
            row, lane = cell_place(index_ref[pl.ds(q, 1), :], first_ref[0], rows * LANES)
            row = jnp.where(slots < counts_ref[q], row, -1)
            total = total + sum_up(one_hot(row, rows), lane, values, LANES)
        both_ref[...] += total
        return carry

    lax.fori_loop(0, lists // 8, step, 0)
    out_ref[...] = both_ref[:, :LANES] + both_ref[:, LANES:]


def spread(arrived, index, counts, first_cell, rows):
    return pl.pallas_call(
        spread_kernel,
        in_specs=[SMEM, SMEM, VMEM, VMEM],
        out_specs=VMEM,
        out_shape=jax.ShapeDtypeStruct((rows, LANES), jnp.float32),
        scratch_shapes=[pltpu.VMEM((rows, 2 * LANES), jnp.float32)],
        compiler_params=params(),
        name="spread",
    )(first_cell, counts, arrived, index)


MESH = pl.DeviceIdType.MESH


def spot(ens, cols):
    return {"ens": ens, "cols": cols}


def places():
    return (lax.axis_index("ens"), lax.axis_index("cols"), lax.axis_size("ens"), lax.axis_size("cols"))


def greet(barrier, target):
    pl.semaphore_signal(barrier, inc=1, device_id=target, device_id_type=MESH)


def send(source, landing, send_sem, recv_sem, target):
    copy = pltpu.make_async_remote_copy(
        src_ref=source,
        dst_ref=landing,
        send_sem=send_sem,
        recv_sem=recv_sem,
        device_id=target,
        device_id_type=MESH,
    )
    copy.start()
    return copy


def to_observers_kernel(picked_ref, out_ref, landing, send_sem, recv_sem):
    e, c, ens, cols = places()
    group = cols // ens
    z = c // group
    barrier = pltpu.get_barrier_semaphore()

    def hello(n, carry):
        e2 = n // group
        p = group * e + n % group

        @pl.when((e2 != e) | (p != c))
        def _():
            greet(barrier, spot(e2, p))

        return carry

    lax.fori_loop(0, cols, hello, 0)

    @pl.when(z == e)
    def _():
        pl.semaphore_wait(barrier, cols - 1)
        landing[e, c % group] = picked_ref[c]

    @pl.when(z != e)
    def _():
        pl.semaphore_wait(barrier, cols)
        send(picked_ref.at[c], landing.at[e, c % group], send_sem, recv_sem, spot(z, c))

    def step(d, carry):
        q = (c + d) % cols
        send(picked_ref.at[q], landing.at[e, c % group], send_sem, recv_sem, spot(z, q))
        return carry

    lax.fori_loop(1, cols, step, 0)
    wait_lists(z == e, picked_ref, send_sem, recv_sem, cols)
    total = landing[0]
    for n in range(1, ens):
        total = total + landing[n]
    out_ref[...] = total


def wait_lists(short, whole_ref, send_sem, recv_sem, count):
    few = whole_ref.at[pl.ds(0, count - 1)]

    @pl.when(short)
    def _():
        pltpu.make_async_copy(few, few, send_sem).wait()
        pltpu.make_async_copy(few, few, recv_sem).wait()

    @pl.when(jnp.logical_not(short))
    def _():
        pltpu.make_async_copy(whole_ref, whole_ref, send_sem).wait()
        pltpu.make_async_copy(whole_ref, whole_ref, recv_sem).wait()


def to_observers(picked, ens):
    lists, rows, lanes = picked.shape
    return pl.pallas_call(
        to_observers_kernel,
        in_specs=[VMEM],
        out_specs=VMEM,
        out_shape=jax.ShapeDtypeStruct((lists // ens, rows, lanes), jnp.float32),
        scratch_shapes=[
            pltpu.VMEM((ens, lists // ens, rows, lanes), jnp.float32),
            pltpu.SemaphoreType.DMA,
            pltpu.SemaphoreType.DMA,
        ],
        compiler_params=params(collective_id=1, has_side_effects=True),
        name="to_observers",
    )(picked)


def to_columns_kernel(returned_ref, out_ref, send_sem, recv_sem):
    e, c, ens, cols = places()
    group = cols // ens
    z = c // group
    barrier = pltpu.get_barrier_semaphore()

    def hello(d, carry):
        greet(barrier, spot(z, (c + d) % cols))
        return carry

    lax.fori_loop(1, cols, hello, 0)

    @pl.when(z == e)
    def _():
        pl.semaphore_wait(barrier, cols - 1)
        out_ref[c] = returned_ref[c % group]

    @pl.when(z != e)
    def _():
        greet(barrier, spot(z, c))
        pl.semaphore_wait(barrier, cols)

    def step(n, carry):
        e2 = n // group
        i = (c + n) % group

        @pl.when((e2 != e) | (group * e + i != c))
        def _():
            send(returned_ref.at[i], out_ref.at[c], send_sem, recv_sem, spot(e2, group * e + i))

        return carry

    lax.fori_loop(0, cols, step, 0)
    wait_lists(z == e, out_ref, send_sem, recv_sem, cols)


def to_columns(returned, ens):
    lists, rows, lanes = returned.shape
    return pl.pallas_call(
        to_columns_kernel,
        in_specs=[VMEM],
        out_specs=VMEM,
        out_shape=jax.ShapeDtypeStruct((lists * ens, rows, lanes), jnp.float32),
        scratch_shapes=[pltpu.SemaphoreType.DMA, pltpu.SemaphoreType.DMA],
        compiler_params=params(collective_id=2, has_side_effects=True),
        name="to_columns",
    )(returned)


def odd_rows():
    return (lax.broadcasted_iota(jnp.int32, (64, LANES), 0) & 1) == 1


def swapped(tile):
    return jnp.where(odd_rows(), pltpu.roll(tile, 1, 0), pltpu.roll(tile, 63, 0))


def east_of(tile):
    near = pltpu.roll(tile, LANES - 1, 1)
    lane = lax.broadcasted_iota(jnp.int32, (64, LANES), 1)
    return jnp.where(lane == LANES - 1, pltpu.roll(near, 62, 0), near)


def west_of(tile):
    near = pltpu.roll(tile, 1, 1)
    lane = lax.broadcasted_iota(jnp.int32, (64, LANES), 1)
    return jnp.where(lane == 0, pltpu.roll(near, 2, 0), near)


COEFS = 10


def make_coefs(coef_ref, north, east, north_up, east_up, north_down, east_down, has_up, has_down):
    odd = odd_rows()
    keep_up = has_up.astype(jnp.float32)
    keep_down = has_down.astype(jnp.float32)
    north_down = north_down * keep_down
    pair = jnp.where(odd, north, swapped(north))
    outer = jnp.where(odd, swapped(north_down), north)
    east_rim = jnp.where(odd, east_up, east_down)
    west = west_of(east)
    west_rim = west_of(east_rim)
    inner = swapped(outer)
    far = jnp.where(odd, north_up, swapped(north_down))
    coef_ref[0] = 1.0 - pair - outer - east - west
    coef_ref[1] = pair
    coef_ref[2] = outer * jnp.where(odd, keep_down, keep_up)
    coef_ref[3] = east
    coef_ref[4] = west
    coef_ref[5] = 1.0 - inner - far - east_rim - west_rim
    coef_ref[6] = inner
    coef_ref[7] = far
    coef_ref[8] = east_rim
    coef_ref[9] = west_rim


def two_steps(coef_ref, own, up, down):
    odd = odd_rows()
    rim = jnp.where(odd, up, down)
    far = jnp.where(odd, down, up)
    own_swap = swapped(own)
    first = (
        coef_ref[0] * own
        + coef_ref[1] * own_swap
        + coef_ref[2] * swapped(rim)
        + coef_ref[3] * east_of(own)
        + coef_ref[4] * west_of(own)
    )
    rim = (
        coef_ref[5] * rim
        + coef_ref[6] * own_swap
        + coef_ref[7] * swapped(far)
        + coef_ref[8] * east_of(rim)
        + coef_ref[9] * west_of(rim)
    )
    return (
        coef_ref[0] * first
        + coef_ref[1] * swapped(first)
        + coef_ref[2] * swapped(rim)
        + coef_ref[3] * east_of(first)
        + coef_ref[4] * west_of(first)
    )


def neighbours():
    e, c, ens, cols = places()
    return spot(e, (c + cols - 1) % cols), spot(e, (c + 1) % cols)


def exchange_tiles(source, landing, send_sems, recv_sems):
    upper, lower = neighbours()
    return [
        send(source, landing.at[0], send_sems.at[0], recv_sems.at[0], lower),
        send(source, landing.at[1], send_sems.at[1], recv_sems.at[1], upper),
    ]


def increment_kernel(
    root_ref,
    static_ref,
    part_ref,
    north_ref,
    east_ref,
    out_ref,
    coef_ref,
    faces,
    fields,
    halos,
    terms,
    face_send,
    face_recv,
    halo_send,
    halo_recv,
    term_send,
    term_recv,
):
    e, c, ens, cols = places()
    levels = static_ref.shape[0]
    own = levels // ens
    upper, lower = neighbours()
    barrier = pltpu.get_barrier_semaphore()
    for target in (upper, lower):
        greet(barrier, target)
    for d in range(1, ens):
        greet(barrier, spot((e + d) % ens, c))
    pl.semaphore_wait(barrier, ens + 1)

    copies = []
    for side, target in enumerate((lower, upper)):
        for n, source in enumerate((north_ref, east_ref)):
            copies.append(
                send(source, faces.at[side, n], face_send.at[side, n], face_recv.at[side, n], target)
            )
    sums = []
    for d in (2, 1, 3):
        peer = (e + d) % ens
        sums.append(
            send(
                part_ref.at[pl.ds(peer * own, own)],
                terms.at[d - 1],
                term_send.at[d - 1],
                term_recv.at[d - 1],
                spot(peer, c),
            )
        )

    def product(i, carry):
        l = i // 4
        rows = pl.ds(pl.multiple_of((i % 4) * 16, 16), 16)
        total = root_ref[e * own + l, 0] * static_ref[0, rows, :]
        for m in range(1, levels):
            total = total + root_ref[e * own + l, m] * static_ref[m, rows, :]
        fields[0, l, rows, :] = total
        return carry

    lax.fori_loop(0, own * 4, product, 0)
    halo = exchange_tiles(fields.at[0], halos.at[0], halo_send.at[0], halo_recv.at[0])
    for copy in copies:
        copy.wait()
    make_coefs(
        coef_ref,
        north_ref[...],
        east_ref[...],
        faces[0, 0],
        faces[0, 1],
        faces[1, 0],
        faces[1, 1],
        c > 0,
        c < cols - 1,
    )
    for copy in halo:
        copy.wait()
    for l in range(own):
        fields[1, l] = two_steps(coef_ref, fields[0, l], halos[0, 0, l], halos[0, 1, l])
    halo = exchange_tiles(fields.at[1], halos.at[1], halo_send.at[1], halo_recv.at[1])
    for copy in sums + halo:
        copy.wait()
    for l in range(own):
        total = two_steps(coef_ref, fields[1, l], halos[1, 0, l], halos[1, 1, l])
        total = total + part_ref[e * own + l]
        for d in range(ens - 1):
            total = total + terms[d, l]
        out_ref[l] = total


def increment_of(root, static, part, north, east, ens):
    levels, rows, lanes = static.shape
    own = levels // ens
    return pl.pallas_call(
        increment_kernel,
        in_specs=[SMEM, VMEM, VMEM, VMEM, VMEM],
        out_specs=[VMEM, VMEM],
        out_shape=[
            jax.ShapeDtypeStruct((own, rows, lanes), jnp.float32),
            jax.ShapeDtypeStruct((COEFS, rows, lanes), jnp.float32),
        ],
        scratch_shapes=[
            pltpu.VMEM((2, 2, rows, lanes), jnp.float32),
            pltpu.VMEM((2, own, rows, lanes), jnp.float32),
            pltpu.VMEM((2, 2, own, rows, lanes), jnp.float32),
            pltpu.VMEM((ens - 1, own, rows, lanes), jnp.float32),
            pltpu.SemaphoreType.DMA((2, 2)),
            pltpu.SemaphoreType.DMA((2, 2)),
            pltpu.SemaphoreType.DMA((2, 2)),
            pltpu.SemaphoreType.DMA((2, 2)),
            pltpu.SemaphoreType.DMA((ens - 1,)),
            pltpu.SemaphoreType.DMA((ens - 1,)),
        ],
        compiler_params=params(collective_id=3, has_side_effects=True),
        name="increment",
    )(root, static, part, north, east)


def share(own_ref, whole_ref, send_sems, recv_sems):
    e, c, ens, cols = places()
    own = own_ref.shape[0]
    return [
        send(
            own_ref,
            whole_ref.at[pl.ds(e * own, own)],
            send_sems.at[d - 1],
            recv_sems.at[d - 1],
            spot((e + d) % ens, c),
        )
        for d in (2, 1, 3)
    ]


def smooth_kernel(
    adjoint_ref,
    coef_ref,
    whole_ref,
    smooth_ref,
    fields,
    halos,
    halo_send,
    halo_recv,
    whole_send,
    whole_recv,
    smooth_send,
    smooth_recv,
):
    e, c, ens, cols = places()
    own = adjoint_ref.shape[0]
    upper, lower = neighbours()
    barrier = pltpu.get_barrier_semaphore()
    for target in (upper, lower):
        greet(barrier, target)
    for d in range(1, ens):
        greet(barrier, spot((e + d) % ens, c))
    pl.semaphore_wait(barrier, ens + 1)
    halo = exchange_tiles(adjoint_ref, halos.at[0], halo_send.at[0], halo_recv.at[0])
    wholes = share(adjoint_ref, whole_ref, whole_send, whole_recv)
    for l in range(own):
        whole_ref[e * own + l] = adjoint_ref[l]
    for copy in halo:
        copy.wait()
    for l in range(own):
        fields[0, l] = two_steps(coef_ref, adjoint_ref[l], halos[0, 0, l], halos[0, 1, l])
    halo = exchange_tiles(fields.at[0], halos.at[1], halo_send.at[1], halo_recv.at[1])
    for copy in halo:
        copy.wait()
    for l in range(own):
        fields[1, l] = two_steps(coef_ref, fields[0, l], halos[1, 0, l], halos[1, 1, l])
    smooths = share(fields.at[1], smooth_ref, smooth_send, smooth_recv)
    for l in range(own):
        smooth_ref[e * own + l] = fields[1, l]
    for copy in wholes + smooths:
        copy.wait()


def smooth_of(adjoint, coefs, ens):
    own, rows, lanes = adjoint.shape
    whole = jax.ShapeDtypeStruct((own * ens, rows, lanes), jnp.float32)
    return pl.pallas_call(
        smooth_kernel,
        in_specs=[VMEM, VMEM],
        out_specs=[VMEM, VMEM],
        out_shape=[whole, whole],
        scratch_shapes=[
            pltpu.VMEM((2, own, rows, lanes), jnp.float32),
            pltpu.VMEM((2, 2, own, rows, lanes), jnp.float32),
            pltpu.SemaphoreType.DMA((2, 2)),
            pltpu.SemaphoreType.DMA((2, 2)),
            pltpu.SemaphoreType.DMA((ens - 1,)),
            pltpu.SemaphoreType.DMA((ens - 1,)),
            pltpu.SemaphoreType.DMA((ens - 1,)),
            pltpu.SemaphoreType.DMA((ens - 1,)),
        ],
        compiler_params=params(collective_id=4, has_side_effects=True),
        name="smooth",
    )(adjoint, coefs)


def local(
    static_control,
    ensemble_control,
    perturbations,
    vertical_root,
    vertical_local,
    face_north,
    face_east,
    innovation,
    obs_weight,
    obs_slot,
    send_index,
    send_count,
):
    levels, grid_rows, length = static_control.shape
    ens = lax.axis_size("ens")
    me = lax.axis_index("ens")
    own_levels = levels // ens
    member_scale = 1.0 / math.sqrt(ensemble_control.shape[0] * ens - 1)
    first_cell = (me * own_levels * grid_rows * length).astype(jnp.int32).reshape(1)
    lists, capacity = send_index.shape
    list_rows = capacity // LANES
    own_lists = lists // ens
    first_slot = (me * own_lists * capacity).astype(jnp.int32).reshape(1)

    static = to_tiles(static_control)
    control = to_tiles(ensemble_control)
    pert = to_tiles(perturbations)

    part = ens_part(control, pert, vertical_local, member_scale)
    increment, coefs = increment_of(
        vertical_root, static, part, to_tiles(face_north), to_tiles(face_east), ens
    )
    picked = pick(increment.reshape(-1, LANES), send_index, send_count, first_cell)
    table = to_observers(picked.reshape(lists, list_rows, LANES), ens).reshape(-1, LANES)
    returned = observe(table, obs_slot, innovation, obs_weight, first_slot)
    arrived = to_columns(returned.reshape(own_lists, list_rows, LANES), ens)
    adjoint = spread(arrived.reshape(-1, LANES), send_index, send_count, first_cell, own_levels * 64)
    whole, smoothed = smooth_of(adjoint.reshape(own_levels, 64, LANES), coefs, ens)
    ensemble_grad, static_grad = gradients(
        whole, smoothed, control, pert, static, vertical_local, vertical_root, member_scale
    )
    return (from_tiles(static_grad, grid_rows), from_tiles(ensemble_grad, grid_rows))


def solution(mesh):
    placed = (
        P(None, "cols", None),
        P("ens", None, "cols", None),
        P("ens", None, "cols", None),
        P(),
        P(),
        P("cols", None),
        P("cols", None),
        P("cols"),
        P("cols"),
        P("cols"),
        P("cols", None),
        P("cols"),
    )
    return jax.shard_map(
        local,
        mesh=mesh,
        in_specs=placed,
        out_specs=(P(None, "cols", None), P("ens", None, "cols", None)),
        check_vma=False,
    )
```

```python
import functools
import math

import jax
import jax.numpy as jnp
from jax import lax
from jax.experimental import pallas as pl
from jax.experimental.pallas import tpu as pltpu
from jax.sharding import PartitionSpec as P

NDIFF = 4
LANES = 128
VMEM_LIMIT = 48 * 1024 * 1024

precise = lax.Precision.HIGHEST

SMEM = pl.BlockSpec(memory_space=pltpu.SMEM)
VMEM = pl.BlockSpec(memory_space=pltpu.VMEM)


def params(**more):
    return pltpu.CompilerParams(vmem_limit_bytes=VMEM_LIMIT, **more)


def to_tiles(cells):
    lead = cells.shape[:-2]
    rows, length = cells.shape[-2:]
    split = cells.reshape(lead + (rows, length // LANES, LANES))
    return jnp.swapaxes(split, -3, -2).reshape(lead + (rows * length // LANES, LANES))


def from_tiles(tiles, rows):
    lead = tiles.shape[:-2]
    count = tiles.shape[-2] // rows
    split = tiles.reshape(lead + (count, rows, LANES))
    return jnp.swapaxes(split, -3, -2).reshape(lead + (rows, count * LANES))


def iota(shape, dim):
    return lax.broadcasted_iota(jnp.int32, shape, dim)


def small(ids):
    return ids.astype(jnp.float32).astype(jnp.bfloat16)


def one_hot(ids, count):
    width = ids.shape[1]
    hit = small(iota((count, width), 0)) == small(ids)
    return jnp.where(hit, jnp.bfloat16(1), jnp.bfloat16(0))


def table_parts(table, parts_ref):
    lanes = table.shape[1]
    high = table.astype(jnp.bfloat16).astype(jnp.float32)
    parts_ref[:lanes, :] = high.T.astype(jnp.bfloat16)
    parts_ref[lanes:, :] = (table - high).T.astype(jnp.bfloat16)


def look_up(parts_ref, hot, lane):
    lanes = parts_ref.shape[0] // 2
    found = jnp.dot(parts_ref[...], hot, preferred_element_type=jnp.float32)
    found = found[:lanes] + found[lanes:]
    found = jnp.where(iota(found.shape, 0) == lane, found, 0.0)
    return jnp.sum(found, axis=0, keepdims=True)


def sum_up(hot, lane, values, lanes):
    high = values.astype(jnp.bfloat16)
    low = (values - high.astype(jnp.float32)).astype(jnp.bfloat16)
    hit = small(iota((lanes, lane.shape[1]), 0)) == small(lane)
    zero = jnp.bfloat16(0)
    parts = jnp.concatenate([jnp.where(hit, high, zero), jnp.where(hit, low, zero)], axis=0)
    return lax.dot_general(hot, parts, (((1,), (1,)), ((), ())), preferred_element_type=jnp.float32)


def as_row(block):
    return jnp.concatenate([block[i : i + 1, :] for i in range(block.shape[0])], axis=1)


def cell_place(index, first_cell, cells):
    inside = index - first_cell
    level = inside >> 13
    row = (level << 6) + (((inside >> 7) & 31) << 1) + ((inside >> 12) & 1)
    mine = (inside >= 0) & (inside < cells)
    return jnp.where(mine, row, -1), inside & (LANES - 1)


MESH = pl.DeviceIdType.MESH


def spot(ens, cols):
    return {"ens": ens, "cols": cols}


def places():
    return (lax.axis_index("ens"), lax.axis_index("cols"), lax.axis_size("ens"), lax.axis_size("cols"))


def greet(barrier, target):
    pl.semaphore_signal(barrier, inc=1, device_id=target, device_id_type=MESH)


def send(source, landing, send_sem, recv_sem, target):
    copy = pltpu.make_async_remote_copy(
        src_ref=source,
        dst_ref=landing,
        send_sem=send_sem,
        recv_sem=recv_sem,
        device_id=target,
        device_id_type=MESH,
    )
    copy.start()
    return copy


def odd_rows():
    return (lax.broadcasted_iota(jnp.int32, (64, LANES), 0) & 1) == 1


def swapped(tile):
    return jnp.where(odd_rows(), pltpu.roll(tile, 1, 0), pltpu.roll(tile, 63, 0))


def east_of(tile):
    near = pltpu.roll(tile, LANES - 1, 1)
    lane = lax.broadcasted_iota(jnp.int32, (64, LANES), 1)
    return jnp.where(lane == LANES - 1, pltpu.roll(near, 62, 0), near)


def west_of(tile):
    near = pltpu.roll(tile, 1, 1)
    lane = lax.broadcasted_iota(jnp.int32, (64, LANES), 1)
    return jnp.where(lane == 0, pltpu.roll(near, 2, 0), near)


COEFS = 10


def make_coefs(coef_ref, north, east, north_up, east_up, north_down, east_down, has_up, has_down):
    odd = odd_rows()
    keep_up = has_up.astype(jnp.float32)
    keep_down = has_down.astype(jnp.float32)
    north_down = north_down * keep_down
    pair = jnp.where(odd, north, swapped(north))
    outer = jnp.where(odd, swapped(north_down), north)
    east_rim = jnp.where(odd, east_up, east_down)
    west = west_of(east)
    west_rim = west_of(east_rim)
    inner = swapped(outer)
    far = jnp.where(odd, north_up, swapped(north_down))
    coef_ref[0] = 1.0 - pair - outer - east - west
    coef_ref[1] = pair
    coef_ref[2] = outer * jnp.where(odd, keep_down, keep_up)
    coef_ref[3] = east
    coef_ref[4] = west
    coef_ref[5] = 1.0 - inner - far - east_rim - west_rim
    coef_ref[6] = inner
    coef_ref[7] = far
    coef_ref[8] = east_rim
    coef_ref[9] = west_rim


def two_steps(coef_ref, own, up, down):
    odd = odd_rows()
    rim = jnp.where(odd, up, down)
    far = jnp.where(odd, down, up)
    own_swap = swapped(own)
    first = (
        coef_ref[0] * own
        + coef_ref[1] * own_swap
        + coef_ref[2] * swapped(rim)
        + coef_ref[3] * east_of(own)
        + coef_ref[4] * west_of(own)
    )
    rim = (
        coef_ref[5] * rim
        + coef_ref[6] * own_swap
        + coef_ref[7] * swapped(far)
        + coef_ref[8] * east_of(rim)
        + coef_ref[9] * west_of(rim)
    )
    return (
        coef_ref[0] * first
        + coef_ref[1] * swapped(first)
        + coef_ref[2] * swapped(rim)
        + coef_ref[3] * east_of(first)
        + coef_ref[4] * west_of(first)
    )


def neighbours():
    e, c, ens, cols = places()
    return spot(e, (c + cols - 1) % cols), spot(e, (c + 1) % cols)


def tile_copies(source, landing, send_sems, recv_sems):
    upper, lower = neighbours()
    return [
        pltpu.make_async_remote_copy(
            src_ref=source,
            dst_ref=landing.at[side],
            send_sem=send_sems.at[side],
            recv_sem=recv_sems.at[side],
            device_id=target,
            device_id_type=MESH,
        )
        for side, target in ((0, lower), (1, upper))
    ]


def start_tiles(copies):
    e, c, ens, cols = places()

    @pl.when(c < cols - 1)
    def _():
        copies[0].start()

    @pl.when(c > 0)
    def _():
        copies[1].start()


def wait_tiles(copies):
    e, c, ens, cols = places()

    @pl.when(c < cols - 1)
    def _():
        copies[0].wait_send()
        copies[1].wait_recv()

    @pl.when(c > 0)
    def _():
        copies[1].wait_send()
        copies[0].wait_recv()


def clear_rims(refs):
    e, c, ens, cols = places()
    for ref in refs:

        @pl.when(c == 0)
        def _(ref=ref):
            ref[0] = jnp.zeros(ref.shape[1:], jnp.float32)

        @pl.when(c == cols - 1)
        def _(ref=ref):
            ref[1] = jnp.zeros(ref.shape[1:], jnp.float32)


def greet_neighbours(barrier):
    e, c, ens, cols = places()
    upper, lower = neighbours()

    @pl.when(c > 0)
    def _():
        greet(barrier, upper)

    @pl.when(c < cols - 1)
    def _():
        greet(barrier, lower)

    for d in range(1, ens):
        greet(barrier, spot((e + d) % ens, c))


def wait_barrier(barrier):
    e, c, ens, cols = places()
    has_upper = (c + cols - 1) // cols
    has_lower = 1 - (c + 1) // cols
    all_leave = ((e - c // (cols // ens) + ens) % ens + ens - 1) // ens
    pl.semaphore_wait(barrier, ens - 1 + cols - 1 + has_upper + has_lower + all_leave)


def wait_sends(lists_ref, send_sem):
    e, c, ens, cols = places()
    few = lists_ref.at[pl.ds(0, cols - 1)]

    @pl.when(e == c // (cols // ens))
    def _():
        pltpu.make_async_copy(few, few, send_sem).wait()

    @pl.when(e != c // (cols // ens))
    def _():
        pltpu.make_async_copy(lists_ref, lists_ref, send_sem).wait()


def observers_kernel(
    scale,
    local_ref,
    root_ref,
    counts_ref,
    static_ref,
    north_ref,
    east_ref,
    index_ref,
    control_hbm,
    pert_hbm,
    out_ref,
    coef_ref,
    control_ref,
    pert_ref,
    part_ref,
    faces,
    fields,
    halos,
    terms,
    table_ref,
    parts_ref,
    picked,
    landing,
    load_sems,
    face_send,
    face_recv,
    halo_send,
    halo_recv,
    term_send,
    term_recv,
    list_send,
    list_recv,
):
    e, c, ens, cols = places()
    levels = static_ref.shape[0]
    members = control_ref.shape[0]
    own = levels // ens
    group = cols // ens
    z = c // group
    loads = [
        pltpu.make_async_copy(control_hbm, control_ref, load_sems.at[0]),
        pltpu.make_async_copy(pert_hbm, pert_ref, load_sems.at[1]),
    ]
    for load in loads:
        load.start()
    barrier = pltpu.get_barrier_semaphore()
    greet_neighbours(barrier)

    def hello(n, carry):
        e2 = n // group
        p = group * e + n % group

        @pl.when((e2 != e) | (p != c))
        def _():
            greet(barrier, spot(e2, p))

        return carry

    lax.fori_loop(0, cols, hello, 0)
    clear_rims([faces, halos.at[0], halos.at[1]])

    def product(i, carry):
        rows = pl.ds(pl.multiple_of(i * 32, 32), 32)
        totals = [jnp.zeros((32, LANES), jnp.float32)] * own
        for m in range(levels):
            source = static_ref[m, rows, :]
            totals = [totals[l] + root_ref[e * own + l, m] * source for l in range(own)]
        for l in range(own):
            fields[0, l, rows, :] = totals[l]
        return carry

    lax.fori_loop(0, 2, product, 0)
    wait_barrier(barrier)
    first_halo = tile_copies(fields.at[0], halos.at[0], halo_send.at[0], halo_recv.at[0])
    start_tiles(first_halo)
    norths = tile_copies(north_ref, faces.at[:, 0], face_send.at[0], face_recv.at[0])
    easts = tile_copies(east_ref, faces.at[:, 1], face_send.at[1], face_recv.at[1])
    start_tiles(norths)
    start_tiles(easts)
    for load in loads:
        load.wait()

    def part_of(peer):
        first = peer * own

        def chunk(i, carry):
            rows = pl.ds(pl.multiple_of(i * 32, 32), 32)

            def member(k, totals):
                sums = [jnp.zeros((32, LANES), jnp.float32)] * own
                for m in range(levels):
                    source = control_ref[k, m, rows, :]
                    sums = [sums[l] + local_ref[first + l, m] * source for l in range(own)]
                return tuple(
                    totals[l] + pert_ref[k, first + l, rows, :].astype(jnp.float32) * sums[l]
                    for l in range(own)
                )

            totals = lax.fori_loop(0, members, member, (jnp.zeros((32, LANES), jnp.float32),) * own)
            for l in range(own):
                part_ref[first + l, rows, :] = totals[l] * scale
            return carry

        lax.fori_loop(0, 2, chunk, 0)

    def send_part(d):
        peer = (e + d) % ens
        return send(
            part_ref.at[pl.ds(peer * own, own)],
            terms.at[d - 1],
            term_send.at[d - 1],
            term_recv.at[d - 1],
            spot(peer, c),
        )

    part_of((e + 2) % ens)
    sums = [send_part(2)]
    wait_tiles(norths)
    wait_tiles(easts)
    make_coefs(
        coef_ref,
        north_ref[...],
        east_ref[...],
        faces[0, 0],
        faces[0, 1],
        faces[1, 0],
        faces[1, 1],
        c > 0,
        c < cols - 1,
    )
    wait_tiles(first_halo)
    for l in range(own):
        fields[1, l] = two_steps(coef_ref, fields[0, l], halos[0, 0, l], halos[0, 1, l])
    second_halo = tile_copies(fields.at[1], halos.at[1], halo_send.at[1], halo_recv.at[1])
    start_tiles(second_halo)
    part_of((e + 1) % ens)
    sums.append(send_part(1))
    part_of((e + 3) % ens)
    sums.append(send_part(3))
    part_of(e)
    wait_tiles(second_halo)
    rows = table_ref.shape[0] // own
    for l in range(own):
        total = two_steps(coef_ref, fields[1, l], halos[1, 0, l], halos[1, 1, l])
        table_ref[l * rows : (l + 1) * rows, :] = total + part_ref[e * own + l]
    for copy in sums:
        copy.wait()
    for l in range(own):
        total = table_ref[l * rows : (l + 1) * rows, :]
        for d in range(ens - 1):
            total = total + terms[d, l]
        table_ref[l * rows : (l + 1) * rows, :] = total

    table_parts(table_ref[...], parts_ref)
    capacity = index_ref.shape[1]
    slots = iota((1, capacity), 1)
    cells = table_ref.shape[0] * LANES

    def pick(i, carry):
        for j in range(8):
            q = (c + i * 8 + j) % cols
            row, lane = cell_place(index_ref[pl.ds(q, 1), :], e * cells, cells)
            row = jnp.where(slots < counts_ref[q], row, -1)
            found = look_up(parts_ref, one_hot(row, table_ref.shape[0]), lane)
            for t in range(capacity // LANES):
                picked[q, pl.ds(t, 1), :] = found[:, t * LANES : (t + 1) * LANES]
        for j in range(8):
            q = (c + i * 8 + j) % cols
            place = landing.at[e, c % group]

            @pl.when((q != c) | (e != z))
            def _(q=q, place=place):
                send(picked.at[q], place, list_send, list_recv, spot(z, q))

            @pl.when((q == c) & (e == z))
            def _(q=q, place=place):
                pltpu.make_async_copy(picked.at[q], place, list_recv).start()

        return carry

    lax.fori_loop(0, cols // 8, pick, 0)
    pltpu.make_async_copy(landing, landing, list_recv).wait()
    total = landing[0]
    for n in range(1, ens):
        total = total + landing[n]
    out_ref[...] = total
    wait_sends(picked, list_send)


def observer_lists(local_root, root, counts, static, north, east, index, control, pert, ens, scale):
    levels, rows, lanes = static.shape
    own = levels // ens
    lists, capacity = index.shape
    list_rows = capacity // LANES
    dma = pltpu.SemaphoreType.DMA
    anywhere = pl.BlockSpec(memory_space=pl.ANY)
    return pl.pallas_call(
        functools.partial(observers_kernel, scale),
        in_specs=[SMEM, SMEM, SMEM, VMEM, VMEM, VMEM, VMEM, anywhere, anywhere],
        out_specs=[VMEM, VMEM],
        out_shape=[
            jax.ShapeDtypeStruct((lists // ens, list_rows, LANES), jnp.float32),
            jax.ShapeDtypeStruct((COEFS, rows, lanes), jnp.float32),
        ],
        scratch_shapes=[
            pltpu.VMEM(control.shape, jnp.float32),
            pltpu.VMEM(pert.shape, jnp.bfloat16),
            pltpu.VMEM(static.shape, jnp.float32),
            pltpu.VMEM((2, 2, rows, lanes), jnp.float32),
            pltpu.VMEM((2, own, rows, lanes), jnp.float32),
            pltpu.VMEM((2, 2, own, rows, lanes), jnp.float32),
            pltpu.VMEM((ens - 1, own, rows, lanes), jnp.float32),
            pltpu.VMEM((own * rows, lanes), jnp.float32),
            pltpu.VMEM((2 * LANES, own * rows), jnp.bfloat16),
            pltpu.VMEM((lists, list_rows, LANES), jnp.float32),
            pltpu.VMEM((ens, lists // ens, list_rows, LANES), jnp.float32),
            dma((2,)),
            dma((2, 2)),
            dma((2, 2)),
            dma((2, 2)),
            dma((2, 2)),
            dma((ens - 1,)),
            dma((ens - 1,)),
            dma,
            dma,
        ],
        compiler_params=params(collective_id=1, has_side_effects=True),
        name="observer_lists",
    )(local_root, root, counts, static, north, east, index, control, pert)


HALF = 64


def share(own_ref, whole_ref, send_sems, recv_sems):
    e, c, ens, cols = places()
    own = own_ref.shape[0]
    return [
        send(
            own_ref,
            whole_ref.at[pl.ds(e * own, own)],
            send_sems.at[d - 1],
            recv_sems.at[d - 1],
            spot((e + d) % ens, c),
        )
        for d in (2, 1, 3)
    ]


def gradient_kernel(
    scale,
    local_ref,
    root_ref,
    counts_ref,
    lists_ref,
    coef_ref,
    slot_ref,
    innovation_ref,
    weight_ref,
    index_ref,
    static_ref,
    pert_ref,
    out_ref,
    static_out_ref,
    parts_ref,
    seen_ref,
    returned,
    arrived,
    both_ref,
    adjoint,
    whole,
    smooth,
    fields,
    halos,
    list_send,
    list_recv,
    halo_send,
    halo_recv,
    whole_send,
    whole_recv,
    smooth_send,
    smooth_recv,
):
    e, c, ens, cols = places()
    group = cols // ens
    z = c // group
    levels = static_ref.shape[0]
    own = levels // ens
    members = pert_ref.shape[0]
    barrier = pltpu.get_barrier_semaphore()
    greet_neighbours(barrier)

    def hello(d, carry):
        greet(barrier, spot(z, (c + d) % cols))
        return carry

    lax.fori_loop(1, cols, hello, 0)

    @pl.when(z != e)
    def _():
        greet(barrier, spot(z, c))

    clear_rims([halos.at[0], halos.at[1]])

    tiles = lists_ref.shape[1]
    half_rows = lists_ref.shape[0] * tiles
    table = lists_ref[...].reshape(half_rows, LANES)
    table_parts(jnp.concatenate([table[:, :HALF], table[:, HALF:]], axis=0), parts_ref)
    seen_ref[...] = jnp.zeros_like(seen_ref)
    block = 32

    def observe(i, carry):
        total = jnp.zeros(seen_ref.shape, jnp.float32)
        for j in range(2):
            at = pl.ds(pl.multiple_of((i * 2 + j) * block, block), block)
            inside = as_row(slot_ref[at, :]) - e * (half_rows * LANES)
            row = inside >> 7
            mine = (inside >= 0) & (row < half_rows)
            row = jnp.where(mine, row + ((inside >> 6) & 1) * half_rows, -1)
            lane = inside & (HALF - 1)
            hot = one_hot(row, 2 * half_rows)
            found = look_up(parts_ref, hot, lane)
            weighted = as_row(weight_ref[at, :]) * (found - as_row(innovation_ref[at, :]))
            total = total + sum_up(hot, lane, jnp.where(mine, weighted, 0.0), HALF)
        seen_ref[...] += total
        return carry

    lax.fori_loop(0, slot_ref.shape[0] // (2 * block), observe, 0)
    seen = seen_ref[:, :HALF] + seen_ref[:, HALF:]
    returned[...] = jnp.concatenate([seen[:half_rows], seen[half_rows:]], axis=1).reshape(returned.shape)
    wait_barrier(barrier)

    def give_back(n, carry):
        e2 = (e + n // group) % ens
        i = (c + n) % group
        p = group * e + i

        @pl.when((e2 != e) | (p != c))
        def _():
            send(returned.at[i], arrived.at[c], list_send, list_recv.at[z], spot(e2, p))

        @pl.when((e2 == e) & (p == c))
        def _():
            pltpu.make_async_copy(returned.at[i], arrived.at[c], list_recv.at[z]).start()

        return carry

    lax.fori_loop(0, cols, give_back, 0)

    capacity = index_ref.shape[1]
    slots = iota((1, capacity), 1)
    cell_rows = both_ref.shape[0]
    both_ref[...] = jnp.zeros_like(both_ref)

    def spread(i, carry):
        some = arrived.at[pl.ds(i * group, group)]
        pltpu.make_async_copy(some, some, list_recv.at[i]).wait()
        total = jnp.zeros(both_ref.shape, jnp.float32)
        for j in range(group):
            q = i * group + j
            values = as_row(arrived[q])
            row, lane = cell_place(index_ref[pl.ds(q, 1), :], e * (cell_rows * LANES), cell_rows * LANES)
            row = jnp.where(slots < counts_ref[q], row, -1)
            total = total + sum_up(one_hot(row, cell_rows), lane, values, LANES)
        both_ref[...] += total
        return carry

    lax.fori_loop(0, ens, spread, 0)
    adjoint[...] = (both_ref[:, :LANES] + both_ref[:, LANES:]).reshape(adjoint.shape)

    first_halo = tile_copies(adjoint, halos.at[0], halo_send.at[0], halo_recv.at[0])
    start_tiles(first_halo)
    wholes = share(adjoint, whole, whole_send, whole_recv)
    for l in range(own):
        whole[e * own + l] = adjoint[l]
    wait_sends(arrived, list_send)
    wait_tiles(first_halo)
    for l in range(own):
        fields[0, l] = two_steps(coef_ref, adjoint[l], halos[0, 0, l], halos[0, 1, l])
    second_halo = tile_copies(fields.at[0], halos.at[1], halo_send.at[1], halo_recv.at[1])
    start_tiles(second_halo)
    for copy in wholes:
        copy.wait()

    def products(k, carry):
        def chunk(i, inner):
            rows = pl.ds(pl.multiple_of((i // 2) * 32, 32), 32)
            first = (i % 2) * 8
            totals = [jnp.zeros((32, LANES), jnp.float32)] * 8
            for m in range(levels):
                source = pert_ref[k, m, rows, :].astype(jnp.float32) * whole[m, rows, :]
                totals = [totals[n] + local_ref[m, first + n] * source for n in range(8)]
            for n in range(8):
                out_ref[k, first + n, rows, :] = totals[n] * scale
            return inner

        lax.fori_loop(0, 4, chunk, 0)
        return carry

    lax.fori_loop(0, 2, products, 0)
    wait_tiles(second_halo)
    for l in range(own):
        fields[1, l] = two_steps(coef_ref, fields[0, l], halos[1, 0, l], halos[1, 1, l])
    smooths = share(fields.at[1], smooth, smooth_send, smooth_recv)
    for l in range(own):
        smooth[e * own + l] = fields[1, l]
    lax.fori_loop(2, members, products, 0)
    for copy in smooths:
        copy.wait()

    def static_product(i, carry):
        rows = pl.ds(pl.multiple_of((i // 2) * 32, 32), 32)
        first = (i % 2) * 8
        totals = [static_ref[first + n, rows, :] for n in range(8)]
        for m in range(levels):
            source = smooth[m, rows, :]
            totals = [totals[n] + root_ref[m, first + n] * source for n in range(8)]
        for n in range(8):
            static_out_ref[first + n, rows, :] = totals[n]
        return carry

    lax.fori_loop(0, 4, static_product, 0)


def gradient_terms(
    local_root, root, counts, lists, coefs, slots, innovation, weight, index, static, pert, ens, scale
):
    levels, rows, lanes = static.shape
    own = levels // ens
    all_lists = index.shape[0]
    tiles = lists.shape[1]
    half_rows = lists.shape[0] * tiles
    dma = pltpu.SemaphoreType.DMA
    shaped = [a.reshape(-1, LANES) for a in (slots, innovation, weight)]
    return pl.pallas_call(
        functools.partial(gradient_kernel, scale),
        in_specs=[SMEM, SMEM, SMEM] + [VMEM] * 8,
        out_specs=[VMEM, VMEM],
        out_shape=[
            jax.ShapeDtypeStruct(pert.shape, jnp.float32),
            jax.ShapeDtypeStruct(static.shape, jnp.float32),
        ],
        scratch_shapes=[
            pltpu.VMEM((2 * HALF, 2 * half_rows), jnp.bfloat16),
            pltpu.VMEM((2 * half_rows, 2 * HALF), jnp.float32),
            pltpu.VMEM(lists.shape, jnp.float32),
            pltpu.VMEM((all_lists, tiles, LANES), jnp.float32),
            pltpu.VMEM((own * rows, 2 * LANES), jnp.float32),
            pltpu.VMEM((own, rows, lanes), jnp.float32),
            pltpu.VMEM(static.shape, jnp.float32),
            pltpu.VMEM(static.shape, jnp.float32),
            pltpu.VMEM((2, own, rows, lanes), jnp.float32),
            pltpu.VMEM((2, 2, own, rows, lanes), jnp.float32),
            dma,
            dma((ens,)),
            dma((2, 2)),
            dma((2, 2)),
            dma((ens - 1,)),
            dma((ens - 1,)),
            dma((ens - 1,)),
            dma((ens - 1,)),
        ],
        compiler_params=params(collective_id=2, has_side_effects=True),
        name="gradient_terms",
    )(local_root, root, counts, lists, coefs, *shaped, index, static, pert)


def local(
    static_control,
    ensemble_control,
    perturbations,
    vertical_root,
    vertical_local,
    face_north,
    face_east,
    innovation,
    obs_weight,
    obs_slot,
    send_index,
    send_count,
):
    grid_rows = static_control.shape[1]
    ens = lax.axis_size("ens")
    member_scale = 1.0 / math.sqrt(ensemble_control.shape[0] * ens - 1)
    static = to_tiles(static_control)
    control = to_tiles(ensemble_control)
    pert = to_tiles(perturbations)
    lists, coefs = observer_lists(
        vertical_local,
        vertical_root,
        send_count,
        static,
        to_tiles(face_north),
        to_tiles(face_east),
        send_index,
        control,
        pert,
        ens,
        member_scale,
    )
    terms, static_grad = gradient_terms(
        vertical_local,
        vertical_root,
        send_count,
        lists,
        coefs,
        obs_slot,
        innovation,
        obs_weight,
        send_index,
        static,
        pert,
        ens,
        member_scale,
    )
    return (from_tiles(static_grad, grid_rows), from_tiles(control + terms, grid_rows))


def solution(mesh):
    placed = (
        P(None, "cols", None),
        P("ens", None, "cols", None),
        P("ens", None, "cols", None),
        P(),
        P(),
        P("cols", None),
        P("cols", None),
        P("cols"),
        P("cols"),
        P("cols"),
        P("cols", None),
        P("cols"),
    )
    return jax.shard_map(
        local,
        mesh=mesh,
        in_specs=placed,
        out_specs=(P(None, "cols", None), P("ens", None, "cols", None)),
        check_vma=False,
    )
```

```python
import functools
import math
import types

import jax
import jax.numpy as jnp
from jax import lax
from jax.experimental import pallas as pl
from jax.experimental.pallas import tpu as pltpu
from jax.sharding import PartitionSpec as P

NDIFF = 4
LANES = 128
VMEM_LIMIT = 52 * 1024 * 1024

precise = lax.Precision.HIGHEST

SMEM = pl.BlockSpec(memory_space=pltpu.SMEM)
VMEM = pl.BlockSpec(memory_space=pltpu.VMEM)


def params(**more):
    return pltpu.CompilerParams(vmem_limit_bytes=VMEM_LIMIT, **more)


def to_tiles(cells):
    lead = cells.shape[:-2]
    rows, length = cells.shape[-2:]
    split = cells.reshape(lead + (rows, length // LANES, LANES))
    return jnp.swapaxes(split, -3, -2).reshape(lead + (rows * length // LANES, LANES))


def from_tiles(tiles, rows):
    lead = tiles.shape[:-2]
    count = tiles.shape[-2] // rows
    split = tiles.reshape(lead + (count, rows, LANES))
    return jnp.swapaxes(split, -3, -2).reshape(lead + (rows, count * LANES))


def iota(shape, dim):
    return lax.broadcasted_iota(jnp.int32, shape, dim)


def small(ids):
    return ids.astype(jnp.float32).astype(jnp.bfloat16)


def one_hot(ids, count):
    width = ids.shape[1]
    hit = small(iota((count, width), 0)) == small(ids)
    return jnp.where(hit, jnp.bfloat16(1), jnp.bfloat16(0))


def table_parts(table, parts_ref):
    lanes = table.shape[1]
    high = table.astype(jnp.bfloat16).astype(jnp.float32)
    parts_ref[:lanes, :] = high.T.astype(jnp.bfloat16)
    parts_ref[lanes:, :] = (table - high).T.astype(jnp.bfloat16)


def look_up(parts_ref, hot, lane):
    lanes = parts_ref.shape[0] // 2
    found = jnp.dot(parts_ref[...], hot, preferred_element_type=jnp.float32)
    found = found[:lanes] + found[lanes:]
    found = jnp.where(iota(found.shape, 0) == lane, found, 0.0)
    return jnp.sum(found, axis=0, keepdims=True)


def sum_up(hot, lane, values, lanes):
    high = values.astype(jnp.bfloat16)
    low = (values - high.astype(jnp.float32)).astype(jnp.bfloat16)
    hit = small(iota((lanes, lane.shape[1]), 0)) == small(lane)
    zero = jnp.bfloat16(0)
    parts = jnp.concatenate([jnp.where(hit, high, zero), jnp.where(hit, low, zero)], axis=0)
    return lax.dot_general(hot, parts, (((1,), (1,)), ((), ())), preferred_element_type=jnp.float32)


def as_row(block):
    return jnp.concatenate([block[i : i + 1, :] for i in range(block.shape[0])], axis=1)


def cell_place(index, first_cell, cells):
    inside = index - first_cell
    level = inside >> 13
    row = (level << 6) + (((inside >> 7) & 31) << 1) + ((inside >> 12) & 1)
    mine = (inside >= 0) & (inside < cells)
    return jnp.where(mine, row, -1), inside & (LANES - 1)


MESH = pl.DeviceIdType.MESH


def spot(ens, cols):
    return {"ens": ens, "cols": cols}


def places():
    return (lax.axis_index("ens"), lax.axis_index("cols"), lax.axis_size("ens"), lax.axis_size("cols"))


def greet(barrier, target):
    pl.semaphore_signal(barrier, inc=1, device_id=target, device_id_type=MESH)


def send(source, landing, send_sem, recv_sem, target):
    copy = pltpu.make_async_remote_copy(
        src_ref=source,
        dst_ref=landing,
        send_sem=send_sem,
        recv_sem=recv_sem,
        device_id=target,
        device_id_type=MESH,
    )
    copy.start()
    return copy


def odd_rows():
    return (lax.broadcasted_iota(jnp.int32, (64, LANES), 0) & 1) == 1


def swapped(tile):
    return jnp.where(odd_rows(), pltpu.roll(tile, 1, 0), pltpu.roll(tile, 63, 0))


def east_of(tile):
    near = pltpu.roll(tile, LANES - 1, 1)
    lane = lax.broadcasted_iota(jnp.int32, (64, LANES), 1)
    return jnp.where(lane == LANES - 1, pltpu.roll(near, 62, 0), near)


def west_of(tile):
    near = pltpu.roll(tile, 1, 1)
    lane = lax.broadcasted_iota(jnp.int32, (64, LANES), 1)
    return jnp.where(lane == 0, pltpu.roll(near, 2, 0), near)


COEFS = 10


def make_coefs(coef_ref, north, east, north_up, east_up, north_down, east_down, has_up, has_down):
    odd = odd_rows()
    keep_up = has_up.astype(jnp.float32)
    keep_down = has_down.astype(jnp.float32)
    north_down = north_down * keep_down
    pair = jnp.where(odd, north, swapped(north))
    outer = jnp.where(odd, swapped(north_down), north)
    east_rim = jnp.where(odd, east_up, east_down)
    west = west_of(east)
    west_rim = west_of(east_rim)
    inner = swapped(outer)
    far = jnp.where(odd, north_up, swapped(north_down))
    coef_ref[0] = 1.0 - pair - outer - east - west
    coef_ref[1] = pair
    coef_ref[2] = outer * jnp.where(odd, keep_down, keep_up)
    coef_ref[3] = east
    coef_ref[4] = west
    coef_ref[5] = 1.0 - inner - far - east_rim - west_rim
    coef_ref[6] = inner
    coef_ref[7] = far
    coef_ref[8] = east_rim
    coef_ref[9] = west_rim


def two_steps(coef_ref, own, up, down):
    odd = odd_rows()
    rim = jnp.where(odd, up, down)
    far = jnp.where(odd, down, up)
    own_swap = swapped(own)
    first = (
        coef_ref[0] * own
        + coef_ref[1] * own_swap
        + coef_ref[2] * swapped(rim)
        + coef_ref[3] * east_of(own)
        + coef_ref[4] * west_of(own)
    )
    rim = (
        coef_ref[5] * rim
        + coef_ref[6] * own_swap
        + coef_ref[7] * swapped(far)
        + coef_ref[8] * east_of(rim)
        + coef_ref[9] * west_of(rim)
    )
    return (
        coef_ref[0] * first
        + coef_ref[1] * swapped(first)
        + coef_ref[2] * swapped(rim)
        + coef_ref[3] * east_of(first)
        + coef_ref[4] * west_of(first)
    )


def neighbours():
    e, c, ens, cols = places()
    return spot(e, (c + cols - 1) % cols), spot(e, (c + 1) % cols)


def tile_copies(source, landing, send_sems, recv_sems):
    upper, lower = neighbours()
    return [
        pltpu.make_async_remote_copy(
            src_ref=source,
            dst_ref=landing.at[side],
            send_sem=send_sems.at[side],
            recv_sem=recv_sems.at[side],
            device_id=target,
            device_id_type=MESH,
        )
        for side, target in ((0, lower), (1, upper))
    ]


def start_tiles(copies):
    e, c, ens, cols = places()

    @pl.when(c < cols - 1)
    def _():
        copies[0].start()

    @pl.when(c > 0)
    def _():
        copies[1].start()


def wait_tiles(copies):
    e, c, ens, cols = places()

    @pl.when(c < cols - 1)
    def _():
        copies[0].wait_send()
        copies[1].wait_recv()

    @pl.when(c > 0)
    def _():
        copies[1].wait_send()
        copies[0].wait_recv()


def clear_rims(refs):
    e, c, ens, cols = places()
    for ref in refs:

        @pl.when(c == 0)
        def _(ref=ref):
            ref[0] = jnp.zeros(ref.shape[1:], jnp.float32)

        @pl.when(c == cols - 1)
        def _(ref=ref):
            ref[1] = jnp.zeros(ref.shape[1:], jnp.float32)


def greet_neighbours(barrier):
    e, c, ens, cols = places()
    upper, lower = neighbours()

    @pl.when(c > 0)
    def _():
        greet(barrier, upper)

    @pl.when(c < cols - 1)
    def _():
        greet(barrier, lower)

    for d in range(1, ens):
        greet(barrier, spot((e + d) % ens, c))


def wait_barrier(barrier):
    e, c, ens, cols = places()
    has_upper = (c + cols - 1) // cols
    has_lower = 1 - (c + 1) // cols
    all_leave = ((e - c // (cols // ens) + ens) % ens + ens - 1) // ens
    pl.semaphore_wait(barrier, ens - 1 + has_upper + has_lower + 2 * (cols - 1 + all_leave))


def wait_sends(lists_ref, send_sem):
    e, c, ens, cols = places()
    few = lists_ref.at[pl.ds(0, cols - 1)]

    @pl.when(e == c // (cols // ens))
    def _():
        pltpu.make_async_copy(few, few, send_sem).wait()

    @pl.when(e != c // (cols // ens))
    def _():
        pltpu.make_async_copy(lists_ref, lists_ref, send_sem).wait()


HALF = 64
BLOCK = 32
ANY = pl.BlockSpec(memory_space=pl.ANY)


def greet_all(barrier):
    e, c, ens, cols = places()
    group = cols // ens
    z = c // group
    greet_neighbours(barrier)

    def senders(n, carry):
        e2 = n // group
        p = group * e + n % group

        @pl.when((e2 != e) | (p != c))
        def _():
            greet(barrier, spot(e2, p))

        return carry

    lax.fori_loop(0, cols, senders, 0)

    def returners(d, carry):
        greet(barrier, spot(z, (c + d) % cols))
        return carry

    lax.fori_loop(1, cols, returners, 0)

    @pl.when(z != e)
    def _():
        greet(barrier, spot(z, c))


def share(own_ref, whole_ref, send_sems, recv_sems):
    e, c, ens, cols = places()
    own = own_ref.shape[0]
    return [
        send(
            own_ref,
            whole_ref.at[pl.ds(e * own, own)],
            send_sems.at[d - 1],
            recv_sems.at[d - 1],
            spot((e + d) % ens, c),
        )
        for d in (2, 1, 3)
    ]


def level_part(r, peer, own, scale, loads):
    members, levels = r.control.shape[:2]
    first = peer * own

    def chunk(i, carry):
        rows = pl.ds(pl.multiple_of(i * 32, 32), 32)

        def member(k, totals):
            if loads is not None:

                @pl.when(i == 0)
                def _():
                    for load in loads(k):
                        load.wait()

            sums = [jnp.zeros((32, LANES), jnp.float32)] * own
            for m in range(levels):
                source = r.control[k, m, rows, :]
                sums = [sums[l] + r.local[first + l, m] * source for l in range(own)]
            return tuple(
                totals[l] + r.pert[k, first + l, rows, :].astype(jnp.float32) * sums[l] for l in range(own)
            )

        totals = lax.fori_loop(0, members, member, (jnp.zeros((32, LANES), jnp.float32),) * own)
        for l in range(own):
            r.part[first + l, rows, :] = totals[l] * scale
        return carry

    lax.fori_loop(0, 2, chunk, 0)


def picks(r):
    e, c, ens, cols = places()
    group = cols // ens
    z = c // group
    cell_rows = r.table.shape[0]
    cells = cell_rows * LANES
    capacity = r.index.shape[1]
    slots = iota((1, capacity), 1)
    place = r.landing.at[e, c % group]
    table_parts(r.table[...], r.cell_parts)

    def some(i, carry):
        for j in range(8):
            q = (c + 1 + i * 8 + j) % cols
            row, lane = cell_place(r.index[pl.ds(q, 1), :], e * cells, cells)
            row = jnp.where(slots < r.counts[q], row, -1)
            found = look_up(r.cell_parts, one_hot(row, cell_rows), lane)
            for t in range(capacity // LANES):
                r.picked[q, pl.ds(t, 1), :] = found[:, t * LANES : (t + 1) * LANES]
        for j in range(7):
            q = (c + 1 + i * 8 + j) % cols
            send(r.picked.at[q], place, r.list_send, r.list_recv, spot(z, q))
        q = (c + 8 + i * 8) % cols

        @pl.when((q != c) | (e != z))
        def _():
            send(r.picked.at[q], place, r.list_send, r.list_recv, spot(z, q))

        @pl.when((q == c) & (e == z))
        def _():
            pltpu.make_async_copy(r.picked.at[q], place, r.list_recv).start()

        return carry

    lax.fori_loop(0, cols // 8, some, 0)


def observe(r):
    e, c, ens, cols = places()
    total = r.landing[0]
    for n in range(1, ens):
        total = total + r.landing[n]
    half_rows = total.shape[0] * total.shape[1]
    table = total.reshape(half_rows, LANES)
    table_parts(jnp.concatenate([table[:, :HALF], table[:, HALF:]], axis=0), r.list_parts)
    r.seen[...] = jnp.zeros_like(r.seen)

    def some(i, carry):
        total = jnp.zeros(r.seen.shape, jnp.float32)
        for j in range(2):
            at = pl.ds(pl.multiple_of((i * 2 + j) * BLOCK, BLOCK), BLOCK)
            inside = as_row(r.slot[at, :]) - e * (half_rows * LANES)
            row = inside >> 7
            mine = (inside >= 0) & (row < half_rows)
            row = jnp.where(mine, row + ((inside >> 6) & 1) * half_rows, -1)
            lane = inside & (HALF - 1)
            hot = one_hot(row, 2 * half_rows)
            found = look_up(r.list_parts, hot, lane)
            weighted = as_row(r.weight[at, :]) * (found - as_row(r.innovation[at, :]))
            total = total + sum_up(hot, lane, jnp.where(mine, weighted, 0.0), HALF)
        r.seen[...] += total
        return carry

    lax.fori_loop(0, r.slot.shape[0] // (2 * BLOCK), some, 0)
    seen = r.seen[:, :HALF] + r.seen[:, HALF:]
    r.returned[...] = jnp.concatenate([seen[:half_rows], seen[half_rows:]], axis=1).reshape(r.returned.shape)


def give_back(r):
    e, c, ens, cols = places()
    group = cols // ens
    z = c // group
    last = cols - 1

    def step(n, carry):
        p = group * e + (c + 1 + n) % group
        e2 = (e + 1 + n // group) % ens
        send(r.returned.at[p % group], r.arrived.at[c], r.back_send, r.back_recv.at[z], spot(e2, p))
        return carry

    lax.fori_loop(0, last, step, 0)
    own = c % group
    p = group * e + own

    @pl.when(p != c)
    def _():
        send(r.returned.at[own], r.arrived.at[c], r.back_send, r.back_recv.at[z], spot(e, p))

    @pl.when(p == c)
    def _():
        pltpu.make_async_copy(r.returned.at[own], r.arrived.at[c], r.back_recv.at[z]).start()


def spread(r):
    e, c, ens, cols = places()
    group = cols // ens
    capacity = r.index.shape[1]
    slots = iota((1, capacity), 1)
    cell_rows = r.both.shape[0]
    cells = cell_rows * LANES
    r.both[...] = jnp.zeros_like(r.both)

    def some(i, carry):
        lists = r.arrived.at[pl.ds(i * group, group)]
        pltpu.make_async_copy(lists, lists, r.back_recv.at[i]).wait()
        total = jnp.zeros(r.both.shape, jnp.float32)
        for j in range(group):
            q = i * group + j
            row, lane = cell_place(r.index[pl.ds(q, 1), :], e * cells, cells)
            row = jnp.where(slots < r.counts[q], row, -1)
            total = total + sum_up(one_hot(row, cell_rows), lane, as_row(r.arrived[q]), LANES)
        r.both[...] += total
        return carry

    lax.fori_loop(0, ens, some, 0)
    r.adjoint[...] = (r.both[:, :LANES] + r.both[:, LANES:]).reshape(r.adjoint.shape)


def member_products(r, scale, first_member, last_member):
    levels = r.static.shape[0]

    def member(k, carry):
        def chunk(i, inner):
            rows = pl.ds(pl.multiple_of((i // 2) * 32, 32), 32)
            first = (i % 2) * 8
            totals = [jnp.zeros((32, LANES), jnp.float32)] * 8
            for m in range(levels):
                source = r.pert[k, m, rows, :].astype(jnp.float32) * r.whole[m, rows, :]
                totals = [totals[n] + r.local[m, first + n] * source for n in range(8)]
            for n in range(8):
                r.grad[k, first + n, rows, :] = r.control[k, first + n, rows, :] + totals[n] * scale
            return inner

        lax.fori_loop(0, 4, chunk, 0)
        return carry

    lax.fori_loop(first_member, last_member, member, 0)


def kernel(names, scale, *refs):
    r = types.SimpleNamespace(**dict(zip(names, refs)))
    e, c, ens, cols = places()
    levels = r.static.shape[0]
    members = r.control.shape[0]
    own = levels // ens

    def member_loads(k):
        return [
            pltpu.make_async_copy(r.control_hbm.at[k], r.control.at[k], r.control_load.at[k]),
            pltpu.make_async_copy(r.pert_hbm.at[k], r.pert.at[k], r.pert_load.at[k]),
        ]

    def load(name, n):
        return pltpu.make_async_copy(getattr(r, name + "_hbm"), getattr(r, name), r.load.at[n])

    early = [load("static", 0), load("north", 1), load("east", 2)]
    late = [load("index", 3), load("slot", 4), load("innovation", 5), load("weight", 6)]
    for one in early:
        one.start()

    def start_members(k, carry):
        for one in member_loads(k):
            one.start()
        return carry

    lax.fori_loop(0, members, start_members, 0)
    for one in late:
        one.start()
    barrier = pltpu.get_barrier_semaphore()
    greet_all(barrier)
    clear_rims([r.faces, r.halos.at[0], r.halos.at[1], r.halos.at[2], r.halos.at[3]])
    for one in early:
        one.wait()

    def product(i, carry):
        rows = pl.ds(pl.multiple_of(i * 32, 32), 32)
        totals = [jnp.zeros((32, LANES), jnp.float32)] * own
        for m in range(levels):
            source = r.static[m, rows, :]
            totals = [totals[l] + r.root[e * own + l, m] * source for l in range(own)]
        for l in range(own):
            r.fields[0, l, rows, :] = totals[l]
        return carry

    lax.fori_loop(0, 2, product, 0)
    wait_barrier(barrier)

    def halo_copies(field, n):
        return tile_copies(field, r.halos.at[n], r.halo_send.at[n], r.halo_recv.at[n])

    halo = halo_copies(r.fields.at[0], 0)
    start_tiles(halo)
    norths = tile_copies(r.north, r.faces.at[:, 0], r.face_send.at[0], r.face_recv.at[0])
    easts = tile_copies(r.east, r.faces.at[:, 1], r.face_send.at[1], r.face_recv.at[1])
    start_tiles(norths)
    start_tiles(easts)

    def send_part(d):
        peer = (e + d) % ens
        return send(
            r.part.at[pl.ds(peer * own, own)],
            r.terms.at[d - 1],
            r.term_send.at[d - 1],
            r.term_recv.at[d - 1],
            spot(peer, c),
        )

    level_part(r, (e + 2) % ens, own, scale, member_loads)
    sums = [send_part(2)]
    wait_tiles(norths)
    wait_tiles(easts)
    make_coefs(
        r.coefs,
        r.north[...],
        r.east[...],
        r.faces[0, 0],
        r.faces[0, 1],
        r.faces[1, 0],
        r.faces[1, 1],
        c > 0,
        c < cols - 1,
    )
    wait_tiles(halo)
    for l in range(own):
        r.fields[1, l] = two_steps(r.coefs, r.fields[0, l], r.halos[0, 0, l], r.halos[0, 1, l])
    halo = halo_copies(r.fields.at[1], 1)
    start_tiles(halo)
    level_part(r, (e + 1) % ens, own, scale, None)
    sums.append(send_part(1))
    level_part(r, (e + 3) % ens, own, scale, None)
    sums.append(send_part(3))
    level_part(r, e, own, scale, None)
    wait_tiles(halo)
    rows = r.table.shape[0] // own
    for l in range(own):
        total = two_steps(r.coefs, r.fields[1, l], r.halos[1, 0, l], r.halos[1, 1, l])
        r.table[l * rows : (l + 1) * rows, :] = total + r.part[e * own + l]
    for copy in sums:
        copy.wait()
    for l in range(own):
        total = r.table[l * rows : (l + 1) * rows, :]
        for d in range(ens - 1):
            total = total + r.terms[d, l]
        r.table[l * rows : (l + 1) * rows, :] = total
    for one in late:
        one.wait()
    picks(r)
    pltpu.make_async_copy(r.landing, r.landing, r.list_recv).wait()
    observe(r)
    give_back(r)
    wait_sends(r.picked, r.list_send)
    spread(r)

    halo = halo_copies(r.adjoint, 2)
    start_tiles(halo)
    wholes = share(r.adjoint, r.whole, r.whole_send, r.whole_recv)
    for l in range(own):
        r.whole[e * own + l] = r.adjoint[l]
    wait_sends(r.arrived, r.back_send)
    wait_tiles(halo)
    for l in range(own):
        r.fields[2, l] = two_steps(r.coefs, r.adjoint[l], r.halos[2, 0, l], r.halos[2, 1, l])
    halo = halo_copies(r.fields.at[2], 3)
    start_tiles(halo)
    for copy in wholes:
        copy.wait()
    member_products(r, scale, 0, 2)
    wait_tiles(halo)
    for l in range(own):
        r.fields[3, l] = two_steps(r.coefs, r.fields[2, l], r.halos[3, 0, l], r.halos[3, 1, l])
    smooths = share(r.fields.at[3], r.smooth, r.smooth_send, r.smooth_recv)
    for l in range(own):
        r.smooth[e * own + l] = r.fields[3, l]
    member_products(r, scale, 2, members)
    for copy in smooths:
        copy.wait()

    def static_product(i, carry):
        rows = pl.ds(pl.multiple_of((i // 2) * 32, 32), 32)
        first = (i % 2) * 8
        totals = [r.static[first + n, rows, :] for n in range(8)]
        for m in range(levels):
            source = r.smooth[m, rows, :]
            totals = [totals[n] + r.root[m, first + n] * source for n in range(8)]
        for n in range(8):
            r.static_grad[first + n, rows, :] = totals[n]
        return carry

    lax.fori_loop(0, 4, static_product, 0)


def store_kernel(static_ref, grad_ref, static_hbm, grad_hbm, static_sem, grad_sem):
    copies = [
        pltpu.make_async_copy(static_ref, static_hbm, static_sem),
        pltpu.make_async_copy(grad_ref, grad_hbm, grad_sem),
    ]
    for copy in copies:
        copy.start()
    for copy in copies:
        copy.wait()


def in_hbm(array):
    return pltpu.with_memory_space_constraint(array, pltpu.HBM)


def gradients(arrays, ens, scale):
    levels, rows, lanes = arrays["static"].shape
    own = levels // ens
    members = arrays["control"].shape[0]
    lists, capacity = arrays["index"].shape
    tiles = capacity // LANES
    half_rows = lists // ens * tiles
    f32, bf16 = jnp.float32, jnp.bfloat16
    dma = pltpu.SemaphoreType.DMA
    scalars = ("local", "root", "counts")
    loaded = ("static", "north", "east", "index", "slot", "innovation", "weight", "control", "pert")
    scratch = {name: pltpu.VMEM(arrays[name].shape, arrays[name].dtype) for name in loaded}
    scratch |= {
        "part": pltpu.VMEM((levels, rows, lanes), f32),
        "faces": pltpu.VMEM((2, 2, rows, lanes), f32),
        "coefs": pltpu.VMEM((COEFS, rows, lanes), f32),
        "fields": pltpu.VMEM((4, own, rows, lanes), f32),
        "halos": pltpu.VMEM((4, 2, own, rows, lanes), f32),
        "terms": pltpu.VMEM((ens - 1, own, rows, lanes), f32),
        "table": pltpu.VMEM((own * rows, lanes), f32),
        "cell_parts": pltpu.VMEM((2 * LANES, own * rows), bf16),
        "picked": pltpu.VMEM((lists, tiles, LANES), f32),
        "landing": pltpu.VMEM((ens, lists // ens, tiles, LANES), f32),
        "list_parts": pltpu.VMEM((2 * HALF, 2 * half_rows), bf16),
        "seen": pltpu.VMEM((2 * half_rows, 2 * HALF), f32),
        "returned": pltpu.VMEM((lists // ens, tiles, LANES), f32),
        "arrived": pltpu.VMEM((lists, tiles, LANES), f32),
        "both": pltpu.VMEM((own * rows, 2 * LANES), f32),
        "adjoint": pltpu.VMEM((own, rows, lanes), f32),
        "whole": pltpu.VMEM((levels, rows, lanes), f32),
        "smooth": pltpu.VMEM((levels, rows, lanes), f32),
        "load": dma((7,)),
        "control_load": dma((members,)),
        "pert_load": dma((members,)),
        "face_send": dma((2, 2)),
        "face_recv": dma((2, 2)),
        "halo_send": dma((4, 2)),
        "halo_recv": dma((4, 2)),
        "term_send": dma((ens - 1,)),
        "term_recv": dma((ens - 1,)),
        "list_send": dma,
        "list_recv": dma,
        "back_send": dma,
        "back_recv": dma((ens,)),
        "whole_send": dma((ens - 1,)),
        "whole_recv": dma((ens - 1,)),
        "smooth_send": dma((ens - 1,)),
        "smooth_recv": dma((ens - 1,)),
    }
    names = scalars + tuple(name + "_hbm" for name in loaded) + ("static_grad", "grad") + tuple(scratch)
    shapes = [arrays["static"].shape, arrays["control"].shape]
    static_grad, grad = pl.pallas_call(
        functools.partial(kernel, names, scale),
        in_specs=[SMEM] * len(scalars) + [ANY] * len(loaded),
        out_specs=[VMEM, VMEM],
        out_shape=[pltpu.VMEM(shape, f32) for shape in shapes],
        scratch_shapes=list(scratch.values()),
        compiler_params=params(collective_id=1, has_side_effects=True),
        name="gradients",
    )(*[arrays[name] for name in scalars], *[in_hbm(arrays[name]) for name in loaded])
    return pl.pallas_call(
        store_kernel,
        in_specs=[VMEM, VMEM],
        out_specs=[ANY, ANY],
        out_shape=[jax.ShapeDtypeStruct(shape, f32) for shape in shapes],
        scratch_shapes=[dma, dma],
        name="store",
    )(static_grad, grad)


def local(
    static_control,
    ensemble_control,
    perturbations,
    vertical_root,
    vertical_local,
    face_north,
    face_east,
    innovation,
    obs_weight,
    obs_slot,
    send_index,
    send_count,
):
    grid_rows = static_control.shape[1]
    ens = lax.axis_size("ens")
    arrays = {
        "local": vertical_local,
        "root": vertical_root,
        "counts": send_count,
        "static": to_tiles(static_control),
        "north": to_tiles(face_north),
        "east": to_tiles(face_east),
        "index": send_index,
        "slot": obs_slot.reshape(-1, LANES),
        "innovation": innovation.reshape(-1, LANES),
        "weight": obs_weight.reshape(-1, LANES),
        "control": to_tiles(ensemble_control),
        "pert": to_tiles(perturbations),
    }
    scale = 1.0 / math.sqrt(ensemble_control.shape[0] * ens - 1)
    static_grad, grad = gradients(arrays, ens, scale)
    return (from_tiles(static_grad, grid_rows), from_tiles(grad, grid_rows))


def solution(mesh):
    placed = (
        P(None, "cols", None),
        P("ens", None, "cols", None),
        P("ens", None, "cols", None),
        P(),
        P(),
        P("cols", None),
        P("cols", None),
        P("cols"),
        P("cols"),
        P("cols"),
        P("cols", None),
        P("cols"),
    )
    return jax.shard_map(
        local,
        mesh=mesh,
        in_specs=placed,
        out_specs=(P(None, "cols", None), P("ens", None, "cols", None)),
        check_vma=False,
    )
```

```python
import functools
import math
import types

import jax
import jax.numpy as jnp
from jax import lax
from jax.experimental import pallas as pl
from jax.experimental.pallas import tpu as pltpu
from jax.sharding import PartitionSpec as P

NDIFF = 4
LANES = 128
VMEM_LIMIT = 52 * 1024 * 1024

precise = lax.Precision.HIGHEST

SMEM = pl.BlockSpec(memory_space=pltpu.SMEM)
VMEM = pl.BlockSpec(memory_space=pltpu.VMEM)


def params(**more):
    return pltpu.CompilerParams(vmem_limit_bytes=VMEM_LIMIT, **more)


def to_tiles(cells):
    lead = cells.shape[:-2]
    rows, length = cells.shape[-2:]
    split = cells.reshape(lead + (rows, length // LANES, LANES))
    return jnp.swapaxes(split, -3, -2).reshape(lead + (rows * length // LANES, LANES))


def from_tiles(tiles, rows):
    lead = tiles.shape[:-2]
    count = tiles.shape[-2] // rows
    split = tiles.reshape(lead + (count, rows, LANES))
    return jnp.swapaxes(split, -3, -2).reshape(lead + (rows, count * LANES))


def iota(shape, dim):
    return lax.broadcasted_iota(jnp.int32, shape, dim)


def small(ids):
    return ids.astype(jnp.float32).astype(jnp.bfloat16)


def one_hot(ids, count):
    width = ids.shape[1]
    hit = small(iota((count, width), 0)) == small(ids)
    return jnp.where(hit, jnp.bfloat16(1), jnp.bfloat16(0))


def table_parts(table, parts_ref):
    lanes = table.shape[1]
    high = table.astype(jnp.bfloat16).astype(jnp.float32)
    parts_ref[:lanes, :] = high.T.astype(jnp.bfloat16)
    parts_ref[lanes:, :] = (table - high).T.astype(jnp.bfloat16)


def look_up(parts_ref, hot, lane):
    lanes = parts_ref.shape[0] // 2
    found = jnp.dot(parts_ref[...], hot, preferred_element_type=jnp.float32)
    found = found[:lanes] + found[lanes:]
    found = jnp.where(iota(found.shape, 0) == lane, found, 0.0)
    return jnp.sum(found, axis=0, keepdims=True)


def sum_up(hot, lane, values, lanes):
    high = values.astype(jnp.bfloat16)
    low = (values - high.astype(jnp.float32)).astype(jnp.bfloat16)
    hit = small(iota((lanes, lane.shape[1]), 0)) == small(lane)
    zero = jnp.bfloat16(0)
    parts = jnp.concatenate([jnp.where(hit, high, zero), jnp.where(hit, low, zero)], axis=0)
    return lax.dot_general(hot, parts, (((1,), (1,)), ((), ())), preferred_element_type=jnp.float32)


def as_row(block):
    return jnp.concatenate([block[i : i + 1, :] for i in range(block.shape[0])], axis=1)


def cell_place(index, first_cell, cells):
    inside = index - first_cell
    level = inside >> 13
    row = (level << 6) + (((inside >> 7) & 31) << 1) + ((inside >> 12) & 1)
    mine = (inside >= 0) & (inside < cells)
    return jnp.where(mine, row, -1), inside & (LANES - 1)


MESH = pl.DeviceIdType.MESH


def spot(ens, cols):
    return {"ens": ens, "cols": cols}


def places():
    return (lax.axis_index("ens"), lax.axis_index("cols"), lax.axis_size("ens"), lax.axis_size("cols"))


def greet(barrier, target):
    pl.semaphore_signal(barrier, inc=1, device_id=target, device_id_type=MESH)


def send(source, landing, send_sem, recv_sem, target):
    copy = pltpu.make_async_remote_copy(
        src_ref=source,
        dst_ref=landing,
        send_sem=send_sem,
        recv_sem=recv_sem,
        device_id=target,
        device_id_type=MESH,
    )
    copy.start()
    return copy


def odd_rows():
    return (lax.broadcasted_iota(jnp.int32, (64, LANES), 0) & 1) == 1


def swapped(tile):
    return jnp.where(odd_rows(), pltpu.roll(tile, 1, 0), pltpu.roll(tile, 63, 0))


def east_of(tile):
    near = pltpu.roll(tile, LANES - 1, 1)
    lane = lax.broadcasted_iota(jnp.int32, (64, LANES), 1)
    return jnp.where(lane == LANES - 1, pltpu.roll(near, 62, 0), near)


def west_of(tile):
    near = pltpu.roll(tile, 1, 1)
    lane = lax.broadcasted_iota(jnp.int32, (64, LANES), 1)
    return jnp.where(lane == 0, pltpu.roll(near, 2, 0), near)


COEFS = 10


def make_coefs(coef_ref, north, east, north_up, east_up, north_down, east_down, has_up, has_down):
    odd = odd_rows()
    keep_up = has_up.astype(jnp.float32)
    keep_down = has_down.astype(jnp.float32)
    north_down = north_down * keep_down
    pair = jnp.where(odd, north, swapped(north))
    outer = jnp.where(odd, swapped(north_down), north)
    east_rim = jnp.where(odd, east_up, east_down)
    west = west_of(east)
    west_rim = west_of(east_rim)
    inner = swapped(outer)
    far = jnp.where(odd, north_up, swapped(north_down))
    coef_ref[0] = 1.0 - pair - outer - east - west
    coef_ref[1] = pair
    coef_ref[2] = outer * jnp.where(odd, keep_down, keep_up)
    coef_ref[3] = east
    coef_ref[4] = west
    coef_ref[5] = 1.0 - inner - far - east_rim - west_rim
    coef_ref[6] = inner
    coef_ref[7] = far
    coef_ref[8] = east_rim
    coef_ref[9] = west_rim


def two_steps(coef_ref, own, up, down):
    odd = odd_rows()
    rim = jnp.where(odd, up, down)
    far = jnp.where(odd, down, up)
    own_swap = swapped(own)
    first = (
        coef_ref[0] * own
        + coef_ref[1] * own_swap
        + coef_ref[2] * swapped(rim)
        + coef_ref[3] * east_of(own)
        + coef_ref[4] * west_of(own)
    )
    rim = (
        coef_ref[5] * rim
        + coef_ref[6] * own_swap
        + coef_ref[7] * swapped(far)
        + coef_ref[8] * east_of(rim)
        + coef_ref[9] * west_of(rim)
    )
    return (
        coef_ref[0] * first
        + coef_ref[1] * swapped(first)
        + coef_ref[2] * swapped(rim)
        + coef_ref[3] * east_of(first)
        + coef_ref[4] * west_of(first)
    )


def neighbours():
    e, c, ens, cols = places()
    return spot(e, (c + cols - 1) % cols), spot(e, (c + 1) % cols)


def tile_copies(source, landing, send_sems, recv_sems):
    upper, lower = neighbours()
    return [
        pltpu.make_async_remote_copy(
            src_ref=source,
            dst_ref=landing.at[side],
            send_sem=send_sems.at[side],
            recv_sem=recv_sems.at[side],
            device_id=target,
            device_id_type=MESH,
        )
        for side, target in ((0, lower), (1, upper))
    ]


def start_tiles(copies):
    e, c, ens, cols = places()

    @pl.when(c < cols - 1)
    def _():
        copies[0].start()

    @pl.when(c > 0)
    def _():
        copies[1].start()


def wait_tiles(copies):
    e, c, ens, cols = places()

    @pl.when(c < cols - 1)
    def _():
        copies[0].wait_send()
        copies[1].wait_recv()

    @pl.when(c > 0)
    def _():
        copies[1].wait_send()
        copies[0].wait_recv()


def clear_rims(refs):
    e, c, ens, cols = places()
    for ref in refs:

        @pl.when(c == 0)
        def _(ref=ref):
            ref[0] = jnp.zeros(ref.shape[1:], jnp.float32)

        @pl.when(c == cols - 1)
        def _(ref=ref):
            ref[1] = jnp.zeros(ref.shape[1:], jnp.float32)


def greet_neighbours(barrier):
    e, c, ens, cols = places()
    upper, lower = neighbours()

    @pl.when(c > 0)
    def _():
        greet(barrier, upper)

    @pl.when(c < cols - 1)
    def _():
        greet(barrier, lower)

    for d in (1, ens - 1):
        greet(barrier, spot((e + d) % ens, c))


def list_home(c):
    z, y, core = c // 8, (c // 2) % 4, c % 2
    return (y + z + 2 * core) % 4, 2 * z + y // 2


def column_of(home, place):
    z = place // 2
    y = (place % 2) * 2 + (home + z) % 2
    return z * 8 + y * 2 + ((home + 8 - y - z) // 2) % 2


def wait_barrier(barrier):
    e, c, ens, cols = places()
    has_upper = (c + cols - 1) // cols
    has_lower = 1 - (c + 1) // cols
    home, place = list_home(c)
    all_leave = ((e - home + ens) % ens + ens - 1) // ens
    pl.semaphore_wait(barrier, 2 + has_upper + has_lower + cols - 1 + all_leave)


def wait_sends(lists_ref, send_sem):
    e, c, ens, cols = places()
    home, place = list_home(c)
    few = lists_ref.at[pl.ds(0, cols - 1)]

    @pl.when(e == home)
    def _():
        pltpu.make_async_copy(few, few, send_sem).wait()

    @pl.when(e != home)
    def _():
        pltpu.make_async_copy(lists_ref, lists_ref, send_sem).wait()


HALF = 64
BLOCK = 32
ANY = pl.BlockSpec(memory_space=pl.ANY)


def greet_all(barrier):
    e, c, ens, cols = places()
    group = cols // ens
    home, place = list_home(c)
    greet_neighbours(barrier)
    for n in range(cols - 1):
        greet(barrier, spot((e + 1 + n // group) % ens, column_of(e, (place + 1 + n) % group)))

    @pl.when(e != home)
    def _():
        greet(barrier, spot(e, column_of(e, place)))


def ring_neighbours():
    e, c, ens, cols = places()
    return spot((e + 1) % ens, c), spot((e + ens - 1) % ens, c)


class Share:
    def __init__(self, own_ref, whole_ref, send_sems, recv_sems):
        self.own, self.whole = own_ref, whole_ref
        self.send_sems, self.recv_sems = send_sems, recv_sems

    def start(self):
        e, c, ens, cols = places()
        count = self.own.shape[0]
        place = self.whole.at[pl.ds(e * count, count)]
        self.first = [
            send(self.own, place, self.send_sems.at[n], self.recv_sems.at[n], target)
            for n, target in enumerate(ring_neighbours())
        ]

    def pass_on(self):
        e, c, ens, cols = places()
        count = self.own.shape[0]
        half = count // 2
        starts = (((e + ens - 1) % ens) * count, ((e + 1) % ens) * count + half)
        self.second = []
        for n, target in enumerate(ring_neighbours()):
            self.first[n].wait_recv()
            part = self.whole.at[pl.ds(starts[n], half)]
            self.second.append(send(part, part, self.send_sems.at[2 + n], self.recv_sems.at[2 + n], target))

    def finish(self):
        for copy in self.first:
            copy.wait_send()
        for copy in self.second:
            copy.wait()


def level_part(r, peer, own, scale, loads):
    members, levels = r.control.shape[:2]
    first = peer * own

    def chunk(i, carry):
        rows = pl.ds(pl.multiple_of(i * 32, 32), 32)

        def member(k, totals):
            if loads is not None:

                @pl.when(i == 0)
                def _():
                    for load in loads(k):
                        load.wait()

            sums = [jnp.zeros((32, LANES), jnp.float32)] * own
            for m in range(levels):
                source = r.control[k, m, rows, :]
                sums = [sums[l] + r.local[first + l, m] * source for l in range(own)]
            return tuple(
                totals[l] + r.pert[k, first + l, rows, :].astype(jnp.float32) * sums[l] for l in range(own)
            )

        totals = lax.fori_loop(0, members, member, (jnp.zeros((32, LANES), jnp.float32),) * own)
        for l in range(own):
            r.part[first + l, rows, :] = totals[l] * scale
        return carry

    lax.fori_loop(0, 2, chunk, 0)


def picks(r):
    e, c, ens, cols = places()
    home, at = list_home(c)
    cell_rows = r.table.shape[0]
    cells = cell_rows * LANES
    capacity = r.index.shape[1]
    slots = iota((1, capacity), 1)
    place = r.landing.at[e, at]
    table_parts(r.table[...], r.cell_parts)

    def some(i, carry):
        for j in range(8):
            q = (c + 1 + i * 8 + j) % cols
            row, lane = cell_place(r.index[pl.ds(q, 1), :], e * cells, cells)
            row = jnp.where(slots < r.counts[q], row, -1)
            found = look_up(r.cell_parts, one_hot(row, cell_rows), lane)
            for t in range(capacity // LANES):
                r.picked[q, pl.ds(t, 1), :] = found[:, t * LANES : (t + 1) * LANES]
        for j in range(7):
            q = (c + 1 + i * 8 + j) % cols
            send(r.picked.at[q], place, r.list_send, r.list_recv, spot(home, q))
        q = (c + 8 + i * 8) % cols

        @pl.when((q != c) | (e != home))
        def _():
            send(r.picked.at[q], place, r.list_send, r.list_recv, spot(home, q))

        @pl.when((q == c) & (e == home))
        def _():
            pltpu.make_async_copy(r.picked.at[q], place, r.list_recv).start()

        return carry

    lax.fori_loop(0, cols // 8, some, 0)


def observe(r):
    e, c, ens, cols = places()
    total = r.landing[0]
    for n in range(1, ens):
        total = total + r.landing[n]
    half_rows = total.shape[0] * total.shape[1]
    table = total.reshape(half_rows, LANES)
    table_parts(jnp.concatenate([table[:, :HALF], table[:, HALF:]], axis=0), r.list_parts)
    r.seen[...] = jnp.zeros_like(r.seen)

    def some(i, carry):
        total = jnp.zeros(r.seen.shape, jnp.float32)
        for j in range(2):
            at = pl.ds(pl.multiple_of((i * 2 + j) * BLOCK, BLOCK), BLOCK)
            slot = r.slot[at, :]
            z, y, core = slot >> 13, (slot >> 11) & 3, (slot >> 10) & 1
            mine = ((y + z + 2 * core) & 3) == e
            row = (((z << 1) + (y >> 1)) << 3) + ((slot >> 7) & 7) + ((slot >> 6) & 1) * half_rows
            lane = as_row(slot & (HALF - 1))
            hot = one_hot(as_row(jnp.where(mine, row, -1)), 2 * half_rows)
            found = look_up(r.list_parts, hot, lane)
            weighted = as_row(r.weight[at, :]) * (found - as_row(r.innovation[at, :]))
            total = total + sum_up(hot, lane, weighted, HALF)
        r.seen[...] += total
        return carry

    lax.fori_loop(0, r.slot.shape[0] // (2 * BLOCK), some, 0)
    seen = r.seen[:, :HALF] + r.seen[:, HALF:]
    r.returned[...] = jnp.concatenate([seen[:half_rows], seen[half_rows:]], axis=1).reshape(r.returned.shape)


def give_back(r):
    e, c, ens, cols = places()
    group = cols // ens
    z = c // group
    home, at = list_home(c)

    def step(n, carry):
        i = (at + 1 + n) % group
        target = spot((e + 1 + n // group) % ens, column_of(e, i))
        send(r.returned.at[i], r.arrived.at[c], r.back_send, r.back_recv.at[z], target)
        return carry

    lax.fori_loop(0, cols - 1, step, 0)

    @pl.when(e != home)
    def _():
        target = spot(e, column_of(e, at))
        send(r.returned.at[at], r.arrived.at[c], r.back_send, r.back_recv.at[z], target)

    @pl.when(e == home)
    def _():
        pltpu.make_async_copy(r.returned.at[at], r.arrived.at[c], r.back_recv.at[z]).start()


def spread(r):
    e, c, ens, cols = places()
    group = cols // ens
    capacity = r.index.shape[1]
    slots = iota((1, capacity), 1)
    cell_rows = r.both.shape[0]
    cells = cell_rows * LANES
    r.both[...] = jnp.zeros_like(r.both)

    def some(i, carry):
        lists = r.arrived.at[pl.ds(i * group, group)]
        pltpu.make_async_copy(lists, lists, r.back_recv.at[i]).wait()
        total = jnp.zeros(r.both.shape, jnp.float32)
        for j in range(group):
            q = i * group + j
            row, lane = cell_place(r.index[pl.ds(q, 1), :], e * cells, cells)
            row = jnp.where(slots < r.counts[q], row, -1)
            total = total + sum_up(one_hot(row, cell_rows), lane, as_row(r.arrived[q]), LANES)
        r.both[...] += total
        return carry

    lax.fori_loop(0, ens, some, 0)
    r.adjoint[...] = (r.both[:, :LANES] + r.both[:, LANES:]).reshape(r.adjoint.shape)


def member_products(r, scale, first_member, last_member):
    levels = r.static.shape[0]

    def member(k, carry):
        def chunk(i, inner):
            rows = pl.ds(pl.multiple_of((i // 2) * 32, 32), 32)
            first = (i % 2) * 8
            totals = [jnp.zeros((32, LANES), jnp.float32)] * 8
            for m in range(levels):
                source = r.pert[k, m, rows, :].astype(jnp.float32) * r.whole[m, rows, :]
                totals = [totals[n] + r.local[m, first + n] * source for n in range(8)]
            for n in range(8):
                r.grad[k, first + n, rows, :] = r.control[k, first + n, rows, :] + totals[n] * scale
            return inner

        lax.fori_loop(0, 4, chunk, 0)
        return carry

    lax.fori_loop(first_member, last_member, member, 0)


def kernel(names, scale, *refs):
    r = types.SimpleNamespace(**dict(zip(names, refs)))
    e, c, ens, cols = places()
    levels = r.static.shape[0]
    members = r.control.shape[0]
    own = levels // ens

    def member_loads(k):
        return [
            pltpu.make_async_copy(r.control_hbm.at[k], r.control.at[k], r.control_load.at[k]),
            pltpu.make_async_copy(r.pert_hbm.at[k], r.pert.at[k], r.pert_load.at[k]),
        ]

    def load(name, n):
        return pltpu.make_async_copy(getattr(r, name + "_hbm"), getattr(r, name), r.load.at[n])

    early = [load("static", 0), load("north", 1), load("east", 2)]
    late = [load("index", 3), load("slot", 4), load("innovation", 5), load("weight", 6)]
    for one in early:
        one.start()

    def start_members(k, carry):
        for one in member_loads(k):
            one.start()
        return carry

    lax.fori_loop(0, members, start_members, 0)
    for one in late:
        one.start()
    barrier = pltpu.get_barrier_semaphore()
    greet_all(barrier)
    clear_rims([r.faces, r.halos.at[0], r.halos.at[1], r.halos.at[2], r.halos.at[3]])
    for one in early:
        one.wait()

    def product(i, carry):
        rows = pl.ds(pl.multiple_of(i * 32, 32), 32)
        totals = [jnp.zeros((32, LANES), jnp.float32)] * own
        for m in range(levels):
            source = r.static[m, rows, :]
            totals = [totals[l] + r.root[e * own + l, m] * source for l in range(own)]
        for l in range(own):
            r.fields[0, l, rows, :] = totals[l]
        return carry

    lax.fori_loop(0, 2, product, 0)
    wait_barrier(barrier)

    def halo_copies(field, n):
        return tile_copies(field, r.halos.at[n], r.halo_send.at[n], r.halo_recv.at[n])

    halo = halo_copies(r.fields.at[0], 0)
    start_tiles(halo)
    norths = tile_copies(r.north, r.faces.at[:, 0], r.face_send.at[0], r.face_recv.at[0])
    easts = tile_copies(r.east, r.faces.at[:, 1], r.face_send.at[1], r.face_recv.at[1])
    start_tiles(norths)
    start_tiles(easts)

    right, left = (e + 1) % ens, (e + ens - 1) % ens
    opposite = (e + 2) % ens
    half = own // 2
    ring = ring_neighbours()
    level_part(r, opposite, own, scale, member_loads)
    relays = [
        send(
            r.part.at[pl.ds(opposite * own + n * half, half)],
            r.relayed.at[n],
            r.term_send.at[n],
            r.term_recv.at[n],
            ring[n],
        )
        for n in range(2)
    ]

    def send_part(peer, n):
        relays[n].wait_recv()
        for l in range(half):
            r.part[peer * own + n * half + l] += r.relayed[n, l]
        return send(
            r.part.at[pl.ds(peer * own, own)],
            r.terms.at[n],
            r.term_send.at[2 + n],
            r.term_recv.at[2 + n],
            ring[n],
        )

    wait_tiles(norths)
    wait_tiles(easts)
    make_coefs(
        r.coefs,
        r.north[...],
        r.east[...],
        r.faces[0, 0],
        r.faces[0, 1],
        r.faces[1, 0],
        r.faces[1, 1],
        c > 0,
        c < cols - 1,
    )
    wait_tiles(halo)
    for l in range(own):
        r.fields[1, l] = two_steps(r.coefs, r.fields[0, l], r.halos[0, 0, l], r.halos[0, 1, l])
    halo = halo_copies(r.fields.at[1], 1)
    start_tiles(halo)
    level_part(r, right, own, scale, None)
    sums = [send_part(right, 0)]
    level_part(r, left, own, scale, None)
    sums.append(send_part(left, 1))
    level_part(r, e, own, scale, None)
    wait_tiles(halo)
    rows = r.table.shape[0] // own
    for l in range(own):
        total = two_steps(r.coefs, r.fields[1, l], r.halos[1, 0, l], r.halos[1, 1, l])
        r.table[l * rows : (l + 1) * rows, :] = total + r.part[e * own + l]
    for copy in relays:
        copy.wait_send()
    for copy in sums:
        copy.wait()
    for l in range(own):
        at = slice(l * rows, (l + 1) * rows)
        r.table[at, :] = r.table[at, :] + (r.terms[0, l] + r.terms[1, l])
    for one in late:
        one.wait()
    picks(r)
    pltpu.make_async_copy(r.landing, r.landing, r.list_recv).wait()
    observe(r)
    give_back(r)
    wait_sends(r.picked, r.list_send)
    spread(r)

    halo = halo_copies(r.adjoint, 2)
    start_tiles(halo)
    wholes = Share(r.adjoint, r.whole, r.whole_send, r.whole_recv)
    wholes.start()
    for l in range(own):
        r.whole[e * own + l] = r.adjoint[l]
    wait_sends(r.arrived, r.back_send)
    wait_tiles(halo)
    for l in range(own):
        r.fields[2, l] = two_steps(r.coefs, r.adjoint[l], r.halos[2, 0, l], r.halos[2, 1, l])
    halo = halo_copies(r.fields.at[2], 3)
    start_tiles(halo)
    wholes.pass_on()
    wholes.finish()
    member_products(r, scale, 0, 1)
    wait_tiles(halo)
    for l in range(own):
        r.fields[3, l] = two_steps(r.coefs, r.fields[2, l], r.halos[3, 0, l], r.halos[3, 1, l])
    smooths = Share(r.fields.at[3], r.smooth, r.smooth_send, r.smooth_recv)
    smooths.start()
    for l in range(own):
        r.smooth[e * own + l] = r.fields[3, l]
    member_products(r, scale, 1, 4)
    smooths.pass_on()
    member_products(r, scale, 4, members)
    smooths.finish()

    def static_product(i, carry):
        rows = pl.ds(pl.multiple_of((i // 2) * 32, 32), 32)
        first = (i % 2) * 8
        totals = [r.static[first + n, rows, :] for n in range(8)]
        for m in range(levels):
            source = r.smooth[m, rows, :]
            totals = [totals[n] + r.root[m, first + n] * source for n in range(8)]
        for n in range(8):
            r.static_grad[first + n, rows, :] = totals[n]
        return carry

    lax.fori_loop(0, 4, static_product, 0)


def in_hbm(array):
    return pltpu.with_memory_space_constraint(array, pltpu.HBM)


def gradients(arrays, ens, scale):
    levels, rows, lanes = arrays["static"].shape
    own = levels // ens
    members = arrays["control"].shape[0]
    lists, capacity = arrays["index"].shape
    tiles = capacity // LANES
    half_rows = lists // ens * tiles
    f32, bf16 = jnp.float32, jnp.bfloat16
    dma = pltpu.SemaphoreType.DMA
    scalars = ("local", "root", "counts")
    loaded = ("static", "north", "east", "index", "slot", "innovation", "weight", "control", "pert")
    scratch = {name: pltpu.VMEM(arrays[name].shape, arrays[name].dtype) for name in loaded}
    scratch |= {
        "part": pltpu.VMEM((levels, rows, lanes), f32),
        "faces": pltpu.VMEM((2, 2, rows, lanes), f32),
        "coefs": pltpu.VMEM((COEFS, rows, lanes), f32),
        "fields": pltpu.VMEM((4, own, rows, lanes), f32),
        "halos": pltpu.VMEM((4, 2, own, rows, lanes), f32),
        "relayed": pltpu.VMEM((2, own // 2, rows, lanes), f32),
        "terms": pltpu.VMEM((2, own, rows, lanes), f32),
        "table": pltpu.VMEM((own * rows, lanes), f32),
        "cell_parts": pltpu.VMEM((2 * LANES, own * rows), bf16),
        "picked": pltpu.VMEM((lists, tiles, LANES), f32),
        "landing": pltpu.VMEM((ens, lists // ens, tiles, LANES), f32),
        "list_parts": pltpu.VMEM((2 * HALF, 2 * half_rows), bf16),
        "seen": pltpu.VMEM((2 * half_rows, 2 * HALF), f32),
        "returned": pltpu.VMEM((lists // ens, tiles, LANES), f32),
        "arrived": pltpu.VMEM((lists, tiles, LANES), f32),
        "both": pltpu.VMEM((own * rows, 2 * LANES), f32),
        "adjoint": pltpu.VMEM((own, rows, lanes), f32),
        "whole": pltpu.VMEM((levels, rows, lanes), f32),
        "smooth": pltpu.VMEM((levels, rows, lanes), f32),
        "load": dma((7,)),
        "control_load": dma((members,)),
        "pert_load": dma((members,)),
        "face_send": dma((2, 2)),
        "face_recv": dma((2, 2)),
        "halo_send": dma((4, 2)),
        "halo_recv": dma((4, 2)),
        "term_send": dma((4,)),
        "term_recv": dma((4,)),
        "list_send": dma,
        "list_recv": dma,
        "back_send": dma,
        "back_recv": dma((ens,)),
        "whole_send": dma((4,)),
        "whole_recv": dma((4,)),
        "smooth_send": dma((4,)),
        "smooth_recv": dma((4,)),
    }
    names = scalars + tuple(name + "_hbm" for name in loaded) + ("static_grad", "grad") + tuple(scratch)
    shapes = [arrays["static"].shape, arrays["control"].shape]
    return pl.pallas_call(
        functools.partial(kernel, names, scale),
        in_specs=[SMEM] * len(scalars) + [ANY] * len(loaded),
        out_specs=[VMEM, VMEM],
        out_shape=[pltpu.VMEM(shape, f32) for shape in shapes],
        scratch_shapes=list(scratch.values()),
        compiler_params=params(collective_id=1, has_side_effects=True),
        name="gradients",
    )(*[arrays[name] for name in scalars], *[in_hbm(arrays[name]) for name in loaded])


def local(
    static_control,
    ensemble_control,
    perturbations,
    vertical_root,
    vertical_local,
    face_north,
    face_east,
    innovation,
    obs_weight,
    obs_slot,
    send_index,
    send_count,
):
    grid_rows = static_control.shape[1]
    ens = lax.axis_size("ens")
    arrays = {
        "local": vertical_local,
        "root": vertical_root,
        "counts": send_count,
        "static": to_tiles(static_control),
        "north": to_tiles(face_north),
        "east": to_tiles(face_east),
        "index": send_index,
        "slot": obs_slot.reshape(-1, LANES),
        "innovation": innovation.reshape(-1, LANES),
        "weight": obs_weight.reshape(-1, LANES),
        "control": to_tiles(ensemble_control),
        "pert": to_tiles(perturbations),
    }
    scale = 1.0 / math.sqrt(ensemble_control.shape[0] * ens - 1)
    static_grad, grad = gradients(arrays, ens, scale)
    return (from_tiles(static_grad, grid_rows), from_tiles(grad, grid_rows))


def solution(mesh):
    placed = (
        P(None, "cols", None),
        P("ens", None, "cols", None),
        P("ens", None, "cols", None),
        P(),
        P(),
        P("cols", None),
        P("cols", None),
        P("cols"),
        P("cols"),
        P("cols"),
        P("cols", None),
        P("cols"),
    )
    return jax.shard_map(
        local,
        mesh=mesh,
        in_specs=placed,
        out_specs=(P(None, "cols", None), P("ens", None, "cols", None)),
        check_vma=False,
    )
```

```python
import functools
import math
import types

import jax
import jax.numpy as jnp
from jax import lax
from jax.experimental import pallas as pl
from jax.experimental.pallas import tpu as pltpu
from jax.sharding import PartitionSpec as P

NDIFF = 4
LANES = 128
VMEM_LIMIT = 52 * 1024 * 1024

precise = lax.Precision.HIGHEST

SMEM = pl.BlockSpec(memory_space=pltpu.SMEM)
VMEM = pl.BlockSpec(memory_space=pltpu.VMEM)


def params(**more):
    return pltpu.CompilerParams(vmem_limit_bytes=VMEM_LIMIT, **more)


def to_tiles(cells):
    lead = cells.shape[:-2]
    rows, length = cells.shape[-2:]
    split = cells.reshape(lead + (rows, length // LANES, LANES))
    return jnp.swapaxes(split, -3, -2).reshape(lead + (rows * length // LANES, LANES))


def from_tiles(tiles, rows):
    lead = tiles.shape[:-2]
    count = tiles.shape[-2] // rows
    split = tiles.reshape(lead + (count, rows, LANES))
    return jnp.swapaxes(split, -3, -2).reshape(lead + (rows, count * LANES))


def iota(shape, dim):
    return lax.broadcasted_iota(jnp.int32, shape, dim)


def small(ids):
    return ids.astype(jnp.float32).astype(jnp.bfloat16)


def one_hot(ids, count):
    width = ids.shape[1]
    hit = small(iota((count, width), 0)) == small(ids)
    return jnp.where(hit, jnp.bfloat16(1), jnp.bfloat16(0))


def table_parts(table, parts_ref):
    lanes = table.shape[1]
    high = table.astype(jnp.bfloat16).astype(jnp.float32)
    parts_ref[:lanes, :] = high.T.astype(jnp.bfloat16)
    parts_ref[lanes:, :] = (table - high).T.astype(jnp.bfloat16)


def look_up(parts_ref, hot, lane):
    lanes = parts_ref.shape[0] // 2
    found = jnp.dot(parts_ref[...], hot, preferred_element_type=jnp.float32)
    found = found[:lanes] + found[lanes:]
    found = jnp.where(iota(found.shape, 0) == lane, found, 0.0)
    return jnp.sum(found, axis=0, keepdims=True)


def sum_up(hot, lane, values, lanes):
    high = values.astype(jnp.bfloat16)
    low = (values - high.astype(jnp.float32)).astype(jnp.bfloat16)
    hit = small(iota((lanes, lane.shape[1]), 0)) == small(lane)
    zero = jnp.bfloat16(0)
    parts = jnp.concatenate([jnp.where(hit, high, zero), jnp.where(hit, low, zero)], axis=0)
    return lax.dot_general(hot, parts, (((1,), (1,)), ((), ())), preferred_element_type=jnp.float32)


def as_row(block):
    return jnp.concatenate([block[i : i + 1, :] for i in range(block.shape[0])], axis=1)


def cell_place(index, first_cell, cells):
    inside = index - first_cell
    level = inside >> 13
    row = (level << 6) + (((inside >> 7) & 31) << 1) + ((inside >> 12) & 1)
    mine = (inside >= 0) & (inside < cells)
    return jnp.where(mine, row, -1), inside & (LANES - 1)


MESH = pl.DeviceIdType.MESH


def spot(ens, cols):
    return {"ens": ens, "cols": cols}


def places():
    return (lax.axis_index("ens"), lax.axis_index("cols"), lax.axis_size("ens"), lax.axis_size("cols"))


def greet(barrier, target):
    pl.semaphore_signal(barrier, inc=1, device_id=target, device_id_type=MESH)


def send(source, landing, send_sem, recv_sem, target):
    copy = pltpu.make_async_remote_copy(
        src_ref=source,
        dst_ref=landing,
        send_sem=send_sem,
        recv_sem=recv_sem,
        device_id=target,
        device_id_type=MESH,
    )
    copy.start()
    return copy


def odd_rows():
    return (iota((64, LANES), 0) & 1) == 1


def blend(odd, even):
    return jnp.where(odd_rows(), odd, even)


def swapped(tile):
    return blend(pltpu.roll(tile, 1, 0), pltpu.roll(tile, 63, 0))


def east_of(tile):
    near = pltpu.roll(tile, LANES - 1, 1)
    return jnp.where(iota((64, LANES), 1) == LANES - 1, pltpu.roll(near, 62, 0), near)


def west_of(tile):
    near = pltpu.roll(tile, 1, 1)
    return jnp.where(iota((64, LANES), 1) == 0, pltpu.roll(near, 2, 0), near)


SIDES = ((0, 2), (1, 1), (2, -1), (3, -2))
UP1, OWN, DOWN1, RIM2, RIM1 = range(5)


def make_coefs(coefs, own, faces):
    e, c, ens, cols = places()

    def keep(condition):
        return condition.astype(jnp.float32)

    up2, up1, down1, down2 = [faces[n, 0] for n in range(4)]
    norths = (up1, own[0], down1)
    belows = (own[0], down1, down2)
    easts = (faces[1, 1], own[1], faces[2, 1])
    keeps = (keep(c > 0), 1.0, keep(c < cols - 1))

    def put(t, pair, outer, east, kept):
        west = west_of(east)
        coefs[t, 0] = (1.0 - pair - outer - east - west) * kept
        coefs[t, 1] = pair * kept
        coefs[t, 2] = outer * kept
        coefs[t, 3] = east * kept
        coefs[t, 4] = west * kept

    for t in range(3):
        north = norths[t]
        put(t, blend(north, swapped(north)), blend(swapped(belows[t]), north), easts[t], keeps[t])
    put(
        RIM2,
        blend(up2, swapped(down2)),
        blend(swapped(up1), down2),
        blend(faces[0, 1], faces[3, 1]),
        blend(keep(c > 1), keep(c < cols - 2)),
    )
    for n in range(5):
        coefs[RIM1, n] = blend(coefs[UP1, n], coefs[DOWN1, n])


def step_tile(coefs, t, tile, beside, beyond):
    return (
        coefs[t, 0] * tile
        + coefs[t, 1] * swapped(beside)
        + coefs[t, 2] * swapped(beyond)
        + coefs[t, 3] * east_of(tile)
        + coefs[t, 4] * west_of(tile)
    )


def diffused(coefs, own, up2, up1, down1, down2):
    rim = step_tile(coefs, RIM2, blend(up2, down2), blend(down2, up2), blend(down1, up1))
    up, here, down = (
        step_tile(coefs, UP1, up1, up1, blend(up2, own)),
        step_tile(coefs, OWN, own, own, blend(up1, down1)),
        step_tile(coefs, DOWN1, down1, down1, blend(own, down2)),
    )
    up, here, down = (
        step_tile(coefs, UP1, up, up, blend(rim, here)),
        step_tile(coefs, OWN, here, here, blend(up, down)),
        step_tile(coefs, DOWN1, down, down, blend(here, rim)),
    )
    rim = blend(up, down)
    rim, here = (
        step_tile(coefs, RIM1, rim, blend(down, up), here),
        step_tile(coefs, OWN, here, here, rim),
    )
    return step_tile(coefs, OWN, here, here, rim)


def with_side(by, action):
    e, c, ens, cols = places()
    pl.when(c < cols - by if by > 0 else c >= -by)(action)


def tile_copies(source, landing, send_sems, recv_sems):
    e, c, ens, cols = places()
    return [
        pltpu.make_async_remote_copy(
            src_ref=source,
            dst_ref=landing.at[n],
            send_sem=send_sems.at[n],
            recv_sem=recv_sems.at[n],
            device_id=spot(e, (c + by + cols) % cols),
            device_id_type=MESH,
        )
        for n, by in SIDES
    ]


def start_tiles(copies):
    for n, by in SIDES:
        with_side(by, copies[n].start)


def wait_tiles(copies):
    for n, by in SIDES:
        with_side(by, copies[n].wait_send)
        with_side(-by, copies[n].wait_recv)


def clear_rims(refs):
    e, c, ens, cols = places()
    for ref in refs:
        for n, by in SIDES:

            @pl.when(c < by if by > 0 else c >= cols + by)
            def _(ref=ref, n=n):
                ref[n] = jnp.zeros(ref.shape[1:], jnp.float32)


def greet_neighbours(barrier):
    e, c, ens, cols = places()
    for n, by in SIDES:
        with_side(by, functools.partial(greet, barrier, spot(e, (c + by + cols) % cols)))
    for d in range(1, ens):
        greet(barrier, spot((e + d) % ens, c))


def column_of(place):
    e, c, ens, cols = places()
    return place * ens + (e - c + cols) % ens


def wait_barrier(barrier):
    e, c, ens, cols = places()
    around = 0
    for n, by in SIDES:
        around = around + (1 - (c + by) // cols if by > 0 else (c + cols + by) // cols)
    all_leave = ((e - 2 * c + 2 * cols) % ens + ens - 1) // ens
    pl.semaphore_wait(barrier, ens - 1 + around + cols - 1 + all_leave)


def wait_sends(lists_ref, send_sem):
    e, c, ens, cols = places()
    few = lists_ref.at[pl.ds(0, cols - 1)]

    @pl.when(e == (2 * c) % ens)
    def _():
        pltpu.make_async_copy(few, few, send_sem).wait()

    @pl.when(e != (2 * c) % ens)
    def _():
        pltpu.make_async_copy(lists_ref, lists_ref, send_sem).wait()


HALF = 64
BLOCK = 32
ANY = pl.BlockSpec(memory_space=pl.ANY)


def greet_all(barrier):
    e, c, ens, cols = places()
    group = cols // ens
    at = c // ens
    greet_neighbours(barrier)

    def senders(n, carry):
        greet(barrier, spot((e + 1 + n // group) % ens, column_of((at + 1 + n) % group)))
        return carry

    lax.fori_loop(0, cols - 1, senders, 0)

    @pl.when(e != (2 * c) % ens)
    def _():
        greet(barrier, spot(e, column_of(at)))


def share(own_ref, whole_ref, send_sems, recv_sems):
    e, c, ens, cols = places()
    count = own_ref.shape[0]
    return [
        send(
            own_ref,
            whole_ref.at[pl.ds(e * count, count)],
            send_sems.at[d - 1],
            recv_sems.at[d - 1],
            spot((e + d) % ens, c),
        )
        for d in (2, 1, 3)
    ]


def level_part(r, peer, own, scale, i, loads=None):
    members, levels = r.control.shape[:2]
    first = peer * own
    rows = pl.ds(i * 32, 32)

    def member(k, totals):
        if loads is not None:
            for load in loads(k):
                load.wait()
        sums = [jnp.zeros((32, LANES), jnp.float32)] * own
        for m in range(levels):
            source = r.control[k, m, rows, :]
            sums = [sums[l] + r.local[first + l, m] * source for l in range(own)]
        return tuple(
            totals[l] + r.pert[k, first + l, rows, :].astype(jnp.float32) * sums[l] for l in range(own)
        )

    totals = lax.fori_loop(0, members, member, (jnp.zeros((32, LANES), jnp.float32),) * own)
    for l in range(own):
        r.part[first + l, rows, :] = totals[l] * scale


def picks(r):
    e, c, ens, cols = places()
    cell_rows = r.table.shape[0]
    cells = cell_rows * LANES
    capacity = r.index.shape[1]
    slots = iota((1, capacity), 1)
    place = r.landing.at[e, c // ens]
    table_parts(r.table[...], r.cell_parts)

    def some(i, carry):
        for j in range(8):
            q = (c + 1 + i * 8 + j) % cols
            row, lane = cell_place(r.index[pl.ds(q, 1), :], e * cells, cells)
            row = jnp.where(slots < r.counts[q], row, -1)
            found = look_up(r.cell_parts, one_hot(row, cell_rows), lane)
            for t in range(capacity // LANES):
                r.picked[q, pl.ds(t, 1), :] = found[:, t * LANES : (t + 1) * LANES]
        for j in range(7):
            q = (c + 1 + i * 8 + j) % cols
            send(r.picked.at[q], place, r.list_send, r.list_recv, spot((c + q) % ens, q))
        q = (c + 8 + i * 8) % cols

        @pl.when((q != c) | (e != (2 * c) % ens))
        def _():
            send(r.picked.at[q], place, r.list_send, r.list_recv, spot((c + q) % ens, q))

        @pl.when((q == c) & (e == (2 * c) % ens))
        def _():
            pltpu.make_async_copy(r.picked.at[q], place, r.list_recv).start()

        return carry

    lax.fori_loop(0, cols // 8, some, 0)


def observe(r):
    e, c, ens, cols = places()
    total = r.landing[0]
    for n in range(1, ens):
        total = total + r.landing[n]
    half_rows = total.shape[0] * total.shape[1]
    table = total.reshape(half_rows, LANES)
    table_parts(jnp.concatenate([table[:, :HALF], table[:, HALF:]], axis=0), r.list_parts)
    r.seen[...] = jnp.zeros_like(r.seen)

    def some(i, carry):
        total = jnp.zeros(r.seen.shape, jnp.float32)
        for j in range(2):
            at = pl.ds(pl.multiple_of((i * 2 + j) * BLOCK, BLOCK), BLOCK)
            slot = r.slot[at, :]
            column = slot >> 10
            mine = ((column + c) & (ens - 1)) == e
            row = ((column >> 2) << 3) + ((slot >> 7) & 7) + ((slot >> 6) & 1) * half_rows
            lane = as_row(slot & (HALF - 1))
            hot = one_hot(as_row(jnp.where(mine, row, -1)), 2 * half_rows)
            found = look_up(r.list_parts, hot, lane)
            weighted = as_row(r.weight[at, :]) * (found - as_row(r.innovation[at, :]))
            total = total + sum_up(hot, lane, weighted, HALF)
        r.seen[...] += total
        return carry

    lax.fori_loop(0, r.slot.shape[0] // (2 * BLOCK), some, 0)
    seen = r.seen[:, :HALF] + r.seen[:, HALF:]
    r.returned[...] = jnp.concatenate([seen[:half_rows], seen[half_rows:]], axis=1).reshape(r.returned.shape)


def give_back(r):
    e, c, ens, cols = places()
    group = cols // ens
    at = c // ens
    recv = r.back_recv.at[c // group]

    def step(n, carry):
        i = (at + 1 + n) % group
        target = spot((e + 1 + n // group) % ens, column_of(i))
        send(r.returned.at[i], r.arrived.at[c], r.back_send, recv, target)
        return carry

    lax.fori_loop(0, cols - 1, step, 0)

    @pl.when(e != (2 * c) % ens)
    def _():
        send(r.returned.at[at], r.arrived.at[c], r.back_send, recv, spot(e, column_of(at)))

    @pl.when(e == (2 * c) % ens)
    def _():
        pltpu.make_async_copy(r.returned.at[at], r.arrived.at[c], recv).start()


def spread(r):
    e, c, ens, cols = places()
    group = cols // ens
    capacity = r.index.shape[1]
    slots = iota((1, capacity), 1)
    cell_rows = r.both.shape[0]
    cells = cell_rows * LANES
    r.both[...] = jnp.zeros_like(r.both)

    def some(i, carry):
        lists = r.arrived.at[pl.ds(i * group, group)]
        pltpu.make_async_copy(lists, lists, r.back_recv.at[i]).wait()
        total = jnp.zeros(r.both.shape, jnp.float32)
        for j in range(group):
            q = i * group + j
            row, lane = cell_place(r.index[pl.ds(q, 1), :], e * cells, cells)
            row = jnp.where(slots < r.counts[q], row, -1)
            total = total + sum_up(one_hot(row, cell_rows), lane, as_row(r.arrived[q]), LANES)
        r.both[...] += total
        return carry

    lax.fori_loop(0, ens, some, 0)
    r.adjoint[...] = (r.both[:, :LANES] + r.both[:, LANES:]).reshape(r.adjoint.shape)


def member_products(r, scale, first_member, last_member):
    levels = r.static.shape[0]

    def member(k, carry):
        def chunk(i, inner):
            rows = pl.ds(pl.multiple_of((i // 2) * 32, 32), 32)
            first = (i % 2) * 8
            totals = [jnp.zeros((32, LANES), jnp.float32)] * 8
            for m in range(levels):
                source = r.pert[k, m, rows, :].astype(jnp.float32) * r.whole[m, rows, :]
                totals = [totals[n] + r.local[m, first + n] * source for n in range(8)]
            for n in range(8):
                r.grad[k, first + n, rows, :] = r.control[k, first + n, rows, :] + totals[n] * scale
            return inner

        lax.fori_loop(0, 4, chunk, 0)
        return carry

    lax.fori_loop(first_member, last_member, member, 0)


def kernel(names, scale, *refs):
    r = types.SimpleNamespace(**dict(zip(names, refs)))
    e, c, ens, cols = places()
    levels = r.static.shape[0]
    members = r.control.shape[0]
    own = levels // ens

    def member_loads(k):
        return [
            pltpu.make_async_copy(r.control_hbm.at[k], r.control.at[k], r.control_load.at[k]),
            pltpu.make_async_copy(r.pert_hbm.at[k], r.pert.at[k], r.pert_load.at[k]),
        ]

    def load(name, n):
        return pltpu.make_async_copy(getattr(r, name + "_hbm"), getattr(r, name), r.load.at[n])

    early = [
        load("static", 0),
        pltpu.make_async_copy(r.north_hbm, r.own_faces.at[0], r.load.at[1]),
        pltpu.make_async_copy(r.east_hbm, r.own_faces.at[1], r.load.at[2]),
    ]
    late = [load("index", 3), load("slot", 4), load("innovation", 5), load("weight", 6)]
    for one in early:
        one.start()

    def start_members(k, carry):
        for one in member_loads(k):
            one.start()
        return carry

    lax.fori_loop(0, members, start_members, 0)
    for one in late:
        one.start()
    barrier = pltpu.get_barrier_semaphore()
    greet_all(barrier)
    clear_rims([r.faces, r.halos.at[0], r.halos.at[1]])
    for one in early:
        one.wait()

    def product(i, carry):
        rows = pl.ds(pl.multiple_of(i * 32, 32), 32)
        totals = [jnp.zeros((32, LANES), jnp.float32)] * own
        for m in range(levels):
            source = r.static[m, rows, :]
            totals = [totals[l] + r.root[e * own + l, m] * source for l in range(own)]
        for l in range(own):
            r.fields[0, l, rows, :] = totals[l]
        return carry

    lax.fori_loop(0, 2, product, 0)
    wait_barrier(barrier)

    def halo_copies(field, n):
        return tile_copies(field, r.halos.at[n], r.halo_send.at[n], r.halo_recv.at[n])

    halo = halo_copies(r.fields.at[0], 0)
    start_tiles(halo)
    faces = tile_copies(r.own_faces, r.faces, r.face_send, r.face_recv)
    start_tiles(faces)
    sums = []

    def send_part(d, i):
        peer = (e + d) % ens
        rows = pl.ds(i * 32, 32)
        sums.append(
            send(
                r.part.at[pl.ds(peer * own, own), rows],
                r.terms.at[d - 1, :, rows],
                r.term_send.at[d - 1, i],
                r.term_recv.at[d - 1, i],
                spot(peer, c),
            )
        )

    for n, (d, i) in enumerate(((2, 0), (2, 1), (1, 0), (3, 0), (1, 1), (3, 1))):
        level_part(r, (e + d) % ens, own, scale, i, member_loads if n == 0 else None)
        send_part(d, i)
    wait_tiles(faces)
    make_coefs(r.coefs, r.own_faces, r.faces)
    level_part(r, e, own, scale, 0)
    level_part(r, e, own, scale, 1)
    wait_tiles(halo)
    cell_rows = r.table.shape[0] // own

    def static_level(l, carry):
        around = [r.halos[0, n, l] for n in range(4)]
        total = diffused(r.coefs, r.fields[0, l], *around) + r.part[e * own + l]
        r.table[pl.ds(pl.multiple_of(l * cell_rows, cell_rows), cell_rows), :] = total
        return carry

    lax.fori_loop(0, own, static_level, 0)
    for copy in sums:
        copy.wait()
    for l in range(own):
        at = slice(l * cell_rows, (l + 1) * cell_rows)
        r.table[at, :] = r.table[at, :] + ((r.terms[0, l] + r.terms[1, l]) + r.terms[2, l])
    for one in late:
        one.wait()
    picks(r)
    pltpu.make_async_copy(r.landing, r.landing, r.list_recv).wait()
    observe(r)
    give_back(r)
    wait_sends(r.picked, r.list_send)
    spread(r)

    halo = halo_copies(r.adjoint, 1)
    start_tiles(halo)
    wholes = share(r.adjoint, r.whole, r.whole_send, r.whole_recv)
    for l in range(own):
        r.whole[e * own + l] = r.adjoint[l]
    wait_sends(r.arrived, r.back_send)
    wait_tiles(halo)

    def adjoint_level(l, carry):
        around = [r.halos[1, n, l] for n in range(4)]
        smoothed = diffused(r.coefs, r.adjoint[l], *around)
        r.fields[1, l] = smoothed
        r.smooth[e * own + l] = smoothed
        return carry

    lax.fori_loop(0, own, adjoint_level, 0)
    smooths = share(r.fields.at[1], r.smooth, r.smooth_send, r.smooth_recv)
    for copy in wholes:
        copy.wait()
    member_products(r, scale, 0, members)
    for copy in smooths:
        copy.wait()

    def static_product(i, carry):
        rows = pl.ds(pl.multiple_of((i // 2) * 32, 32), 32)
        first = (i % 2) * 8
        totals = [r.static[first + n, rows, :] for n in range(8)]
        for m in range(levels):
            source = r.smooth[m, rows, :]
            totals = [totals[n] + r.root[m, first + n] * source for n in range(8)]
        for n in range(8):
            r.static_grad[first + n, rows, :] = totals[n]
        return carry

    lax.fori_loop(0, 4, static_product, 0)


def in_hbm(array):
    return pltpu.with_memory_space_constraint(array, pltpu.HBM)


def gradients(arrays, ens, scale):
    levels, rows, lanes = arrays["static"].shape
    own = levels // ens
    members = arrays["control"].shape[0]
    lists, capacity = arrays["index"].shape
    tiles = capacity // LANES
    half_rows = lists // ens * tiles
    f32, bf16 = jnp.float32, jnp.bfloat16
    dma = pltpu.SemaphoreType.DMA
    scalars = ("local", "root", "counts")
    loaded = ("static", "north", "east", "index", "slot", "innovation", "weight", "control", "pert")
    scratch = {
        name: pltpu.VMEM(arrays[name].shape, arrays[name].dtype)
        for name in loaded
        if name not in ("north", "east")
    }
    scratch |= {
        "part": pltpu.VMEM((levels, rows, lanes), f32),
        "own_faces": pltpu.VMEM((2, rows, lanes), f32),
        "faces": pltpu.VMEM((4, 2, rows, lanes), f32),
        "coefs": pltpu.VMEM((5, 5, rows, lanes), f32),
        "fields": pltpu.VMEM((2, own, rows, lanes), f32),
        "halos": pltpu.VMEM((2, 4, own, rows, lanes), f32),
        "terms": pltpu.VMEM((ens - 1, own, rows, lanes), f32),
        "table": pltpu.VMEM((own * rows, lanes), f32),
        "cell_parts": pltpu.VMEM((2 * LANES, own * rows), bf16),
        "picked": pltpu.VMEM((lists, tiles, LANES), f32),
        "landing": pltpu.VMEM((ens, lists // ens, tiles, LANES), f32),
        "list_parts": pltpu.VMEM((2 * HALF, 2 * half_rows), bf16),
        "seen": pltpu.VMEM((2 * half_rows, 2 * HALF), f32),
        "returned": pltpu.VMEM((lists // ens, tiles, LANES), f32),
        "arrived": pltpu.VMEM((lists, tiles, LANES), f32),
        "both": pltpu.VMEM((own * rows, 2 * LANES), f32),
        "adjoint": pltpu.VMEM((own, rows, lanes), f32),
        "whole": pltpu.VMEM((levels, rows, lanes), f32),
        "smooth": pltpu.VMEM((levels, rows, lanes), f32),
        "load": dma((7,)),
        "control_load": dma((members,)),
        "pert_load": dma((members,)),
        "face_send": dma((4,)),
        "face_recv": dma((4,)),
        "halo_send": dma((2, 4)),
        "halo_recv": dma((2, 4)),
        "term_send": dma((ens - 1, 2)),
        "term_recv": dma((ens - 1, 2)),
        "list_send": dma,
        "list_recv": dma,
        "back_send": dma,
        "back_recv": dma((ens,)),
        "whole_send": dma((ens - 1,)),
        "whole_recv": dma((ens - 1,)),
        "smooth_send": dma((ens - 1,)),
        "smooth_recv": dma((ens - 1,)),
    }
    names = scalars + tuple(name + "_hbm" for name in loaded) + ("static_grad", "grad") + tuple(scratch)
    shapes = [arrays["static"].shape, arrays["control"].shape]
    return pl.pallas_call(
        functools.partial(kernel, names, scale),
        in_specs=[SMEM] * len(scalars) + [ANY] * len(loaded),
        out_specs=[VMEM, VMEM],
        out_shape=[pltpu.VMEM(shape, f32) for shape in shapes],
        scratch_shapes=list(scratch.values()),
        compiler_params=params(collective_id=1, has_side_effects=True),
        name="gradients",
    )(*[arrays[name] for name in scalars], *[in_hbm(arrays[name]) for name in loaded])


def local(
    static_control,
    ensemble_control,
    perturbations,
    vertical_root,
    vertical_local,
    face_north,
    face_east,
    innovation,
    obs_weight,
    obs_slot,
    send_index,
    send_count,
):
    grid_rows = static_control.shape[1]
    ens = lax.axis_size("ens")
    arrays = {
        "local": vertical_local,
        "root": vertical_root,
        "counts": send_count,
        "static": to_tiles(static_control),
        "north": to_tiles(face_north),
        "east": to_tiles(face_east),
        "index": send_index,
        "slot": obs_slot.reshape(-1, LANES),
        "innovation": innovation.reshape(-1, LANES),
        "weight": obs_weight.reshape(-1, LANES),
        "control": to_tiles(ensemble_control),
        "pert": to_tiles(perturbations),
    }
    scale = 1.0 / math.sqrt(ensemble_control.shape[0] * ens - 1)
    static_grad, grad = gradients(arrays, ens, scale)
    return (from_tiles(static_grad, grid_rows), from_tiles(grad, grid_rows))


def solution(mesh):
    placed = (
        P(None, "cols", None),
        P("ens", None, "cols", None),
        P("ens", None, "cols", None),
        P(),
        P(),
        P("cols", None),
        P("cols", None),
        P("cols"),
        P("cols"),
        P("cols"),
        P("cols", None),
        P("cols"),
    )
    return jax.shard_map(
        local,
        mesh=mesh,
        in_specs=placed,
        out_specs=(P(None, "cols", None), P("ens", None, "cols", None)),
        check_vma=False,
    )
```

```python
import functools
import math
import types

import jax
import jax.numpy as jnp
from jax import lax
from jax.experimental import pallas as pl
from jax.experimental.pallas import tpu as pltpu
from jax.sharding import PartitionSpec as P

NDIFF = 4
LANES = 128
VMEM_LIMIT = 52 * 1024 * 1024

precise = lax.Precision.HIGHEST

SMEM = pl.BlockSpec(memory_space=pltpu.SMEM)
VMEM = pl.BlockSpec(memory_space=pltpu.VMEM)


def params(**more):
    return pltpu.CompilerParams(vmem_limit_bytes=VMEM_LIMIT, **more)


def to_tiles(cells):
    lead = cells.shape[:-2]
    rows, length = cells.shape[-2:]
    split = cells.reshape(lead + (rows, length // LANES, LANES))
    return jnp.swapaxes(split, -3, -2).reshape(lead + (rows * length // LANES, LANES))


def from_tiles(tiles, rows):
    lead = tiles.shape[:-2]
    count = tiles.shape[-2] // rows
    split = tiles.reshape(lead + (count, rows, LANES))
    return jnp.swapaxes(split, -3, -2).reshape(lead + (rows, count * LANES))


def iota(shape, dim):
    return lax.broadcasted_iota(jnp.int32, shape, dim)


def small(ids):
    return ids.astype(jnp.float32).astype(jnp.bfloat16)


def one_hot(ids, count):
    width = ids.shape[1]
    hit = small(iota((count, width), 0)) == small(ids)
    return jnp.where(hit, jnp.bfloat16(1), jnp.bfloat16(0))


def table_parts(table, parts_ref):
    lanes = table.shape[1]
    high = table.astype(jnp.bfloat16).astype(jnp.float32)
    parts_ref[:lanes, :] = high.T.astype(jnp.bfloat16)
    parts_ref[lanes:, :] = (table - high).T.astype(jnp.bfloat16)


def look_up(parts_ref, hot, lane):
    lanes = parts_ref.shape[0] // 2
    found = jnp.dot(parts_ref[...], hot, preferred_element_type=jnp.float32)
    found = found[:lanes] + found[lanes:]
    found = jnp.where(iota(found.shape, 0) == lane, found, 0.0)
    return jnp.sum(found, axis=0, keepdims=True)


def sum_up(hot, lane, values, lanes):
    high = values.astype(jnp.bfloat16)
    low = (values - high.astype(jnp.float32)).astype(jnp.bfloat16)
    hit = small(iota((lanes, lane.shape[1]), 0)) == small(lane)
    zero = jnp.bfloat16(0)
    parts = jnp.concatenate([jnp.where(hit, high, zero), jnp.where(hit, low, zero)], axis=0)
    return lax.dot_general(hot, parts, (((1,), (1,)), ((), ())), preferred_element_type=jnp.float32)


def as_row(block):
    return jnp.concatenate([block[i : i + 1, :] for i in range(block.shape[0])], axis=1)


def cell_place(index, first_cell, cells):
    inside = index - first_cell
    level = inside >> 13
    row = (level << 6) + (((inside >> 7) & 31) << 1) + ((inside >> 12) & 1)
    mine = (inside >= 0) & (inside < cells)
    return jnp.where(mine, row, -1), inside & (LANES - 1)


MESH = pl.DeviceIdType.MESH


def spot(ens, cols):
    return {"ens": ens, "cols": cols}


def places():
    return (lax.axis_index("ens"), lax.axis_index("cols"), lax.axis_size("ens"), lax.axis_size("cols"))


def greet(barrier, target):
    pl.semaphore_signal(barrier, inc=1, device_id=target, device_id_type=MESH)


def send(source, landing, send_sem, recv_sem, target):
    copy = pltpu.make_async_remote_copy(
        src_ref=source,
        dst_ref=landing,
        send_sem=send_sem,
        recv_sem=recv_sem,
        device_id=target,
        device_id_type=MESH,
    )
    copy.start()
    return copy


def odd_rows():
    return (iota((64, LANES), 0) & 1) == 1


def blend(odd, even):
    return jnp.where(odd_rows(), odd, even)


def swapped(tile):
    return blend(pltpu.roll(tile, 1, 0), pltpu.roll(tile, 63, 0))


def east_of(tile):
    near = pltpu.roll(tile, LANES - 1, 1)
    return jnp.where(iota((64, LANES), 1) == LANES - 1, pltpu.roll(near, 62, 0), near)


def west_of(tile):
    near = pltpu.roll(tile, 1, 1)
    return jnp.where(iota((64, LANES), 1) == 0, pltpu.roll(near, 2, 0), near)


SIDES = ((0, 2), (1, 1), (2, -1), (3, -2))
UP1, OWN, DOWN1, RIM2, RIM1 = range(5)


def make_coefs(coefs, own, faces):
    e, c, ens, cols = places()

    def keep(condition):
        return condition.astype(jnp.float32)

    up2, up1, down1, down2 = [faces[n, 0] for n in range(4)]
    norths = (up1, own[0], down1)
    belows = (own[0], down1, down2)
    easts = (faces[1, 1], own[1], faces[2, 1])
    keeps = (keep(c > 0), 1.0, keep(c < cols - 1))

    def put(t, pair, outer, east, kept):
        west = west_of(east)
        coefs[t, 0] = (1.0 - pair - outer - east - west) * kept
        coefs[t, 1] = pair * kept
        coefs[t, 2] = outer * kept
        coefs[t, 3] = east * kept
        coefs[t, 4] = west * kept

    for t in range(3):
        north = norths[t]
        put(t, blend(north, swapped(north)), blend(swapped(belows[t]), north), easts[t], keeps[t])
    put(
        RIM2,
        blend(up2, swapped(down2)),
        blend(swapped(up1), down2),
        blend(faces[0, 1], faces[3, 1]),
        blend(keep(c > 1), keep(c < cols - 2)),
    )
    for n in range(5):
        coefs[RIM1, n] = blend(coefs[UP1, n], coefs[DOWN1, n])


def step_tile(coefs, t, tile, beside, beyond):
    return (
        coefs[t, 0] * tile
        + coefs[t, 1] * swapped(beside)
        + coefs[t, 2] * swapped(beyond)
        + coefs[t, 3] * east_of(tile)
        + coefs[t, 4] * west_of(tile)
    )


def diffused(coefs, own, up2, up1, down1, down2):
    rim = step_tile(coefs, RIM2, blend(up2, down2), blend(down2, up2), blend(down1, up1))
    up, here, down = (
        step_tile(coefs, UP1, up1, up1, blend(up2, own)),
        step_tile(coefs, OWN, own, own, blend(up1, down1)),
        step_tile(coefs, DOWN1, down1, down1, blend(own, down2)),
    )
    up, here, down = (
        step_tile(coefs, UP1, up, up, blend(rim, here)),
        step_tile(coefs, OWN, here, here, blend(up, down)),
        step_tile(coefs, DOWN1, down, down, blend(here, rim)),
    )
    rim = blend(up, down)
    rim, here = (
        step_tile(coefs, RIM1, rim, blend(down, up), here),
        step_tile(coefs, OWN, here, here, rim),
    )
    return step_tile(coefs, OWN, here, here, rim)


def with_side(by, action):
    e, c, ens, cols = places()
    pl.when(c < cols - by if by > 0 else c >= -by)(action)


def tile_copies(source, landing, send_sems, recv_sems):
    e, c, ens, cols = places()
    return [
        pltpu.make_async_remote_copy(
            src_ref=source,
            dst_ref=landing.at[n],
            send_sem=send_sems.at[n],
            recv_sem=recv_sems.at[n],
            device_id=spot(e, (c + by + cols) % cols),
            device_id_type=MESH,
        )
        for n, by in SIDES
    ]


def start_tiles(copies):
    for n, by in SIDES:
        with_side(by, copies[n].start)


def wait_tiles(copies):
    for n, by in SIDES:
        with_side(by, copies[n].wait_send)
        with_side(-by, copies[n].wait_recv)


def clear_rims(refs):
    e, c, ens, cols = places()
    for ref in refs:
        for n, by in SIDES:

            @pl.when(c < by if by > 0 else c >= cols + by)
            def _(ref=ref, n=n):
                ref[n] = jnp.zeros(ref.shape[1:], jnp.float32)


def greet_neighbours(barrier):
    e, c, ens, cols = places()
    for n, by in SIDES:
        with_side(by, functools.partial(greet, barrier, spot(e, (c + by + cols) % cols)))
    for d in range(1, ens):
        greet(barrier, spot((e + d) % ens, c))


def column_of(place):
    e, c, ens, cols = places()
    return place * ens + (e - c + cols) % ens


def wait_barrier(barrier):
    e, c, ens, cols = places()
    around = 0
    for n, by in SIDES:
        around = around + (1 - (c + by) // cols if by > 0 else (c + cols + by) // cols)
    all_leave = ((e - 2 * c + 2 * cols) % ens + ens - 1) // ens
    pl.semaphore_wait(barrier, ens - 1 + around + cols - 1 + all_leave)


def wait_sends(lists_ref, send_sem):
    e, c, ens, cols = places()
    few = lists_ref.at[pl.ds(0, cols - 1)]

    @pl.when(e == (2 * c) % ens)
    def _():
        pltpu.make_async_copy(few, few, send_sem).wait()

    @pl.when(e != (2 * c) % ens)
    def _():
        pltpu.make_async_copy(lists_ref, lists_ref, send_sem).wait()


HALF = 64
BLOCK = 64
ANY = pl.BlockSpec(memory_space=pl.ANY)


def greet_all(barrier):
    e, c, ens, cols = places()
    group = cols // ens
    at = c // ens
    greet_neighbours(barrier)

    def senders(n, carry):
        greet(barrier, spot((e + 1 + n // group) % ens, column_of((at + 1 + n) % group)))
        return carry

    lax.fori_loop(0, cols - 1, senders, 0)

    @pl.when(e != (2 * c) % ens)
    def _():
        greet(barrier, spot(e, column_of(at)))


def share(own_ref, whole_ref, send_sems, recv_sems):
    e, c, ens, cols = places()
    count = own_ref.shape[0]
    return [
        send(
            own_ref,
            whole_ref.at[pl.ds(e * count, count)],
            send_sems.at[d - 1],
            recv_sems.at[d - 1],
            spot((e + d) % ens, c),
        )
        for d in (2, 1, 3)
    ]


def level_part(r, peer, own, scale, i):
    members, levels = r.control.shape[:2]
    first = peer * own
    rows = pl.ds(i * 32, 32)

    def member(k, totals):
        sums = [jnp.zeros((32, LANES), jnp.float32)] * own
        for m in range(levels):
            source = r.control[k, m, rows, :]
            sums = [sums[l] + r.local[first + l, m] * source for l in range(own)]
        return tuple(
            totals[l] + r.pert[k, first + l, rows, :].astype(jnp.float32) * sums[l] for l in range(own)
        )

    totals = lax.fori_loop(0, members, member, (jnp.zeros((32, LANES), jnp.float32),) * own)
    for l in range(own):
        r.part[first + l, rows, :] = totals[l] * scale


def picks(r):
    e, c, ens, cols = places()
    cell_rows = r.table.shape[0]
    cells = cell_rows * LANES
    capacity = r.index.shape[1]
    slots = iota((1, capacity), 1)
    place = r.landing.at[e, c // ens]
    table_parts(r.table[...], r.cell_parts)

    def some(i, carry):
        for j in range(8):
            q = (c + 1 + i * 8 + j) % cols
            row, lane = cell_place(r.index[pl.ds(q, 1), :], e * cells, cells)
            row = jnp.where(slots < r.counts[q], row, -1)
            found = look_up(r.cell_parts, one_hot(row, cell_rows), lane)
            for t in range(capacity // LANES):
                r.picked[q, pl.ds(t, 1), :] = found[:, t * LANES : (t + 1) * LANES]
        for j in range(7):
            q = (c + 1 + i * 8 + j) % cols
            send(r.picked.at[q], place, r.list_send, r.list_recv, spot((c + q) % ens, q))
        q = (c + 8 + i * 8) % cols

        @pl.when((q != c) | (e != (2 * c) % ens))
        def _():
            send(r.picked.at[q], place, r.list_send, r.list_recv, spot((c + q) % ens, q))

        @pl.when((q == c) & (e == (2 * c) % ens))
        def _():
            pltpu.make_async_copy(r.picked.at[q], place, r.list_recv).start()

        return carry

    lax.fori_loop(0, cols // 8, some, 0)


def observe(r):
    e, c, ens, cols = places()
    total = r.landing[0]
    for n in range(1, ens):
        total = total + r.landing[n]
    half_rows = total.shape[0] * total.shape[1]
    table = total.reshape(half_rows, LANES)
    table_parts(jnp.concatenate([table[:, :HALF], table[:, HALF:]], axis=0), r.list_parts)
    r.seen[...] = jnp.zeros_like(r.seen)

    def some(i, carry):
        total = jnp.zeros(r.seen.shape, jnp.float32)
        for j in range(2):
            at = pl.ds(pl.multiple_of((i * 2 + j) * BLOCK, BLOCK), BLOCK)
            slot = r.slot[at, :]
            column = slot >> 10
            mine = ((column + c) & (ens - 1)) == e
            row = ((column >> 2) << 3) + ((slot >> 7) & 7) + ((slot >> 6) & 1) * half_rows
            lane = as_row(slot & (HALF - 1))
            hot = one_hot(as_row(jnp.where(mine, row, -1)), 2 * half_rows)
            found = look_up(r.list_parts, hot, lane)
            weighted = as_row(r.weight[at, :]) * (found - as_row(r.innovation[at, :]))
            total = total + sum_up(hot, lane, weighted, HALF)
        r.seen[...] += total
        return carry

    lax.fori_loop(0, r.slot.shape[0] // (2 * BLOCK), some, 0)
    seen = r.seen[:, :HALF] + r.seen[:, HALF:]
    r.returned[...] = jnp.concatenate([seen[:half_rows], seen[half_rows:]], axis=1).reshape(r.returned.shape)


def give_back(r):
    e, c, ens, cols = places()
    group = cols // ens
    at = c // ens
    recv = r.back_recv.at[c // group]

    def step(n, carry):
        i = (at + 1 + n) % group
        target = spot((e + 1 + n // group) % ens, column_of(i))
        send(r.returned.at[i], r.arrived.at[c], r.back_send, recv, target)
        return carry

    lax.fori_loop(0, cols - 1, step, 0)

    @pl.when(e != (2 * c) % ens)
    def _():
        send(r.returned.at[at], r.arrived.at[c], r.back_send, recv, spot(e, column_of(at)))

    @pl.when(e == (2 * c) % ens)
    def _():
        pltpu.make_async_copy(r.returned.at[at], r.arrived.at[c], recv).start()


def spread(r):
    e, c, ens, cols = places()
    group = cols // ens
    capacity = r.index.shape[1]
    slots = iota((1, capacity), 1)
    cell_rows = r.both.shape[0]
    cells = cell_rows * LANES
    r.both[...] = jnp.zeros_like(r.both)

    def some(i, carry):
        lists = r.arrived.at[pl.ds(i * group, group)]
        pltpu.make_async_copy(lists, lists, r.back_recv.at[i]).wait()
        total = jnp.zeros(r.both.shape, jnp.float32)
        for j in range(group):
            q = i * group + j
            row, lane = cell_place(r.index[pl.ds(q, 1), :], e * cells, cells)
            row = jnp.where(slots < r.counts[q], row, -1)
            total = total + sum_up(one_hot(row, cell_rows), lane, as_row(r.arrived[q]), LANES)
        r.both[...] += total
        return carry

    lax.fori_loop(0, ens, some, 0)
    r.adjoint[...] = (r.both[:, :LANES] + r.both[:, LANES:]).reshape(r.adjoint.shape)


def member_products(r, scale, first_member, last_member):
    levels = r.static.shape[0]

    def member(k, carry):
        def chunk(i, inner):
            rows = pl.ds(pl.multiple_of((i // 2) * 32, 32), 32)
            first = (i % 2) * 8
            totals = [jnp.zeros((32, LANES), jnp.float32)] * 8
            for m in range(levels):
                source = r.pert[k, m, rows, :].astype(jnp.float32) * r.whole[m, rows, :]
                totals = [totals[n] + r.local[m, first + n] * source for n in range(8)]
            for n in range(8):
                r.grad[k, first + n, rows, :] = r.control[k, first + n, rows, :] + totals[n] * scale
            return inner

        lax.fori_loop(0, 4, chunk, 0)
        return carry

    lax.fori_loop(first_member, last_member, member, 0)


def kernel(names, scale, *refs):
    r = types.SimpleNamespace(**dict(zip(names, refs)))
    e, c, ens, cols = places()
    levels = r.static.shape[0]
    members = r.control.shape[0]
    own = levels // ens

    def load(name, n):
        return pltpu.make_async_copy(getattr(r, name + "_hbm"), getattr(r, name), r.load.at[n])

    early = [
        load("static", 0),
        pltpu.make_async_copy(r.north_hbm, r.own_faces.at[0], r.load.at[1]),
        pltpu.make_async_copy(r.east_hbm, r.own_faces.at[1], r.load.at[2]),
    ]
    members_loads = [load("control", 3), load("pert", 4)]
    late = [load("index", 5), load("slot", 6), load("innovation", 7), load("weight", 8)]
    for one in early + members_loads + late:
        one.start()
    barrier = pltpu.get_barrier_semaphore()
    greet_all(barrier)
    clear_rims([r.faces, r.halos.at[0], r.halos.at[1]])
    for one in early:
        one.wait()

    def product(i, carry):
        rows = pl.ds(pl.multiple_of(i * 32, 32), 32)
        totals = [jnp.zeros((32, LANES), jnp.float32)] * own
        for m in range(levels):
            source = r.static[m, rows, :]
            totals = [totals[l] + r.root[e * own + l, m] * source for l in range(own)]
        for l in range(own):
            r.fields[0, l, rows, :] = totals[l]
        return carry

    lax.fori_loop(0, 2, product, 0)
    for one in members_loads:
        one.wait()
    for i in range(2):
        level_part(r, (e + 2) % ens, own, scale, i)
    wait_barrier(barrier)

    def halo_copies(field, n):
        return tile_copies(field, r.halos.at[n], r.halo_send.at[n], r.halo_recv.at[n])

    halo = halo_copies(r.fields.at[0], 0)
    start_tiles(halo)
    faces = tile_copies(r.own_faces, r.faces, r.face_send, r.face_recv)
    start_tiles(faces)
    sums = []

    def send_part(d, i):
        peer = (e + d) % ens
        rows = pl.ds(i * 32, 32)
        sums.append(
            send(
                r.part.at[pl.ds(peer * own, own), rows],
                r.terms.at[d - 1, :, rows],
                r.term_send.at[d - 1, i],
                r.term_recv.at[d - 1, i],
                spot(peer, c),
            )
        )

    for i in range(2):
        send_part(2, i)
    for d, i in ((1, 0), (3, 0), (1, 1), (3, 1)):
        level_part(r, (e + d) % ens, own, scale, i)
        send_part(d, i)
    wait_tiles(faces)
    make_coefs(r.coefs, r.own_faces, r.faces)
    level_part(r, e, own, scale, 0)
    level_part(r, e, own, scale, 1)
    wait_tiles(halo)
    cell_rows = r.table.shape[0] // own

    def static_level(l, carry):
        around = [r.halos[0, n, l] for n in range(4)]
        total = diffused(r.coefs, r.fields[0, l], *around) + r.part[e * own + l]
        r.table[pl.ds(pl.multiple_of(l * cell_rows, cell_rows), cell_rows), :] = total
        return carry

    lax.fori_loop(0, own, static_level, 0)
    for copy in sums:
        copy.wait()
    for l in range(own):
        at = slice(l * cell_rows, (l + 1) * cell_rows)
        r.table[at, :] = r.table[at, :] + ((r.terms[0, l] + r.terms[1, l]) + r.terms[2, l])
    for one in late:
        one.wait()
    picks(r)
    pltpu.make_async_copy(r.landing, r.landing, r.list_recv).wait()
    observe(r)
    give_back(r)
    wait_sends(r.picked, r.list_send)
    spread(r)

    halo = halo_copies(r.adjoint, 1)
    start_tiles(halo)
    wholes = share(r.adjoint, r.whole, r.whole_send, r.whole_recv)
    for l in range(own):
        r.whole[e * own + l] = r.adjoint[l]
    wait_sends(r.arrived, r.back_send)
    wait_tiles(halo)

    smooths = []
    for l in range(own):
        around = [r.halos[1, n, l] for n in range(4)]
        smoothed = diffused(r.coefs, r.adjoint[l], *around)
        r.fields[1, l] = smoothed
        r.smooth[e * own + l] = smoothed
        for d in (2, 1, 3):
            copy = send(
                r.fields.at[1, l],
                r.smooth.at[e * own + l],
                r.smooth_send.at[d - 1, l],
                r.smooth_recv.at[d - 1, l],
                spot((e + d) % ens, c),
            )
            smooths.append((d, copy))
    for copy in wholes:
        copy.wait()
    member_products(r, scale, 0, members)

    def add_levels(peer, source):
        first = peer * own

        def some(i, carry):
            rows = pl.ds(pl.multiple_of((i // 2) * 32, 32), 32)
            at = (i % 2) * 8
            totals = [source[at + n, rows, :] for n in range(8)]
            for m in range(own):
                level = r.smooth[first + m, rows, :]
                totals = [totals[n] + r.root[first + m, at + n] * level for n in range(8)]
            for n in range(8):
                r.static_grad[at + n, rows, :] = totals[n]
            return carry

        lax.fori_loop(0, 4, some, 0)

    add_levels(e, r.static)
    for d in (1, 3, 2):
        for copy in smooths:
            if copy[0] == d:
                copy[1].wait()
        add_levels((e + ens - d) % ens, r.static_grad)


def in_hbm(array):
    return pltpu.with_memory_space_constraint(array, pltpu.HBM)


def gradients(arrays, ens, scale):
    levels, rows, lanes = arrays["static"].shape
    own = levels // ens
    lists, capacity = arrays["index"].shape
    tiles = capacity // LANES
    half_rows = lists // ens * tiles
    f32, bf16 = jnp.float32, jnp.bfloat16
    dma = pltpu.SemaphoreType.DMA
    scalars = ("local", "root", "counts")
    loaded = ("static", "north", "east", "index", "slot", "innovation", "weight", "control", "pert")
    scratch = {
        name: pltpu.VMEM(arrays[name].shape, arrays[name].dtype)
        for name in loaded
        if name not in ("north", "east")
    }
    scratch |= {
        "part": pltpu.VMEM((levels, rows, lanes), f32),
        "own_faces": pltpu.VMEM((2, rows, lanes), f32),
        "faces": pltpu.VMEM((4, 2, rows, lanes), f32),
        "coefs": pltpu.VMEM((5, 5, rows, lanes), f32),
        "fields": pltpu.VMEM((2, own, rows, lanes), f32),
        "halos": pltpu.VMEM((2, 4, own, rows, lanes), f32),
        "terms": pltpu.VMEM((ens - 1, own, rows, lanes), f32),
        "table": pltpu.VMEM((own * rows, lanes), f32),
        "cell_parts": pltpu.VMEM((2 * LANES, own * rows), bf16),
        "picked": pltpu.VMEM((lists, tiles, LANES), f32),
        "landing": pltpu.VMEM((ens, lists // ens, tiles, LANES), f32),
        "list_parts": pltpu.VMEM((2 * HALF, 2 * half_rows), bf16),
        "seen": pltpu.VMEM((2 * half_rows, 2 * HALF), f32),
        "returned": pltpu.VMEM((lists // ens, tiles, LANES), f32),
        "arrived": pltpu.VMEM((lists, tiles, LANES), f32),
        "both": pltpu.VMEM((own * rows, 2 * LANES), f32),
        "adjoint": pltpu.VMEM((own, rows, lanes), f32),
        "whole": pltpu.VMEM((levels, rows, lanes), f32),
        "smooth": pltpu.VMEM((levels, rows, lanes), f32),
        "load": dma((9,)),
        "face_send": dma((4,)),
        "face_recv": dma((4,)),
        "halo_send": dma((2, 4)),
        "halo_recv": dma((2, 4)),
        "term_send": dma((ens - 1, 2)),
        "term_recv": dma((ens - 1, 2)),
        "list_send": dma,
        "list_recv": dma,
        "back_send": dma,
        "back_recv": dma((ens,)),
        "whole_send": dma((ens - 1,)),
        "whole_recv": dma((ens - 1,)),
        "smooth_send": dma((ens - 1, own)),
        "smooth_recv": dma((ens - 1, own)),
    }
    names = scalars + tuple(name + "_hbm" for name in loaded) + ("static_grad", "grad") + tuple(scratch)
    shapes = [arrays["static"].shape, arrays["control"].shape]
    return pl.pallas_call(
        functools.partial(kernel, names, scale),
        in_specs=[SMEM] * len(scalars) + [ANY] * len(loaded),
        out_specs=[VMEM, VMEM],
        out_shape=[pltpu.VMEM(shape, f32) for shape in shapes],
        scratch_shapes=list(scratch.values()),
        compiler_params=params(collective_id=1, has_side_effects=True),
        name="gradients",
    )(*[arrays[name] for name in scalars], *[in_hbm(arrays[name]) for name in loaded])


def local(
    static_control,
    ensemble_control,
    perturbations,
    vertical_root,
    vertical_local,
    face_north,
    face_east,
    innovation,
    obs_weight,
    obs_slot,
    send_index,
    send_count,
):
    grid_rows = static_control.shape[1]
    ens = lax.axis_size("ens")
    arrays = {
        "local": vertical_local,
        "root": vertical_root,
        "counts": send_count,
        "static": to_tiles(static_control),
        "north": to_tiles(face_north),
        "east": to_tiles(face_east),
        "index": send_index,
        "slot": obs_slot.reshape(-1, LANES),
        "innovation": innovation.reshape(-1, LANES),
        "weight": obs_weight.reshape(-1, LANES),
        "control": to_tiles(ensemble_control),
        "pert": to_tiles(perturbations),
    }
    scale = 1.0 / math.sqrt(ensemble_control.shape[0] * ens - 1)
    static_grad, grad = gradients(arrays, ens, scale)
    return (from_tiles(static_grad, grid_rows), from_tiles(grad, grid_rows))


def solution(mesh):
    placed = (
        P(None, "cols", None),
        P("ens", None, "cols", None),
        P("ens", None, "cols", None),
        P(),
        P(),
        P("cols", None),
        P("cols", None),
        P("cols"),
        P("cols"),
        P("cols"),
        P("cols", None),
        P("cols"),
    )
    return jax.shard_map(
        local,
        mesh=mesh,
        in_specs=placed,
        out_specs=(P(None, "cols", None), P("ens", None, "cols", None)),
        check_vma=False,
    )
```

```python
import functools
import math
import types

import jax
import jax.numpy as jnp
from jax import lax
from jax.experimental import pallas as pl
from jax.experimental.pallas import tpu as pltpu
from jax.sharding import PartitionSpec as P

NDIFF = 4
LANES = 128
VMEM_LIMIT = 52 * 1024 * 1024

precise = lax.Precision.HIGHEST

SMEM = pl.BlockSpec(memory_space=pltpu.SMEM)
VMEM = pl.BlockSpec(memory_space=pltpu.VMEM)


def params(**more):
    return pltpu.CompilerParams(vmem_limit_bytes=VMEM_LIMIT, **more)


def to_tiles(cells):
    lead = cells.shape[:-2]
    rows, length = cells.shape[-2:]
    split = cells.reshape(lead + (rows, length // LANES, LANES))
    return jnp.swapaxes(split, -3, -2).reshape(lead + (rows * length // LANES, LANES))


def from_tiles(tiles, rows):
    lead = tiles.shape[:-2]
    count = tiles.shape[-2] // rows
    split = tiles.reshape(lead + (count, rows, LANES))
    return jnp.swapaxes(split, -3, -2).reshape(lead + (rows, count * LANES))


def iota(shape, dim):
    return lax.broadcasted_iota(jnp.int32, shape, dim)


def small(ids):
    return ids.astype(jnp.float32).astype(jnp.bfloat16)


def one_hot(ids, count):
    width = ids.shape[1]
    hit = small(iota((count, width), 0)) == small(ids)
    return jnp.where(hit, jnp.bfloat16(1), jnp.bfloat16(0))


def table_parts(table, parts_ref):
    lanes = table.shape[1]
    high = table.astype(jnp.bfloat16).astype(jnp.float32)
    parts_ref[:lanes, :] = high.T.astype(jnp.bfloat16)
    parts_ref[lanes:, :] = (table - high).T.astype(jnp.bfloat16)


def look_up(parts_ref, hot, lane):
    lanes = parts_ref.shape[0] // 2
    found = jnp.dot(parts_ref[...], hot, preferred_element_type=jnp.float32)
    found = found[:lanes] + found[lanes:]
    found = jnp.where(iota(found.shape, 0) == lane, found, 0.0)
    return jnp.sum(found, axis=0, keepdims=True)


def sum_up(hot, lane, values, lanes):
    high = values.astype(jnp.bfloat16)
    low = (values - high.astype(jnp.float32)).astype(jnp.bfloat16)
    hit = small(iota((lanes, lane.shape[1]), 0)) == small(lane)
    zero = jnp.bfloat16(0)
    parts = jnp.concatenate([jnp.where(hit, high, zero), jnp.where(hit, low, zero)], axis=0)
    return lax.dot_general(hot, parts, (((1,), (1,)), ((), ())), preferred_element_type=jnp.float32)


def as_row(block):
    return jnp.concatenate([block[i : i + 1, :] for i in range(block.shape[0])], axis=1)


def cell_place(index, first_cell, cells):
    inside = index - first_cell
    level = inside >> 13
    row = (level << 6) + (((inside >> 7) & 31) << 1) + ((inside >> 12) & 1)
    mine = (inside >= 0) & (inside < cells)
    return jnp.where(mine, row, -1), inside & (LANES - 1)


MESH = pl.DeviceIdType.MESH


def spot(ens, cols):
    return {"ens": ens, "cols": cols}


def places():
    return (lax.axis_index("ens"), lax.axis_index("cols"), lax.axis_size("ens"), lax.axis_size("cols"))


def greet(barrier, target):
    pl.semaphore_signal(barrier, inc=1, device_id=target, device_id_type=MESH)


def send(source, landing, send_sem, recv_sem, target):
    copy = pltpu.make_async_remote_copy(
        src_ref=source,
        dst_ref=landing,
        send_sem=send_sem,
        recv_sem=recv_sem,
        device_id=target,
        device_id_type=MESH,
    )
    copy.start()
    return copy


def odd_rows():
    return (iota((64, LANES), 0) & 1) == 1


def blend(odd, even):
    return jnp.where(odd_rows(), odd, even)


def swapped(tile):
    return blend(pltpu.roll(tile, 1, 0), pltpu.roll(tile, 63, 0))


def east_of(tile):
    near = pltpu.roll(tile, LANES - 1, 1)
    return jnp.where(iota((64, LANES), 1) == LANES - 1, pltpu.roll(near, 62, 0), near)


def west_of(tile):
    near = pltpu.roll(tile, 1, 1)
    return jnp.where(iota((64, LANES), 1) == 0, pltpu.roll(near, 2, 0), near)


SIDES = ((0, 2), (1, 1), (2, -1), (3, -2))
UP1, OWN, DOWN1, RIM2, RIM1 = range(5)


def make_coefs(coefs, own, faces):
    e, c, ens, cols = places()

    def keep(condition):
        return condition.astype(jnp.float32)

    up2, up1, down1, down2 = [faces[n, 0] for n in range(4)]
    norths = (up1, own[0], down1)
    belows = (own[0], down1, down2)
    easts = (faces[1, 1], own[1], faces[2, 1])
    keeps = (keep(c > 0), 1.0, keep(c < cols - 1))

    def put(t, pair, outer, east, kept):
        west = west_of(east)
        coefs[t, 0] = (1.0 - pair - outer - east - west) * kept
        coefs[t, 1] = pair * kept
        coefs[t, 2] = outer * kept
        coefs[t, 3] = east * kept
        coefs[t, 4] = west * kept

    for t in range(3):
        north = norths[t]
        put(t, blend(north, swapped(north)), blend(swapped(belows[t]), north), easts[t], keeps[t])
    put(
        RIM2,
        blend(up2, swapped(down2)),
        blend(swapped(up1), down2),
        blend(faces[0, 1], faces[3, 1]),
        blend(keep(c > 1), keep(c < cols - 2)),
    )
    for n in range(5):
        coefs[RIM1, n] = blend(coefs[UP1, n], coefs[DOWN1, n])


def step_tile(coefs, t, tile, beside, beyond):
    return (
        coefs[t, 0] * tile
        + coefs[t, 1] * swapped(beside)
        + coefs[t, 2] * swapped(beyond)
        + coefs[t, 3] * east_of(tile)
        + coefs[t, 4] * west_of(tile)
    )


def diffused(coefs, own, up2, up1, down1, down2):
    rim = step_tile(coefs, RIM2, blend(up2, down2), blend(down2, up2), blend(down1, up1))
    up, here, down = (
        step_tile(coefs, UP1, up1, up1, blend(up2, own)),
        step_tile(coefs, OWN, own, own, blend(up1, down1)),
        step_tile(coefs, DOWN1, down1, down1, blend(own, down2)),
    )
    up, here, down = (
        step_tile(coefs, UP1, up, up, blend(rim, here)),
        step_tile(coefs, OWN, here, here, blend(up, down)),
        step_tile(coefs, DOWN1, down, down, blend(here, rim)),
    )
    rim = blend(up, down)
    rim, here = (
        step_tile(coefs, RIM1, rim, blend(down, up), here),
        step_tile(coefs, OWN, here, here, rim),
    )
    return step_tile(coefs, OWN, here, here, rim)


def with_side(by, action):
    e, c, ens, cols = places()
    pl.when(c < cols - by if by > 0 else c >= -by)(action)


def tile_copies(source, landing, send_sems, recv_sems):
    e, c, ens, cols = places()
    return [
        pltpu.make_async_remote_copy(
            src_ref=source,
            dst_ref=landing.at[n],
            send_sem=send_sems.at[n],
            recv_sem=recv_sems.at[n],
            device_id=spot(e, (c + by + cols) % cols),
            device_id_type=MESH,
        )
        for n, by in SIDES
    ]


def start_tiles(copies):
    for n, by in SIDES:
        with_side(by, copies[n].start)


def wait_tiles(copies):
    for n, by in SIDES:
        with_side(by, copies[n].wait_send)
        with_side(-by, copies[n].wait_recv)


def clear_rims(refs):
    e, c, ens, cols = places()
    for ref in refs:
        for n, by in SIDES:

            @pl.when(c < by if by > 0 else c >= cols + by)
            def _(ref=ref, n=n):
                ref[n] = jnp.zeros(ref.shape[1:], jnp.float32)


def greet_neighbours(barrier):
    e, c, ens, cols = places()
    for n, by in SIDES:
        with_side(by, functools.partial(greet, barrier, spot(e, (c + by + cols) % cols)))
    for d in range(1, ens):
        greet(barrier, spot((e + d) % ens, c))


def column_of(place):
    e, c, ens, cols = places()
    return place * ens + (e - c + cols) % ens


def wait_barrier(barrier):
    e, c, ens, cols = places()
    around = 0
    for n, by in SIDES:
        around = around + (1 - (c + by) // cols if by > 0 else (c + cols + by) // cols)
    all_leave = ((e - 2 * c + 2 * cols) % ens + ens - 1) // ens
    pl.semaphore_wait(barrier, ens - 1 + around + cols - 1 + all_leave)


def wait_sends(lists_ref, send_sem):
    e, c, ens, cols = places()
    few = lists_ref.at[pl.ds(0, cols - 1)]

    @pl.when(e == (2 * c) % ens)
    def _():
        pltpu.make_async_copy(few, few, send_sem).wait()

    @pl.when(e != (2 * c) % ens)
    def _():
        pltpu.make_async_copy(lists_ref, lists_ref, send_sem).wait()


HALF = 64
BLOCK = 64
ANY = pl.BlockSpec(memory_space=pl.ANY)


def greet_all(barrier):
    e, c, ens, cols = places()
    group = cols // ens
    at = c // ens
    greet_neighbours(barrier)

    def senders(n, carry):
        greet(barrier, spot((e + 1 + n // group) % ens, column_of((at + 1 + n) % group)))
        return carry

    lax.fori_loop(0, cols - 1, senders, 0)

    @pl.when(e != (2 * c) % ens)
    def _():
        greet(barrier, spot(e, column_of(at)))


def share(own_ref, whole_ref, send_sems, recv_sems):
    e, c, ens, cols = places()
    count = own_ref.shape[0]
    return [
        send(
            own_ref,
            whole_ref.at[pl.ds(e * count, count)],
            send_sems.at[d - 1],
            recv_sems.at[d - 1],
            spot((e + d) % ens, c),
        )
        for d in (2, 1, 3)
    ]


def level_part(r, peer, own, scale, i):
    members, levels = r.control.shape[:2]
    first = peer * own
    rows = pl.ds(i * 32, 32)

    def member(k, totals):
        sums = [jnp.zeros((32, LANES), jnp.float32)] * own
        for m in range(levels):
            source = r.control[k, m, rows, :]
            sums = [sums[l] + r.local[first + l, m] * source for l in range(own)]
        return tuple(
            totals[l] + r.pert[k, first + l, rows, :].astype(jnp.float32) * sums[l] for l in range(own)
        )

    totals = lax.fori_loop(0, members, member, (jnp.zeros((32, LANES), jnp.float32),) * own)
    for l in range(own):
        r.part[first + l, rows, :] = totals[l] * scale


def picks(r):
    e, c, ens, cols = places()
    cell_rows = r.table.shape[0]
    cells = cell_rows * LANES
    capacity = r.index.shape[1]
    slots = iota((1, capacity), 1)
    place = r.landing.at[e, c // ens]
    table_parts(r.table[...], r.cell_parts)

    def some(i, carry):
        for j in range(8):
            q = (c + 1 + i * 8 + j) % cols
            row, lane = cell_place(r.index[pl.ds(q, 1), :], e * cells, cells)
            row = jnp.where(slots < r.counts[q], row, -1)
            found = look_up(r.cell_parts, one_hot(row, cell_rows), lane)
            for t in range(capacity // LANES):
                r.picked[q, pl.ds(t, 1), :] = found[:, t * LANES : (t + 1) * LANES]
        for j in range(7):
            q = (c + 1 + i * 8 + j) % cols
            send(r.picked.at[q], place, r.list_send, r.list_recv, spot((c + q) % ens, q))
        q = (c + 8 + i * 8) % cols

        @pl.when((q != c) | (e != (2 * c) % ens))
        def _():
            send(r.picked.at[q], place, r.list_send, r.list_recv, spot((c + q) % ens, q))

        @pl.when((q == c) & (e == (2 * c) % ens))
        def _():
            pltpu.make_async_copy(r.picked.at[q], place, r.list_recv).start()

        return carry

    lax.fori_loop(0, cols // 8, some, 0)


def observe(r):
    e, c, ens, cols = places()
    total = r.landing[0]
    for n in range(1, ens):
        total = total + r.landing[n]
    half_rows = total.shape[0] * total.shape[1]
    table = total.reshape(half_rows, LANES)
    table_parts(jnp.concatenate([table[:, :HALF], table[:, HALF:]], axis=0), r.list_parts)
    r.seen[...] = jnp.zeros_like(r.seen)

    def some(i, carry):
        total = jnp.zeros(r.seen.shape, jnp.float32)
        for j in range(2):
            at = pl.ds(pl.multiple_of((i * 2 + j) * BLOCK, BLOCK), BLOCK)
            slot = r.slot[at, :]
            column = slot >> 10
            mine = ((column + c) & (ens - 1)) == e
            row = ((column >> 2) << 3) + ((slot >> 7) & 7) + ((slot >> 6) & 1) * half_rows
            lane = as_row(slot & (HALF - 1))
            hot = one_hot(as_row(jnp.where(mine, row, -1)), 2 * half_rows)
            found = look_up(r.list_parts, hot, lane)
            weighted = as_row(r.weight[at, :]) * (found - as_row(r.innovation[at, :]))
            total = total + sum_up(hot, lane, weighted, HALF)
        r.seen[...] += total
        return carry

    lax.fori_loop(0, r.slot.shape[0] // (2 * BLOCK), some, 0)
    seen = r.seen[:, :HALF] + r.seen[:, HALF:]
    r.returned[...] = jnp.concatenate([seen[:half_rows], seen[half_rows:]], axis=1).reshape(r.returned.shape)


def give_back(r):
    e, c, ens, cols = places()
    group = cols // ens
    at = c // ens
    recv = r.back_recv.at[c // group]

    def step(n, carry):
        i = (at + 1 + n) % group
        target = spot((e + 1 + n // group) % ens, column_of(i))
        send(r.returned.at[i], r.arrived.at[c], r.back_send, recv, target)
        return carry

    lax.fori_loop(0, cols - 1, step, 0)

    @pl.when(e != (2 * c) % ens)
    def _():
        send(r.returned.at[at], r.arrived.at[c], r.back_send, recv, spot(e, column_of(at)))

    @pl.when(e == (2 * c) % ens)
    def _():
        pltpu.make_async_copy(r.returned.at[at], r.arrived.at[c], recv).start()


def spread(r):
    e, c, ens, cols = places()
    group = cols // ens
    capacity = r.index.shape[1]
    slots = iota((1, capacity), 1)
    cell_rows = r.both.shape[0]
    cells = cell_rows * LANES
    r.both[...] = jnp.zeros_like(r.both)

    def some(i, carry):
        lists = r.arrived.at[pl.ds(i * group, group)]
        pltpu.make_async_copy(lists, lists, r.back_recv.at[i]).wait()
        total = jnp.zeros(r.both.shape, jnp.float32)
        for j in range(group):
            q = i * group + j
            row, lane = cell_place(r.index[pl.ds(q, 1), :], e * cells, cells)
            row = jnp.where(slots < r.counts[q], row, -1)
            total = total + sum_up(one_hot(row, cell_rows), lane, as_row(r.arrived[q]), LANES)
        r.both[...] += total
        return carry

    lax.fori_loop(0, ens, some, 0)
    r.adjoint[...] = (r.both[:, :LANES] + r.both[:, LANES:]).reshape(r.adjoint.shape)


def member_products(r, scale, first_member, last_member):
    levels = r.static.shape[0]

    def member(k, carry):
        def chunk(i, inner):
            rows = pl.ds(pl.multiple_of((i // 2) * 32, 32), 32)
            first = (i % 2) * 8
            totals = [jnp.zeros((32, LANES), jnp.float32)] * 8
            for m in range(levels):
                source = r.pert[k, m, rows, :].astype(jnp.float32) * r.whole[m, rows, :]
                totals = [totals[n] + r.local[m, first + n] * source for n in range(8)]
            for n in range(8):
                r.grad[k, first + n, rows, :] = r.control[k, first + n, rows, :] + totals[n] * scale
            return inner

        lax.fori_loop(0, 4, chunk, 0)
        return carry

    lax.fori_loop(first_member, last_member, member, 0)


def kernel(names, scale, *refs):
    r = types.SimpleNamespace(**dict(zip(names, refs)))
    e, c, ens, cols = places()
    levels = r.static.shape[0]
    members = r.control.shape[0]
    own = levels // ens

    def load(name, n):
        return pltpu.make_async_copy(getattr(r, name + "_hbm"), getattr(r, name), r.load.at[n])

    early = [
        load("static", 0),
        pltpu.make_async_copy(r.north_hbm, r.own_faces.at[0], r.load.at[1]),
        pltpu.make_async_copy(r.east_hbm, r.own_faces.at[1], r.load.at[2]),
    ]
    members_loads = [load("control", 3), load("pert", 4)]
    late = [load("index", 5), load("slot", 6), load("innovation", 7), load("weight", 8)]
    for one in early + members_loads + late:
        one.start()
    barrier = pltpu.get_barrier_semaphore()
    greet_all(barrier)
    clear_rims([r.faces, r.halos.at[0], r.halos.at[1]])
    for one in early:
        one.wait()

    def product(i, carry):
        rows = pl.ds(pl.multiple_of(i * 32, 32), 32)
        totals = [jnp.zeros((32, LANES), jnp.float32)] * own
        for m in range(levels):
            source = r.static[m, rows, :]
            totals = [totals[l] + r.root[e * own + l, m] * source for l in range(own)]
        for l in range(own):
            r.fields[0, l, rows, :] = totals[l]
        return carry

    lax.fori_loop(0, 2, product, 0)
    for one in members_loads:
        one.wait()
    for i in range(2):
        level_part(r, (e + 2) % ens, own, scale, i)
    wait_barrier(barrier)

    def halo_copies(field, n):
        return tile_copies(field, r.halos.at[n], r.halo_send.at[n], r.halo_recv.at[n])

    halo = halo_copies(r.fields.at[0], 0)
    start_tiles(halo)
    faces = tile_copies(r.own_faces, r.faces, r.face_send, r.face_recv)
    start_tiles(faces)
    sums = []

    def send_part(d, i):
        peer = (e + d) % ens
        rows = pl.ds(i * 32, 32)
        sums.append(
            send(
                r.part.at[pl.ds(peer * own, own), rows],
                r.terms.at[d - 1, :, rows],
                r.term_send.at[d - 1, i],
                r.term_recv.at[d - 1, i],
                spot(peer, c),
            )
        )

    for i in range(2):
        send_part(2, i)
    for d, i in ((1, 0), (3, 0), (1, 1), (3, 1)):
        level_part(r, (e + d) % ens, own, scale, i)
        send_part(d, i)
    wait_tiles(faces)
    make_coefs(r.coefs, r.own_faces, r.faces)
    level_part(r, e, own, scale, 0)
    level_part(r, e, own, scale, 1)
    wait_tiles(halo)
    cell_rows = r.table.shape[0] // own

    def static_level(l, carry):
        around = [r.halos[0, n, l] for n in range(4)]
        total = diffused(r.coefs, r.fields[0, l], *around) + r.part[e * own + l]
        r.table[pl.ds(pl.multiple_of(l * cell_rows, cell_rows), cell_rows), :] = total
        return carry

    lax.fori_loop(0, own, static_level, 0)
    for copy in sums:
        copy.wait()
    for l in range(own):
        at = slice(l * cell_rows, (l + 1) * cell_rows)
        r.table[at, :] = r.table[at, :] + ((r.terms[0, l] + r.terms[1, l]) + r.terms[2, l])
    for one in late:
        one.wait()
    picks(r)
    pltpu.make_async_copy(r.landing, r.landing, r.list_recv).wait()
    observe(r)
    give_back(r)
    wait_sends(r.picked, r.list_send)
    spread(r)

    halo = halo_copies(r.adjoint, 1)
    start_tiles(halo)
    wholes = share(r.adjoint, r.whole, r.whole_send, r.whole_recv)
    for l in range(own):
        r.whole[e * own + l] = r.adjoint[l]
    wait_sends(r.arrived, r.back_send)
    wait_tiles(halo)

    smooths = []
    for l in range(own):
        around = [r.halos[1, n, l] for n in range(4)]
        smoothed = diffused(r.coefs, r.adjoint[l], *around)
        r.fields[1, l] = smoothed
        r.smooth[e * own + l] = smoothed
        for d in (2, 1, 3):
            copy = send(
                r.fields.at[1, l],
                r.smooth.at[e * own + l],
                r.smooth_send.at[d - 1, l],
                r.smooth_recv.at[d - 1, l],
                spot((e + d) % ens, c),
            )
            smooths.append((d, copy))
    for copy in wholes:
        copy.wait()
    member_products(r, scale, 0, members)

    def add_levels(peer, source):
        first = peer * own

        def some(i, carry):
            rows = pl.ds(pl.multiple_of((i // 2) * 32, 32), 32)
            at = (i % 2) * 8
            totals = [source[at + n, rows, :] for n in range(8)]
            for m in range(own):
                level = r.smooth[first + m, rows, :]
                totals = [totals[n] + r.root[first + m, at + n] * level for n in range(8)]
            for n in range(8):
                r.static_grad[at + n, rows, :] = totals[n]
            return carry

        lax.fori_loop(0, 4, some, 0)

    add_levels(e, r.static)
    for d in (1, 3, 2):
        for copy in smooths:
            if copy[0] == d:
                copy[1].wait()
        add_levels((e + ens - d) % ens, r.static_grad)


def store_kernel(static_ref, grad_ref, static_hbm, grad_hbm, sems):
    members = grad_ref.shape[0]
    copies = [pltpu.make_async_copy(static_ref, static_hbm, sems.at[members])]
    for k in range(members):
        copies.append(pltpu.make_async_copy(grad_ref.at[k], grad_hbm.at[k], sems.at[k]))
    for copy in copies:
        copy.start()
    for copy in copies:
        copy.wait()


def in_hbm(array):
    return pltpu.with_memory_space_constraint(array, pltpu.HBM)


def gradients(arrays, ens, scale):
    levels, rows, lanes = arrays["static"].shape
    own = levels // ens
    members = arrays["control"].shape[0]
    lists, capacity = arrays["index"].shape
    tiles = capacity // LANES
    half_rows = lists // ens * tiles
    f32, bf16 = jnp.float32, jnp.bfloat16
    dma = pltpu.SemaphoreType.DMA
    scalars = ("local", "root", "counts")
    loaded = ("static", "north", "east", "index", "slot", "innovation", "weight", "control", "pert")
    scratch = {
        name: pltpu.VMEM(arrays[name].shape, arrays[name].dtype)
        for name in loaded
        if name not in ("north", "east")
    }
    scratch |= {
        "part": pltpu.VMEM((levels, rows, lanes), f32),
        "own_faces": pltpu.VMEM((2, rows, lanes), f32),
        "faces": pltpu.VMEM((4, 2, rows, lanes), f32),
        "coefs": pltpu.VMEM((5, 5, rows, lanes), f32),
        "fields": pltpu.VMEM((2, own, rows, lanes), f32),
        "halos": pltpu.VMEM((2, 4, own, rows, lanes), f32),
        "terms": pltpu.VMEM((ens - 1, own, rows, lanes), f32),
        "table": pltpu.VMEM((own * rows, lanes), f32),
        "cell_parts": pltpu.VMEM((2 * LANES, own * rows), bf16),
        "picked": pltpu.VMEM((lists, tiles, LANES), f32),
        "landing": pltpu.VMEM((ens, lists // ens, tiles, LANES), f32),
        "list_parts": pltpu.VMEM((2 * HALF, 2 * half_rows), bf16),
        "seen": pltpu.VMEM((2 * half_rows, 2 * HALF), f32),
        "returned": pltpu.VMEM((lists // ens, tiles, LANES), f32),
        "arrived": pltpu.VMEM((lists, tiles, LANES), f32),
        "both": pltpu.VMEM((own * rows, 2 * LANES), f32),
        "adjoint": pltpu.VMEM((own, rows, lanes), f32),
        "whole": pltpu.VMEM((levels, rows, lanes), f32),
        "smooth": pltpu.VMEM((levels, rows, lanes), f32),
        "load": dma((9,)),
        "face_send": dma((4,)),
        "face_recv": dma((4,)),
        "halo_send": dma((2, 4)),
        "halo_recv": dma((2, 4)),
        "term_send": dma((ens - 1, 2)),
        "term_recv": dma((ens - 1, 2)),
        "list_send": dma,
        "list_recv": dma,
        "back_send": dma,
        "back_recv": dma((ens,)),
        "whole_send": dma((ens - 1,)),
        "whole_recv": dma((ens - 1,)),
        "smooth_send": dma((ens - 1, own)),
        "smooth_recv": dma((ens - 1, own)),
    }
    names = scalars + tuple(name + "_hbm" for name in loaded) + ("static_grad", "grad") + tuple(scratch)
    shapes = [arrays["static"].shape, arrays["control"].shape]
    results = pl.pallas_call(
        functools.partial(kernel, names, scale),
        in_specs=[SMEM] * len(scalars) + [ANY] * len(loaded),
        out_specs=[VMEM, VMEM],
        out_shape=[pltpu.VMEM(shape, f32) for shape in shapes],
        scratch_shapes=list(scratch.values()),
        compiler_params=params(collective_id=1, has_side_effects=True),
        name="gradients",
    )(*[arrays[name] for name in scalars], *[in_hbm(arrays[name]) for name in loaded])
    return pl.pallas_call(
        store_kernel,
        in_specs=[VMEM, VMEM],
        out_specs=[ANY, ANY],
        out_shape=[pltpu.HBM(shape, f32) for shape in shapes],
        scratch_shapes=[dma((members + 1,))],
        compiler_params=pltpu.CompilerParams(vmem_limit_bytes=2**20),
        name="store",
    )(*[pltpu.with_memory_space_constraint(result, pltpu.VMEM) for result in results])


def local(
    static_control,
    ensemble_control,
    perturbations,
    vertical_root,
    vertical_local,
    face_north,
    face_east,
    innovation,
    obs_weight,
    obs_slot,
    send_index,
    send_count,
):
    grid_rows = static_control.shape[1]
    ens = lax.axis_size("ens")
    arrays = {
        "local": vertical_local,
        "root": vertical_root,
        "counts": send_count,
        "static": to_tiles(static_control),
        "north": to_tiles(face_north),
        "east": to_tiles(face_east),
        "index": send_index,
        "slot": obs_slot.reshape(-1, LANES),
        "innovation": innovation.reshape(-1, LANES),
        "weight": obs_weight.reshape(-1, LANES),
        "control": to_tiles(ensemble_control),
        "pert": to_tiles(perturbations),
    }
    scale = 1.0 / math.sqrt(ensemble_control.shape[0] * ens - 1)
    static_grad, grad = gradients(arrays, ens, scale)
    return (from_tiles(static_grad, grid_rows), from_tiles(grad, grid_rows))


def solution(mesh):
    placed = (
        P(None, "cols", None),
        P("ens", None, "cols", None),
        P("ens", None, "cols", None),
        P(),
        P(),
        P("cols", None),
        P("cols", None),
        P("cols"),
        P("cols"),
        P("cols"),
        P("cols", None),
        P("cols"),
    )
    return jax.shard_map(
        local,
        mesh=mesh,
        in_specs=placed,
        out_specs=(P(None, "cols", None), P("ens", None, "cols", None)),
        check_vma=False,
    )
```
